32 devices in a mesh: blk: 2 (over x), dp: 16 (over z, y, core).
Axes of the slice: x: 2, y: 2, z: 4, core: 2. Of those that a mesh axis runs over, the one named last changes fastest.
Arguments:
- content_in: bfloat16 [16, 1024, 768], P('dp', 'blk'), may hold values from -6 to 6
- query_in: bfloat16 [16, 1024, 768], P('dp', 'blk'), may hold values from -6 to 6
- cot_content: bfloat16 [16, 1024, 768], P('dp', 'blk'), may hold values from -6 to 6
- cot_query: bfloat16 [16, 1024, 768], P('dp', 'blk'), may hold values from -6 to 6
- attn_weights: bfloat16 [2, 768, 2304], P(None, 'dp'), may hold values from -0.21875 to 0.21875
- out_weight: bfloat16 [2, 768, 768], P(None, 'dp'), may hold values from -3.5 to 3.5
- ffn_in: bfloat16 [2, 768, 3072], P(None, 'dp'), may hold values from -0.21875 to 0.21875
- ffn_out_t: bfloat16 [2, 768, 3072], P(None, 'dp'), may hold values from -0.109375 to 0.109375
- norm_gains: float32 [2, 2, 768], replicated, may hold values from 0.1 to 1.9
- norm_shifts: float32 [2, 2, 768], replicated, may hold values from -1.5 to 1.5
- bias_table: float32 [32, 12], replicated, may hold values from -4 to 4
- permutation: int32 [16, 1024], P('dp'), may hold values from 0 to 1023, each once within a row
- predicted: int32 [16, 1024], P('dp'), may hold values 0 or 1
- doc_lengths: int32 [16, 4], P('dp'), may hold values from 1 to 512, 1024 in all within a row
Outputs:
- content_out: bfloat16 [16, 1024, 768], P('dp', 'blk')
- query_out: bfloat16 [16, 1024, 768], P('dp', 'blk')
- content_grad: float32 [16, 1024, 768], P('dp', 'blk')
- query_grad: float32 [16, 1024, 768], P('dp', 'blk')
- attn_weights_grad: float32 [2, 768, 2304], P(None, 'dp')
- out_weight_grad: float32 [2, 768, 768], P(None, 'dp')
- ffn_in_grad: float32 [2, 768, 3072], P(None, 'dp')
- ffn_out_t_grad: float32 [2, 768, 3072], P(None, 'dp')
- norm_gains_grad: float32 [2, 2, 768], replicated
- norm_shifts_grad: float32 [2, 2, 768], replicated
- bias_table_grad: float32 [32, 12], replicated
The draws below stay inside these ranges and needn't reach their ends.
Inputs may be any that keep to these rules, and one draw needn't show every extreme that they name: Each row is a permutation of the initial positions 0 to 1023; entry r is the initial position of the token at rank r. 1 marks a predicted initial position. `doc_lengths`: each row holds the lengths of the 4 documents of one sequence in initial order and sums to 1024.
All inputs are finite; a program needn't handle non-finite values. No bound on the sum of `predicted` on one device may be relied on, other than what follows from the above.
Results may differ from the reference program's by a relative error of at most 0.025.
Values may be sent and summed in bfloat16 or wider, within the bound.
No kernel may reach another device: no remote copies, remote signals or barrier semaphores. Data moves between devices by JAX's collectives and lax.ppermute only.
A program may use at most 320 MiB of HBM per device.

```python
import math
import jax
import jax.numpy as jnp
import numpy as np
from jax import lax

D = 768
HEADS = 12
FF = 3072
BUCKETS = 32
LAYERS = 2
LENGTH = 1024
DOCS = 4
SEQS = 16


def set_ends(entries, key, least, top_value):
    longest = entries.shape.index(max(entries.shape))
    spots = []
    for shift in (0, 1):
        where = [jax.random.randint(jax.random.fold_in(key, axis), (), 0, length) for axis, length in enumerate(entries.shape)]
        where[longest] = (where[longest] + shift) % entries.shape[longest]
        spots.append(tuple(where))
    return entries.at[spots[0]].set(least).at[spots[1]].set(top_value)


def block_levels(key, shape, shards, least, largest):
    level = 1.0
    for position, shards_of in shards:
        steps = jax.random.uniform(jax.random.fold_in(jax.random.fold_in(key, 6), position), (shards_of,), jnp.float32, least / len(shards), largest / len(shards))
        level = level * jnp.repeat(jnp.exp(steps), shape[position] // shards_of).reshape((-1,) + (1,) * (len(shape) - 1 - position))
    return level


def profile(count, total, limit, skew):
    loads = [(1 << 20) // math.isqrt(grade ** skew) + 1 for grade in range(2, count + 1)]
    spare, counts = total - limit - (count - 1), [1] * (count - 1)
    while spare > 0:
        free = [i for i in range(count - 1) if counts[i] < limit]
        pool, budget = sum([loads[i] for i in free]), spare
        for i in free:
            more = min(limit - counts[i], max(1, budget * loads[i] // pool), spare)
            counts[i] = counts[i] + more
            spare = spare - more
    return np.array([limit] + counts)


def ragged(stream_key, number_of, total, reach, slope):
    if number_of == 2:
        one = jax.random.randint(stream_key, (), max(1, total - reach), min(reach, total - 1) + 1)
        return jnp.stack([one, total - one])
    tallies = jnp.asarray(profile(number_of, total, reach, slope), jnp.int32)
    pairs = (number_of - 1) // 2
    source_of, sink = tallies[1:1 + 2 * pairs:2], tallies[2:2 + 2 * pairs:2]
    margin = jnp.minimum(source_of - 1, reach - sink)
    shifted = jax.random.randint(jax.random.fold_in(stream_key, 1), (pairs,), 0, 1 << 20) % (margin + 1)
    tallies = tallies.at[1:1 + 2 * pairs:2].set(source_of - shifted).at[2:2 + 2 * pairs:2].set(sink + shifted)
    return tallies[jax.random.permutation(jax.random.fold_in(stream_key, 2), number_of)]


def noise(stream_key, shape, deviation, reach, shards=(), kind=jnp.bfloat16):
    loudness = block_levels(stream_key, shape, shards, -0.22, 0.18) if shards else 1.0
    entries = jax.random.normal(stream_key, shape, jnp.float32) * deviation * loudness
    return jnp.minimum(jnp.maximum(entries, -reach), reach).astype(kind)


def setup_inputs(seed: int = 0) -> dict:
    streams_of = jax.random.split(jax.random.key(seed), 15)
    content_in = noise(streams_of[0], (SEQS, LENGTH, D), 1.0, 6.0, ((0, 16), (1, 2)))
    query_in = noise(streams_of[1], (SEQS, LENGTH, D), 1.0, 6.0, ((0, 16), (1, 2)))
    cot_content = noise(streams_of[2], (SEQS, LENGTH, D), 1.0, 6.0, ((0, 16), (1, 2)))
    cot_query = noise(streams_of[3], (SEQS, LENGTH, D), 1.0, 6.0, ((0, 16), (1, 2)))
    attn_weights = noise(streams_of[4], (LAYERS, D, 3 * D), D ** -0.5, 0.21875, ((1, 16),))
    out_weight = noise(streams_of[5], (LAYERS, D, D), (max(1, 4 * D // LENGTH)) ** -0.5, 3.5, ((1, 16),))
    ffn_in = noise(streams_of[6], (LAYERS, D, FF), D ** -0.5, 0.21875, ((1, 16),))
    ffn_out_t = noise(streams_of[7], (LAYERS, D, FF), FF ** -0.5, 0.109375, ((1, 16),))
    norm_gains = jnp.clip(1.0 + 0.18 * jax.random.normal(streams_of[8], (LAYERS, 2, D), jnp.float32), 0.1, 1.9)
    norm_shifts = noise(streams_of[9], (LAYERS, 2, D), 0.3, 1.5, (), jnp.float32)
    bias_table = noise(streams_of[10], (BUCKETS, HEADS), 1.0, 4.0, (), jnp.float32)
    permutation = jax.vmap(lambda own: jax.random.permutation(own, LENGTH))(jax.random.split(streams_of[11], SEQS)).reshape((SEQS, LENGTH)).astype(jnp.int32)
    predicted = set_ends((jax.random.randint(streams_of[12], (SEQS, LENGTH), 0, 100) < 15).astype(jnp.int32), jax.random.fold_in(streams_of[12], 1), 0, 1)
    doc_lengths = jax.vmap(lambda own: ragged(own, DOCS, LENGTH, LENGTH // 2, 0))(jax.random.split(streams_of[13], SEQS)).reshape((SEQS, DOCS)).astype(jnp.int32)
    return dict(content_in=content_in, query_in=query_in, cot_content=cot_content, cot_query=cot_query, attn_weights=attn_weights, out_weight=out_weight, ffn_in=ffn_in, ffn_out_t=ffn_out_t, norm_gains=norm_gains, norm_shifts=norm_shifts, bias_table=bias_table, permutation=permutation, predicted=predicted, doc_lengths=doc_lengths)


@jax.custom_vjp
def low(v):
    return lax.optimization_barrier(v.astype(jnp.bfloat16)).astype(jnp.float32)

@jax.custom_vjp
def low_back(v):
    return v

def low_keep(v):
    return (low(v), None)

def low_pass(kept, grad):
    return (grad,)

def back_keep(v):
    return (v, None)

def back_low(kept, grad):
    return (low(grad),)
low.defvjp(low_keep, low_pass)
low_back.defvjp(back_keep, back_low)
THRESHOLDS = (12, 16, 23, 32, 46, 64, 91)

def bucket_of(relative):
    distance = jnp.abs(relative)
    far_bucket = 8 + sum(((distance >= threshold).astype(jnp.int32) for threshold in THRESHOLDS))
    near_bucket = jnp.where(distance < 8, distance, jnp.minimum(far_bucket, 15))
    return jnp.where(relative > 0, 16, 0).astype(jnp.int32) + near_bucket.astype(jnp.int32)

def layer_norm(tensor, scale_row, shift_row):
    center = tensor - lax.optimization_barrier(jnp.mean(tensor, axis=-1, keepdims=True))
    spread = lax.optimization_barrier(jnp.mean(center * center, axis=-1, keepdims=True))
    return center * lax.rsqrt(spread + 1e-05) * scale_row + shift_row

def matmul(left_side, right_side):
    return jnp.dot(left_side, right_side, precision=lax.Precision.HIGHEST)

def rounded(tensor):
    return low(low_back(tensor))

def sequence_meta(rank_anchor, chosen, lengths):
    positions = jnp.arange(LENGTH, dtype=jnp.int32)
    bounds = jnp.cumsum(lengths).astype(jnp.int32)[:-1]
    doc_anchor = lax.optimization_barrier(jnp.sum((positions[:, None] >= bounds[None, :]).astype(jnp.int32), axis=1)).astype(jnp.int32)
    starts = (positions == 0) | jnp.any(positions[:, None] == bounds[None, :], axis=1)
    chosen_live = (chosen == 1) & jnp.logical_not(starts)
    doc_rank = doc_anchor[rank_anchor]
    pred_rank = chosen_live[rank_anchor]
    same_doc = doc_rank[:, None] == doc_rank[None, :]
    open_key = jnp.logical_not(pred_rank)[None, :]
    see_content = same_doc & (open_key | (positions[None, :] <= positions[:, None]))
    see_query = same_doc & (open_key | (positions[None, :] < positions[:, None]))
    buckets = bucket_of(rank_anchor[None, :] - rank_anchor[:, None])
    return (see_content, see_query, buckets)

def attend(queries, keys, values, bias, visible):
    raw_scores = low_back(jnp.einsum('qhd,khd->hqk', queries, keys, precision=lax.Precision.HIGHEST))
    scores = jnp.where(visible[None], raw_scores * 0.125 + bias, -1e+30)
    log_total = jax.nn.logsumexp(scores, axis=-1, keepdims=True)
    weights = low(jnp.exp(scores - log_total))
    return rounded(jnp.einsum('hqk,khd->qhd', weights, values, precision=lax.Precision.HIGHEST))

def one_layer(content, query, layer_params, bias, see_content, see_query):
    qkv_matrix, proj_matrix, inner_matrix, outer_matrix, gains, shifts = layer_params
    heads_shape = (LENGTH, HEADS, D // HEADS)
    content_low = low(content)
    query_low = low(query)
    projected = rounded(matmul(content_low, qkv_matrix))
    query_own = rounded(matmul(query_low, qkv_matrix[:, :D]))
    keys = projected[:, D:2 * D].reshape(heads_shape)
    values = projected[:, 2 * D:].reshape(heads_shape)
    new_streams = []
    for stream, queries, visible in ((content, projected[:, :D], see_content), (query, query_own, see_query)):
        attended = attend(queries.reshape(heads_shape), keys, values, bias, visible).reshape(LENGTH, D)
        branch = low_back(matmul(attended, proj_matrix))
        middle = layer_norm(stream + branch, gains[0], shifts[0])
        inner_pre = low_back(matmul(low(middle), inner_matrix))
        activation = low(jax.nn.gelu(inner_pre, approximate=False))
        outer_out = low_back(matmul(activation, outer_matrix.T))
        new_streams.append(layer_norm(middle + outer_out, gains[1], shifts[1]))
    return (new_streams[0], new_streams[1])

def sequence_net(params, seq_items):
    content, query, rank_anchor, chosen, lengths = seq_items
    see_content, see_query, buckets = sequence_meta(rank_anchor, chosen, lengths)
    bias = jnp.transpose(jnp.take(params[6], buckets, axis=0), (2, 0, 1))
    for layer_index in range(LAYERS):
        layer_params = tuple((weight_stack[layer_index] for weight_stack in params[:6]))
        content, query = one_layer(content, query, layer_params, bias, see_content, see_query)
    return (content, query)

def reference(content_in, query_in, cot_content, cot_query, attn_weights, out_weight, ffn_in, ffn_out_t, norm_gains, norm_shifts, bias_table, permutation, predicted, doc_lengths):

    def network(content, query, qkv_all, proj_all, inner_all, outer_all, gains_all, shifts_all, table_all):
        params = (qkv_all, proj_all, inner_all, outer_all, gains_all, shifts_all, table_all)

        def one_sequence(seq_items):
            return sequence_net(params, seq_items)
        return lax.map(jax.checkpoint(one_sequence), (content, query, permutation, predicted, doc_lengths))
    primal = tuple((tensor_in.astype(jnp.float32) for tensor_in in (content_in, query_in, attn_weights, out_weight, ffn_in, ffn_out_t)))
    primal = primal + (norm_gains, norm_shifts, bias_table)
    outputs, pullback = jax.vjp(network, *primal)
    gradients = pullback((cot_content.astype(jnp.float32), cot_query.astype(jnp.float32)))
    return (outputs[0].astype(jnp.bfloat16), outputs[1].astype(jnp.bfloat16), gradients[0], gradients[1], gradients[2], gradients[3], gradients[4], gradients[5], gradients[6], gradients[7], gradients[8])
```

```python
import functools

import jax
import jax.numpy as jnp
from jax import lax
from jax.experimental import pallas as pl
from jax.experimental.pallas import tpu as pltpu
from jax.sharding import PartitionSpec as P

THRESHOLDS = (12, 16, 23, 32, 46, 64, 91)
MASKED = -1e30
F32 = jnp.float32
LOW = jnp.bfloat16
VMEM_LIMIT = 56 * 2**20


def dot_nn(left_side, right_side):
    return jnp.dot(left_side, right_side, preferred_element_type=F32)


def dot_nt(left_side, right_side):
    return lax.dot_general(left_side, right_side, (((1,), (1,)), ((), ())), preferred_element_type=F32)


def dot_tn(left_side, right_side):
    return lax.dot_general(left_side, right_side, (((0,), (0,)), ((), ())), preferred_element_type=F32)


def bucket_of(relative):
    distance = jnp.abs(relative)
    far_bucket = 8 + sum(((distance >= threshold).astype(jnp.int32) for threshold in THRESHOLDS))
    near_bucket = jnp.where(distance < 8, distance, jnp.minimum(far_bucket, 15))
    return jnp.where(relative > 0, 16, 0).astype(jnp.int32) + near_bucket


def bias_kernel(table_ref, place_ref, doc_ref, rank_ref, key_doc_ref, key_rank_ref, *refs):
    out_ref = refs[-1]
    head_count, rows, length = out_ref.shape
    place = place_ref[...]
    doc = doc_ref[...]
    rank = rank_ref[...]
    for first in range(0, length, 128):
        key_place = first + lax.broadcasted_iota(jnp.int32, (rows, 128), 1)
        seen = (key_doc_ref[:, first : first + 128] == doc) & (
            key_rank_ref[:, first : first + 128] <= rank
        )
        choice = jnp.where(seen, bucket_of(key_place - place), 32)
        for head in range(head_count):
            for row in range(0, rows, 8):
                line = jnp.broadcast_to(table_ref[head : head + 1, :], (8, 128))
                out_ref[head, row : row + 8, first : first + 128] = jnp.take_along_axis(
                    line, choice[row : row + 8], axis=1
                )


def bias_call(table_rows, place, doc, rank, key_doc, key_rank, *waits):
    head_count = table_rows.shape[0]
    rows, length = place.shape[0], key_doc.shape[1]
    tile = min(32, rows)
    column = pl.BlockSpec((tile, 1), lambda i: (i, 0))
    line = pl.BlockSpec((1, length), lambda i: (0, 0))
    return pl.pallas_call(
        bias_kernel,
        grid=(rows // tile,),
        in_specs=[
            pl.BlockSpec((head_count, 128), lambda i: (0, 0)),
            column,
            column,
            column,
            line,
            line,
        ]
        + [pl.BlockSpec(memory_space=pl.ANY)] * len(waits),
        out_specs=pl.BlockSpec((head_count, tile, length), lambda i: (0, i, 0)),
        out_shape=jax.ShapeDtypeStruct((head_count, rows, length), F32),
        compiler_params=pltpu.CompilerParams(vmem_limit_bytes=VMEM_LIMIT),
        cost_estimate=pl.CostEstimate(
            flops=0, bytes_accessed=head_count * rows * length * 12, transcendentals=0
        ),
        name="bias_rows",
    )(table_rows, place, doc, rank, key_doc, key_rank, *waits)


def attend_kernel(q_ref, k_ref, v_ref, bias_ref, own_ref, *refs):
    o_ref, low_ref, p_ref = refs[-3:]
    rows, length = bias_ref.shape[1:]
    first_half = lax.broadcasted_iota(jnp.int32, (rows, 128), 1) < 64
    key_place = lax.broadcasted_iota(jnp.int32, (rows, length), 1)
    zero = jnp.zeros((rows, 128), LOW)
    for stream in range(2):
        queries = q_ref[stream] * jnp.array(0.125, LOW)
        parts = []
        for half in range(2):
            mine = jnp.where(first_half, queries, zero) if half == 0 else jnp.where(first_half, zero, queries)
            scores = dot_nt(mine, k_ref[...]) + bias_ref[half]
            if stream == 1:
                scores = jnp.where(key_place == own_ref[...], MASKED, scores)
            weights = jnp.exp(scores - jnp.max(scores, axis=1, keepdims=True))
            weights = weights * (1.0 / jnp.sum(weights, axis=1, keepdims=True))
            low = weights.astype(LOW)
            p_ref[half, stream] = low
            parts.append(dot_nn(low, v_ref[...]))
        out = jnp.where(first_half, parts[0], parts[1])
        o_ref[stream] = out
        low_ref[stream] = out.astype(LOW)


def attend_call(queries, keys, values, bias, own, *waits):
    _, rows, width = queries.shape
    length = keys.shape[0]
    tile = min(256, rows)
    pairs = width // 128
    per_row = pl.BlockSpec((2, tile, 128), lambda h, i: (0, i, h))
    per_key = pl.BlockSpec((length, 128), lambda h, i: (0, h))
    return pl.pallas_call(
        attend_kernel,
        grid=(pairs, rows // tile),
        in_specs=[
            per_row,
            per_key,
            per_key,
            pl.BlockSpec((2, tile, length), lambda h, i: (h, i, 0)),
            pl.BlockSpec((tile, 1), lambda h, i: (i, 0)),
        ]
        + [pl.BlockSpec(memory_space=pl.ANY)] * len(waits),
        out_specs=[
            per_row,
            per_row,
            pl.BlockSpec((2, 2, tile, length), lambda h, i: (h, 0, i, 0)),
        ],
        out_shape=[
            jax.ShapeDtypeStruct((2, rows, width), F32),
            jax.ShapeDtypeStruct((2, rows, width), LOW),
            jax.ShapeDtypeStruct((2 * pairs, 2, rows, length), LOW),
        ],
        compiler_params=pltpu.CompilerParams(vmem_limit_bytes=VMEM_LIMIT),
        cost_estimate=pl.CostEstimate(
            flops=16 * rows * length * width,
            bytes_accessed=pairs * rows * length * 16,
            transcendentals=4 * pairs * rows * length,
        ),
        name="attend",
    )(queries, keys, values, bias, own, *waits)


def attend_back_kernel(earlier, *refs):
    q_ref, k_ref, v_ref, do_ref, o_ref, p_ref = refs[:6]
    dq_ref, dk_ref, dv_ref, sum_ref, dk_sum, dv_sum = refs[-6:]
    rows = q_ref.shape[1]
    first_half = lax.broadcasted_iota(jnp.int32, (rows, 128), 1) < 64
    zero = jnp.zeros((rows, 128), LOW)

    @pl.when(pl.program_id(1) == 0)
    def _():
        dk_sum[...] = jnp.zeros_like(dk_sum)
        dv_sum[...] = jnp.zeros_like(dv_sum)

    grads = [[None, None], [None, None]]
    for half in range(2):
        span = slice(64 * half, 64 * half + 64)
        total = refs[6][half] if earlier else None
        for stream in range(2):
            grad_out = do_ref[stream]
            mine = jnp.where(first_half, grad_out, zero) if half == 0 else jnp.where(first_half, zero, grad_out)
            delta = jnp.sum(mine.astype(F32) * o_ref[stream], axis=1, keepdims=True)
            low_p = p_ref[half, stream]
            grad = low_p.astype(F32) * (dot_nt(mine, v_ref[...]) - delta)
            total = grad if total is None else total + grad
            low = grad.astype(LOW)
            grads[stream][half] = dot_nn(low, k_ref[...])
            queries = q_ref[stream] * jnp.array(0.125, LOW)
            dk_sum[span, :] += dot_nn(queries.T[span], low)
            dv_sum[span, :] += dot_nn(grad_out.T[span], low_p)
        sum_ref[half] = total
    for stream in range(2):
        dq_ref[stream] = (jnp.where(first_half, grads[stream][0], grads[stream][1]) * 0.125).astype(LOW)

    @pl.when(pl.program_id(1) == pl.num_programs(1) - 1)
    def _():
        dk_ref[...] = dk_sum[...].T.astype(LOW)
        dv_ref[...] = dv_sum[...].T.astype(LOW)


def attend_back_call(span, queries, keys, values, grad_out, out, weights, earlier, partial, *waits):
    first, pairs = span
    rows, width = queries.shape[1:]
    length = keys.shape[0]
    tile = min(256, rows)
    per_row = pl.BlockSpec((2, tile, 128), lambda h, i: (0, i, h + first))
    per_key = pl.BlockSpec((length, 128), lambda h, i: (0, h + first))
    per_score = pl.BlockSpec((2, tile, length), lambda h, i: (h + first, i, 0))
    more = [] if earlier is None else [earlier]
    begun = [] if partial is None else list(partial)
    return pl.pallas_call(
        functools.partial(attend_back_kernel, earlier is not None),
        grid=(pairs, rows // tile),
        in_specs=[
            per_row,
            per_key,
            per_key,
            per_row,
            per_row,
            pl.BlockSpec((2, 2, tile, length), lambda h, i: (h + first, 0, i, 0)),
        ]
        + [per_score] * len(more)
        + [pl.BlockSpec(memory_space=pl.ANY)] * len(begun + list(waits)),
        out_specs=[per_row, per_key, per_key, per_score],
        out_shape=[
            jax.ShapeDtypeStruct((2, rows, width), LOW),
            jax.ShapeDtypeStruct((length, width), LOW),
            jax.ShapeDtypeStruct((length, width), LOW),
            jax.ShapeDtypeStruct((width // 64, rows, length), F32),
        ],
        input_output_aliases={6 + len(more) + index: index for index in range(len(begun))},
        scratch_shapes=[pltpu.VMEM((128, length), F32)] * 2,
        compiler_params=pltpu.CompilerParams(vmem_limit_bytes=VMEM_LIMIT),
        cost_estimate=pl.CostEstimate(
            flops=32 * rows * length * 128 * pairs,
            bytes_accessed=pairs * rows * length * 24,
            transcendentals=0,
        ),
        name="attend_back",
    )(queries, keys, values, grad_out, out, weights, *more, *begun, *waits)


def table_kernel(sum_count, *refs):
    sum_refs, place_ref, out_ref = refs[:sum_count], refs[sum_count], refs[-1]
    rows, length = sum_refs[0].shape[1:]
    head_count = sum(sum_ref.shape[0] for sum_ref in sum_refs)
    bucket_count = out_ref.shape[0] // 8

    @pl.when(pl.program_id(0) == 0)
    def _():
        out_ref[...] = jnp.zeros_like(out_ref)

    key_place = lax.broadcasted_iota(jnp.int32, (8, length), 1)
    total = jnp.zeros(out_ref.shape, F32)
    for row in range(0, rows, 8):
        choice = bucket_of(key_place - place_ref[row : row + 8])
        chosen = jnp.concatenate(
            [jnp.where(choice == bucket, 1.0, 0.0) for bucket in range(bucket_count)], axis=0
        ).astype(LOW)
        part = jnp.concatenate([sum_ref[:, row : row + 8, :] for sum_ref in sum_refs], axis=0)
        part = part.reshape(head_count * 8, length).astype(LOW)
        total = total + dot_nt(chosen, part)
    out_ref[...] += total


def table_call(score_sums, place, bucket_count, *waits):
    rows, length = score_sums[0].shape[1:]
    head_count = sum(score_sum.shape[0] for score_sum in score_sums)
    tile = min(32, rows)
    grouped = pl.pallas_call(
        functools.partial(table_kernel, len(score_sums)),
        grid=(rows // tile,),
        in_specs=[
            pl.BlockSpec((score_sum.shape[0], tile, length), lambda i: (0, i, 0)) for score_sum in score_sums
        ]
        + [pl.BlockSpec((tile, 1), lambda i: (i, 0))]
        + [pl.BlockSpec(memory_space=pl.ANY)] * len(waits),
        out_specs=pl.BlockSpec((8 * bucket_count, 8 * head_count), lambda i: (0, 0)),
        out_shape=jax.ShapeDtypeStruct((8 * bucket_count, 8 * head_count), F32),
        compiler_params=pltpu.CompilerParams(vmem_limit_bytes=VMEM_LIMIT),
        cost_estimate=pl.CostEstimate(
            flops=512 * rows * length * head_count,
            bytes_accessed=rows * length * head_count * 4,
            transcendentals=0,
        ),
        name="table_sums",
    )(*score_sums, place, *waits)
    grouped = grouped.reshape(bucket_count, 8, head_count, 8)
    return jnp.sum(grouped * jnp.eye(8, dtype=F32)[None, :, None, :], axis=(1, 3))


def norm_rows(tensor, scale_row, shift_row):
    center = tensor - jnp.mean(tensor, axis=1, keepdims=True)
    inverse = lax.rsqrt(jnp.mean(center * center, axis=1, keepdims=True) + 1e-05)
    return center * inverse * scale_row + shift_row, inverse


def norm_rows_back(grad, normal, inverse, scale_row):
    scaled = grad * scale_row
    mean_one = jnp.mean(scaled, axis=1, keepdims=True)
    mean_two = jnp.mean(scaled * normal, axis=1, keepdims=True)
    return inverse * (scaled - mean_one - normal * mean_two)


def pieces_of(pieces):
    arrays, plan = [], []
    for pair in pieces:
        spots = []
        for array, first in pair:
            known = [i for i, other in enumerate(arrays) if other is array]
            if not known:
                arrays.append(array)
            spots.append((known[0] if known else len(arrays) - 1, first))
        plan.append(tuple(spots))
    return arrays, tuple(plan)


def layer_tail_kernel(count, plan, span, *refs):
    (stream_ref, out_ref, proj_ref), refs = refs[:3], refs[3:]
    piece_refs, refs = refs[:count], refs[count:]
    gain_ref, shift_ref = refs[:2]
    result_ref, low_ref, middle_ref, middle_low_ref, active_ref, slope_ref, one_ref, two_ref = refs[-8:]
    mixed = stream_ref[...] + dot_nn(out_ref[...], proj_ref[...])
    middle, one_ref[...] = norm_rows(mixed, gain_ref[0:1], shift_ref[0:1])
    middle_ref[...] = middle
    middle_low = middle.astype(LOW)
    middle_low_ref[...] = middle_low
    total = middle
    for index, ((inner_at, inner_first), (outer_at, outer_first)) in enumerate(plan):
        columns = slice(index * span, (index + 1) * span)
        inner = dot_nn(middle_low, piece_refs[inner_at][:, inner_first : inner_first + span])
        cdf = 0.5 + 0.5 * lax.erf(inner * (2.0**-0.5))
        active = (inner * cdf).astype(LOW)
        active_ref[:, columns] = active
        density = jnp.exp(inner * inner * -0.5) * 0.3989422804014327
        slope_ref[:, columns] = (cdf + inner * density).astype(LOW)
        total = total + dot_nt(active, piece_refs[outer_at][:, outer_first : outer_first + span])
    result, two_ref[...] = norm_rows(total, gain_ref[1:2], shift_ref[1:2])
    result_ref[...] = result
    low_ref[...] = result.astype(LOW)


def layer_tail_call(stream, out_low, proj, pieces, span, gains, shifts, *waits):
    rows, width = stream.shape
    hidden = span * len(pieces)
    pieces, plan = pieces_of(pieces)
    proj, proj_at = proj
    tile = min(256, rows)

    def per_row(columns):
        return pl.BlockSpec((tile, columns), lambda i: (i, 0))

    def fixed(shape):
        return pl.BlockSpec(shape, lambda i: (0, 0), pipeline_mode=pl.Buffered(1))

    def whole(columns, kind):
        return jax.ShapeDtypeStruct((rows, columns), kind)

    return pl.pallas_call(
        functools.partial(layer_tail_kernel, len(pieces), plan, span),
        grid=(rows // tile,),
        in_specs=[per_row(width), per_row(width), pl.BlockSpec((width, width), lambda i: (0, proj_at), pipeline_mode=pl.Buffered(1))]
        + [fixed(piece.shape) for piece in pieces]
        + [fixed((2, width))] * 2
        + [pl.BlockSpec(memory_space=pl.ANY)] * len(waits),
        out_specs=[
            per_row(width), per_row(width), per_row(width), per_row(width),
            per_row(hidden), per_row(hidden), per_row(1), per_row(1),
        ],
        out_shape=[
            whole(width, F32), whole(width, LOW), whole(width, F32), whole(width, LOW),
            whole(hidden, LOW), whole(hidden, LOW), whole(1, F32), whole(1, F32),
        ],
        compiler_params=pltpu.CompilerParams(vmem_limit_bytes=VMEM_LIMIT),
        cost_estimate=pl.CostEstimate(
            flops=2 * rows * width * (width + 2 * hidden),
            bytes_accessed=4 * rows * hidden + 12 * rows * width + 4 * width * hidden,
            transcendentals=2 * rows * hidden,
        ),
        name="layer_tail",
    )(stream, out_low, proj, *pieces, gains, shifts, *waits)


def layer_tail_back_kernel(count, plan, span, *refs):
    (grad_ref, result_ref, two_ref, middle_ref, one_ref, slope_ref, proj_ref), refs = refs[:7], refs[7:]
    piece_refs, refs = refs[:count], refs[count:]
    gain_ref, shift_ref, begun_ref = refs[:3]
    two_low_ref, inner_ref, stream_ref, branch_ref, out_ref, terms_ref = refs[-6:]

    @pl.when(pl.program_id(0) == 0)
    def _():
        terms_ref[...] = begun_ref[...]

    grad = grad_ref[...]
    normal = (result_ref[...] - shift_ref[1:2]) / gain_ref[1:2]
    terms_ref[1:2] += jnp.sum(grad * normal, axis=0, keepdims=True)
    terms_ref[3:4] += jnp.sum(grad, axis=0, keepdims=True)
    grad = norm_rows_back(grad, normal, two_ref[...], gain_ref[1:2])
    low = grad.astype(LOW)
    two_low_ref[...] = low
    for index, ((inner_at, inner_first), (outer_at, outer_first)) in enumerate(plan):
        columns = slice(index * span, (index + 1) * span)
        outer_piece = piece_refs[outer_at][:, outer_first : outer_first + span]
        inner = (dot_nn(low, outer_piece) * slope_ref[:, columns].astype(F32)).astype(LOW)
        inner_ref[:, columns] = inner
        grad = grad + dot_nt(inner, piece_refs[inner_at][:, inner_first : inner_first + span])
    normal = (middle_ref[...] - shift_ref[0:1]) / gain_ref[0:1]
    terms_ref[0:1] += jnp.sum(grad * normal, axis=0, keepdims=True)
    terms_ref[2:3] += jnp.sum(grad, axis=0, keepdims=True)
    grad = norm_rows_back(grad, normal, one_ref[...], gain_ref[0:1])
    stream_ref[...] = grad
    low = grad.astype(LOW)
    branch_ref[...] = low
    out_ref[...] = dot_nt(low, proj_ref[...]).astype(LOW)


def layer_tail_back_call(grad, result, two, middle, one, slope, proj, pieces, span, gains, shifts, part, partial, *waits):
    rows, width = result.shape
    share = 1 if part is None else 2
    hidden = span * len(pieces)
    pieces, plan = pieces_of(pieces)
    proj, proj_at = proj
    tile = min(256, rows // share)

    first = (part or 0) * (rows // 2 // tile)
    begun = [] if partial is None else list(partial[:-1])
    terms = jnp.zeros((8, width), F32) if partial is None else partial[-1]

    def per_row(columns):
        return pl.BlockSpec((tile, columns), lambda i: (i + first, 0))

    def fixed(shape):
        return pl.BlockSpec(shape, lambda i: (0, 0), pipeline_mode=pl.Buffered(1))

    def whole(columns, kind):
        return jax.ShapeDtypeStruct((rows, columns), kind)

    return pl.pallas_call(
        functools.partial(layer_tail_back_kernel, len(pieces), plan, span),
        grid=(rows // share // tile,),
        in_specs=[pl.BlockSpec((tile, width), lambda i: (i, 0)), per_row(width), per_row(1), per_row(width), per_row(1), per_row(hidden)]
        + [pl.BlockSpec((width, width), lambda i: (0, proj_at), pipeline_mode=pl.Buffered(1))]
        + [fixed(piece.shape) for piece in pieces]
        + [fixed((2, width))] * 2
        + [fixed((8, width))]
        + [pl.BlockSpec(memory_space=pl.ANY)] * len(begun + list(waits)),
        out_specs=[
            per_row(width), per_row(hidden), per_row(width), per_row(width), per_row(width),
            pl.BlockSpec((8, width), lambda i: (0, 0)),
        ],
        out_shape=[
            whole(width, LOW), whole(hidden, LOW), whole(width, F32), whole(width, LOW), whole(width, LOW),
            jax.ShapeDtypeStruct((8, width), F32),
        ],
        input_output_aliases={10 + len(pieces) + index: index for index in range(len(begun))},
        compiler_params=pltpu.CompilerParams(vmem_limit_bytes=VMEM_LIMIT),
        cost_estimate=pl.CostEstimate(
            flops=2 * rows // share * width * (width + 2 * hidden),
            bytes_accessed=4 * rows * hidden + 20 * rows * width + 4 * width * hidden,
            transcendentals=0,
        ),
        name="layer_tail_back",
    )(grad, result, two, middle, one, slope, proj, *pieces, gains, shifts, terms, *begun, *waits)


def product_kernel(plan, side_ref, *refs):
    step = pl.program_id(0)
    for index, (lhs, rhs, out, plus) in enumerate(plan):

        @pl.when(step == index)
        def _(lhs=lhs, rhs=rhs, out=out, plus=plus):
            total = dot_tn(refs[lhs][...], refs[rhs][...])
            if plus is not None:
                total = total + refs[plus][...].astype(F32)
            refs[out][...] = total.astype(refs[out].dtype)


def products_call(name, side, steps, outs, waits=()):
    arrays, specs, plan, place = [], [], [], {}
    total = len(steps)

    def column_of(kind, side_ref):
        if kind == "side":
            return side_ref[0]
        if kind == "other":
            return 1 - side_ref[0]
        return kind

    def chain(at):
        table = []
        for step in range(total):
            later = [at[u] for u in sorted(at) if u >= step]
            table.append(later[0] if later else at[max(at)])
        def index(i, side_ref):
            value = column_of(table[-1], side_ref)
            for step in reversed(range(total - 1)):
                if table[step] != table[step + 1]:
                    value = jnp.where(i <= step, column_of(table[step], side_ref), value)
            return (0, value)
        return index

    uses = {}
    for step, (lhs, rhs, span, block, out, out_block, plus) in enumerate(steps):
        uses.setdefault(("in", id(lhs), lhs.shape[1]), [lhs, {}])[1][step] = 0
        uses.setdefault(("in", id(rhs), span), [rhs, {}])[1][step] = block
        if plus is not None:
            uses.setdefault(("in", id(plus), outs[out][2]), [plus, {}])[1][step] = out_block
    for key, (array, at) in uses.items():
        place[key] = len(arrays)
        arrays.append(array)
        specs.append(pl.BlockSpec((array.shape[0], key[2]), chain(at)))
    first_out = len(arrays) + len(waits)
    out_names = list(outs)
    out_specs = []
    for out in out_names:
        at = {step: entry[5] for step, entry in enumerate(steps) if entry[4] == out}
        out_specs.append(pl.BlockSpec((outs[out][0], outs[out][2]), chain(at)))
    flops = 0
    for lhs, rhs, span, block, out, out_block, plus in steps:
        flops += 2 * lhs.shape[0] * lhs.shape[1] * span
        plan.append(
            (
                place[("in", id(lhs), lhs.shape[1])],
                place[("in", id(rhs), span)],
                first_out + out_names.index(out),
                None if plus is None else place[("in", id(plus), outs[out][2])],
            )
        )
    results = pl.pallas_call(
        functools.partial(product_kernel, plan),
        grid_spec=pltpu.PrefetchScalarGridSpec(
            num_scalar_prefetch=1,
            grid=(total,),
            in_specs=specs + [pl.BlockSpec(memory_space=pl.ANY)] * len(waits),
            out_specs=out_specs,
        ),
        out_shape=[jax.ShapeDtypeStruct(outs[out][:2], LOW) for out in out_names],
        compiler_params=pltpu.CompilerParams(vmem_limit_bytes=VMEM_LIMIT),
        cost_estimate=pl.CostEstimate(flops=flops, bytes_accessed=flops // 300, transcendentals=0),
        name=name,
    )(side, *arrays, *waits)
    return dict(zip(out_names, results))


def hold_kernel(*refs):
    del refs


def hold(tensor, *waits):
    anywhere = pl.BlockSpec(memory_space=pl.ANY)
    return pl.pallas_call(
        hold_kernel,
        in_specs=[anywhere] * (1 + len(waits)),
        out_specs=anywhere,
        out_shape=jax.ShapeDtypeStruct(tensor.shape, tensor.dtype),
        input_output_aliases={0: 0},
        cost_estimate=pl.CostEstimate(flops=0, bytes_accessed=0, transcendentals=0),
        name="hold",
    )(tensor, *waits)


def place_kernel(count, place_ref, *refs):
    out_ref = refs[-1]
    for index in range(count):
        out_ref[place_ref[index]] = refs[index][...]


def place_call(name, parts, spots, waits):
    shape = (len(parts), *parts[0].shape)
    return pl.pallas_call(
        functools.partial(place_kernel, len(parts)),
        in_specs=[pl.BlockSpec(memory_space=pltpu.SMEM)]
        + [pl.BlockSpec(memory_space=pltpu.VMEM)] * len(parts)
        + [pl.BlockSpec(memory_space=pl.ANY)] * len(waits),
        out_specs=pl.BlockSpec(memory_space=pltpu.VMEM),
        out_shape=jax.ShapeDtypeStruct(shape, parts[0].dtype),
        compiler_params=pltpu.CompilerParams(vmem_limit_bytes=VMEM_LIMIT),
        cost_estimate=pl.CostEstimate(flops=0, bytes_accessed=4 * parts[0].size * len(parts), transcendentals=0),
        name=name,
    )(jnp.stack(spots).astype(jnp.int32), *parts, *waits)


def weave_kernel(count, place_ref, *refs):
    out_ref = refs[-1]
    for index in range(count):
        for row in range(refs[index].shape[0]):
            out_ref[row, place_ref[index]] = refs[index][row]


def weave_call(name, parts, spots, waits):
    lead, *rest = parts[0].shape
    return pl.pallas_call(
        functools.partial(weave_kernel, len(parts)),
        in_specs=[pl.BlockSpec(memory_space=pltpu.SMEM)]
        + [pl.BlockSpec(memory_space=pltpu.VMEM)] * len(parts)
        + [pl.BlockSpec(memory_space=pl.ANY)] * len(waits),
        out_specs=pl.BlockSpec(memory_space=pltpu.VMEM),
        out_shape=jax.ShapeDtypeStruct((lead, len(parts), *rest), parts[0].dtype),
        compiler_params=pltpu.CompilerParams(vmem_limit_bytes=VMEM_LIMIT),
        cost_estimate=pl.CostEstimate(flops=0, bytes_accessed=4 * parts[0].size * len(parts), transcendentals=0),
        name=name,
    )(jnp.stack(spots).astype(jnp.int32), *parts, *waits)


class Grid:
    def __init__(self, mesh):
        self.blocks = mesh.shape["blk"]
        self.total = mesh.shape["dp"]
        self.paired = self.blocks == 2 and self.total == 16
        self.high = 4
        self.low = self.total // 8

    def place(self):
        index = lax.axis_index("dp")
        self.core_at = index % 2
        self.low_at = index // 2 % self.low
        self.high_at = index // (2 * self.low)
        self.block_at = lax.axis_index("blk")

    def from_core(self, tensor):
        return lax.ppermute(tensor, "dp", [(i, i ^ 1) for i in range(self.total)])

    def from_block(self, tensor):
        return lax.ppermute(tensor, "blk", [(0, 1), (1, 0)])

    def from_low(self, tensor, step):
        span = 2 * self.low
        pairs = [(i, i // span * span + (i + 2 * step) % span) for i in range(self.total)]
        return lax.ppermute(tensor, "dp", pairs)

    def from_high(self, tensor, step):
        return lax.ppermute(tensor, "dp", [(i, (i + 2 * self.low * step) % self.total) for i in range(self.total)])

    def gather(self, shard):
        return lax.all_gather(shard, "dp", axis=0, tiled=True)

    def gather_chip(self, shards, waits):
        rows, columns = shards[0].shape
        width = columns // 4

        def quarter(core):
            first = (2 * self.block_at + core) * width
            parts = [lax.dynamic_slice_in_dim(shard, first, width, 1) for shard in shards]
            return jnp.concatenate(parts, axis=1) if len(parts) > 1 else parts[0]

        mine = quarter(self.core_at)
        other = self.from_core(quarter(1 - self.core_at))
        chip = place_call("chip_rows", [mine, other], [self.core_at, 1 - self.core_at], waits)
        return chip.reshape(2 * rows, -1)

    def gather_line(self, chip, waits):
        parts = [chip] + [self.from_high(chip, step) for step in range(1, self.high)]
        spots = [(self.high_at - step) % self.high for step in range(self.high)]
        return place_call("line_rows", parts, spots, waits)

    def gather_sheet(self, line, waits):
        parts = [line] + [self.from_low(line, step) for step in range(1, self.low)]
        spots = [(self.low_at - step) % self.low for step in range(self.low)]
        return weave_call("sheet_rows", parts, spots, waits).reshape(-1, line.shape[2])

    def scatter_begin(self, tensor, axis):
        size, index, send = (
            (self.low, self.low_at, self.from_low) if axis == 1 else (self.high, self.high_at, self.from_high)
        )

        def at(step):
            return lax.dynamic_index_in_dim(tensor, (index + step) % size, axis, False)

        return at(0), [send(at(step), step) for step in range(1, size)]

    def low_begin(self, tensor):
        rows, columns = tensor.shape
        return self.scatter_begin(tensor.reshape(self.high, self.low, -1, columns), 1)

    def high_begin(self, tensor):
        return self.scatter_begin(tensor, 0)

    def scatter_end(self, begun, *waits):
        own, arrived = begun
        if waits:
            arrived = [hold(arrived[0], *waits), *arrived[1:]]
        return sum((tensor.astype(F32) for tensor in arrived), own.astype(F32)).astype(LOW)

    def sum_blocks(self, tensor):
        return (tensor.astype(F32) + self.from_block(tensor).astype(F32)).astype(LOW)

    def halves(self, tensor):
        rows = tensor.shape[0] // 2
        own = lax.dynamic_slice_in_dim(tensor, self.core_at * rows, rows, 0)
        other = self.from_core(lax.dynamic_slice_in_dim(tensor, (1 - self.core_at) * rows, rows, 0))
        first = self.core_at == 0
        return jnp.where(first, own, other), jnp.where(first, other, own)

    def sum_all(self, tensor):
        if not self.paired or self.total & (self.total - 1):
            return lax.psum(tensor, ("blk", "dp"))
        tensor = tensor + self.from_block(tensor)
        bit = 1
        while bit < self.total:
            tensor = tensor + lax.ppermute(tensor, "dp", [(i, i ^ bit) for i in range(self.total)])
            bit *= 2
        return tensor

    def scatter(self, tensor):
        part = lax.psum_scatter(tensor, "dp", scatter_dimension=0, tiled=True)
        if self.blocks == 2:
            return part.astype(F32) + self.from_block(part).astype(F32)
        return lax.psum(part, "blk").astype(F32)


def shards(
    grid,
    content_in,
    query_in,
    cot_content,
    cot_query,
    attn_weights,
    out_weight,
    ffn_in,
    ffn_out_t,
    norm_gains,
    norm_shifts,
    bias_table,
    permutation,
    predicted,
    doc_lengths,
):
    _, rows, width = content_in.shape
    length = permutation.shape[1]
    blocks = length // rows
    bucket_count, head_count = bias_table.shape
    layer_count = attn_weights.shape[0]
    grid.place()
    block_index = grid.block_at

    anchor = permutation[0]
    positions = jnp.arange(length, dtype=jnp.int32)
    bounds = jnp.cumsum(doc_lengths[0])[:-1].astype(jnp.int32)
    key_doc = jnp.sum((positions[:, None] >= bounds[None, :]).astype(jnp.int32), axis=1)
    starts = (positions == 0) | jnp.any(positions[:, None] == bounds[None, :], axis=1)
    live = (predicted[0] == 1) & jnp.logical_not(starts)
    position_rank = jnp.sum(
        jnp.where(anchor[None, :] == positions[:, None], positions[None, :], 0), axis=1
    )
    key_rank = jnp.where(live, position_rank, -1)
    split = anchor.reshape(blocks, rows)
    order = jnp.sum((split[:, None, :] < split[:, :, None]).astype(jnp.int32), axis=2)
    sorted_place = jnp.sum(
        jnp.where(order[:, None, :] == jnp.arange(rows)[None, :, None], split[:, None, :], 0), axis=2
    )
    own_order = lax.dynamic_index_in_dim(order, block_index, 0, False)
    place = lax.dynamic_index_in_dim(sorted_place, block_index, 0, False)
    sorter = (own_order[None, :] == jnp.arange(rows)[:, None]).astype(LOW)
    if grid.paired:
        own_spread, other_spread = (
            (lax.dynamic_index_in_dim(sorted_place, side, 0, True) == positions[:, None]).astype(LOW)
            for side in (block_index, 1 - block_index)
        )
    spread = (sorted_place.reshape(1, length) == positions[:, None]).astype(LOW)
    at_place = (place[:, None] == positions[None, :]).astype(jnp.int32)
    place_doc = jnp.sum(at_place * key_doc[None, :], axis=1)
    place_rank = jnp.sum(at_place * position_rank[None, :], axis=1)
    place_live = jnp.sum(at_place * live.astype(jnp.int32)[None, :], axis=1)
    own_column = jnp.where(place_live == 1, place, -1)[:, None]
    place_column = place[:, None]
    table_rows = jnp.concatenate(
        [bias_table.T, jnp.full((head_count, 128 - bucket_count), MASKED, F32)], axis=1
    )

    def sort_rows(tensor):
        return dot_nn(sorter, tensor).astype(LOW)

    def other_blocks(tensor):
        if grid.paired:
            other = grid.from_block(tensor)
            return (dot_nn(own_spread, tensor) + dot_nn(other_spread, other)).astype(LOW)
        gathered = lax.all_gather(tensor, "blk", axis=0, tiled=True)
        return dot_nn(spread, gathered).astype(LOW)

    paired = grid.paired
    first_qkv = grid.gather(attn_weights[0])
    others = jnp.concatenate(
        [out_weight[layer_index] for layer_index in range(layer_count)]
        + [attn_weights[layer_index] for layer_index in range(1, layer_count)],
        axis=1,
    )
    others = grid.gather(others)
    starts = [(layer_count + 3 * layer_index) * width for layer_index in range(layer_count - 1)]
    attn_full = [first_qkv] + [others[:, start : start + 3 * width] for start in starts]
    hidden = ffn_in.shape[2]
    span = hidden // 4 if paired else hidden

    def chip_of(layer_index, *waits):
        return grid.gather_chip((ffn_in[layer_index], ffn_out_t[layer_index]), waits)

    stream_low = jnp.concatenate([sort_rows(content_in[0]), sort_rows(query_in[0])], axis=0)
    stream = stream_low.astype(F32)
    if paired:
        chip = chip_of(0)
    bias = bias_call(
        table_rows, place_column, place_doc[:, None], place_rank[:, None], key_doc[None], key_rank[None],
        *((chip, stream_low) if paired else ()),
    )
    if paired:
        line = grid.gather_line(chip, (bias,))
        if layer_count > 1:
            next_chip = chip_of(1, line)
    kept = []
    all_pieces = []
    for layer_index in range(layer_count):
        qkv = attn_full[layer_index]
        all_content = other_blocks(stream_low[:rows])
        queries = dot_nn(stream_low, qkv[:, :width]).astype(LOW).reshape(2, rows, width)
        keys = dot_nn(all_content, qkv[:, width : 2 * width]).astype(LOW)
        values = dot_nn(all_content, qkv[:, 2 * width :]).astype(LOW)
        later = ()
        more = paired and layer_index + 1 < layer_count
        if paired:
            sheet = grid.gather_sheet(line, (queries, keys, values))
            later = (sheet,)
        if more:
            later = (sheet, next_chip)
        out, out_low, weights = attend_call(queries, keys, values, bias, own_column, *later)
        later = ()
        if paired:
            waits_near = (out_low,)
            if more:
                line = grid.gather_line(next_chip, (out_low,))
                waits_near = (out_low, line)
            near = hold(grid.from_block(sheet), *waits_near)
            quarters = (sheet, grid.from_core(sheet), near, grid.from_core(near))
            pieces = [((quarter, 0), (quarter, span)) for quarter in quarters]
        else:
            pieces = [((grid.gather(ffn_in[layer_index]), 0), (grid.gather(ffn_out_t[layer_index]), 0))]
        all_pieces.append(pieces)
        if more:
            later = (line,)
            if layer_index + 2 < layer_count:
                next_chip = chip_of(layer_index + 2, line)
        out_low = out_low.reshape(2 * rows, width)
        result, low, middle, middle_low, active, slope, inverse_one, inverse_two = layer_tail_call(
            stream, out_low, (others, layer_index), pieces, span,
            norm_gains[layer_index], norm_shifts[layer_index], *later,
        )
        kept.append(
            (
                stream_low, all_content, queries, keys, values, out, out_low, weights,
                result, middle, middle_low, active, slope, inverse_one, inverse_two,
            )
        )
        stream, stream_low = result, low

    def unsort(tensor):
        return dot_tn(sorter, tensor)

    def unsort_wide(tensor):
        high = tensor.astype(LOW)
        rest = (tensor - high.astype(F32)).astype(LOW)
        return unsort(high) + unsort(rest)

    content_out = unsort(stream_low[:rows]).astype(LOW)
    query_out = unsort(stream_low[rows:]).astype(LOW)

    grad_stream = [sort_rows(cot_content[0]).astype(F32), sort_rows(cot_query[0]).astype(F32)]
    norm_terms = [None] * layer_count
    matrix_rows = [None] * layer_count
    side = jnp.full((1,), grid.core_at, jnp.int32)
    pairs = width // 128
    score_sum = None
    pending = {}
    third = width // 2

    def keys_back(grad_k, grad_v, qkv):
        return (dot_nt(grad_k, qkv[:, width : 2 * width]) + dot_nt(grad_v, qkv[:, 2 * width :])).astype(LOW)

    def finish_rows(high):
        shared = grid.sum_blocks(high[:, 2 * span :])
        sides = grid.halves(jnp.concatenate([high[:, : 2 * span], shared], axis=1))
        proj_grad = jnp.concatenate([one[:, 2 * span : 2 * span + third] for one in sides], axis=1)
        attn_grad = jnp.concatenate(
            [
                one[:, 2 * span + (1 + index) * third : 2 * span + (2 + index) * third]
                for index in range(3)
                for one in sides
            ],
            axis=1,
        )
        half = jnp.concatenate([one[:, : 2 * span] for one in sides], axis=1)
        other = grid.from_block(half)
        first = grid.block_at == 0
        quarters = (jnp.where(first, half, other), jnp.where(first, other, half))
        inner_grad, outer_grad = (
            jnp.concatenate(
                [
                    one[:, (2 * core + which) * span : (2 * core + which + 1) * span]
                    for one in quarters
                    for core in range(2)
                ],
                axis=1,
            )
            for which in range(2)
        )
        return tuple(tensor.astype(F32) for tensor in (attn_grad, proj_grad, inner_grad, outer_grad))

    def waits(*names):
        return [pending[name] for name in names if name in pending]

    for layer_index in reversed(range(layer_count)):
        (
            stream_low, all_content, queries, keys, values, out, out_low, weights,
            result, middle, middle_low, active, slope, inverse_one, inverse_two,
        ) = kept[layer_index]
        qkv = attn_full[layer_index]
        partial = None
        for part in (None,) if layer_index == layer_count - 1 else (1, 0):
            grad = jnp.concatenate(grad_stream, axis=0) if part is None else grad_stream[part]
            partial = layer_tail_back_call(
                grad, result, inverse_two, middle, inverse_one, slope, (others, layer_index),
                all_pieces[layer_index], span, norm_gains[layer_index], norm_shifts[layer_index],
                part, partial, *waits("sum"),
            )
        two_low, inner_low, grad_one, branch_low, grad_out, norm_terms[layer_index] = partial
        grad_out = grad_out.reshape(2, rows, width)
        back = (queries, keys, values, grad_out, out, weights, score_sum)
        if paired:
            def steps(name, quarter, come=None):
                return [
                    (middle_low, inner_low, span, quarter, name, 0, come),
                    (two_low, active, span, quarter, name, 1, come),
                ]

            sent = products_call(
                "products_sent", side,
                steps("far", 3) + steps("beside", 1) + [(out_low, branch_low, third, "other", "proj", 0, None)],
                {"far": (width, 2 * span, span), "beside": (width, 2 * span, span), "proj": (width, third, third)},
                (),
            )
            come = {name: grid.from_core(tensor) for name, tensor in sent.items()}
            near = products_call(
                "products_near", side, steps("near", 2, come["far"]), {"near": (width, 2 * span, span)}
            )["near"]
            arrived = grid.from_block(near)
            held = products_call(
                "products_held", side,
                steps("mine", 0, come["beside"]) + [(out_low, branch_low, third, "side", "proj", 0, come["proj"])],
                {"mine": (width, 2 * span, span), "proj": (width, third, third)},
                [near],
            )
            partial = attend_back_call((0, pairs // 2), *back, None, *held.values())
            if "low_begun" in pending:
                pending["low"] = grid.scatter_end(pending["low_begun"], partial[0])
                pending["high_begun"] = grid.high_begin(pending["low"])
            grad_q, grad_k, grad_v, score_sum = attend_back_call(
                (pairs // 2, pairs - pairs // 2), *back, partial, *waits("low")
            )
            grad_q = grad_q.reshape(2 * rows, width)
            ffn_sum = (held["mine"].astype(F32) + arrived.astype(F32)).astype(LOW)
            if layer_index == 0:
                ffn_sum = jnp.concatenate([ffn_sum, held["proj"]], axis=1)
                ffn_begun = grid.low_begin(ffn_sum)
            if layer_index > 0:
                grad_all = keys_back(grad_k, grad_v, qkv)
                passed = dot_tn(other_spread, grad_all).astype(LOW)
            attn = products_call(
                "products_attn", side,
                [
                    (lhs, rhs, third, block, out_name, index, None)
                    for block, out_name in (("other", "sent"), ("side", "mine"))
                    for index, (lhs, rhs) in enumerate(
                        ((stream_low, grad_q), (all_content, grad_k), (all_content, grad_v))
                    )
                ],
                {"sent": (width, 3 * third, third), "mine": (width, 3 * third, third)},
                [passed, ffn_sum] if layer_index > 0 else [ffn_sum],
            )
            attn_sum = (attn["mine"].astype(F32) + grid.from_core(attn["sent"]).astype(F32)).astype(LOW)
            if layer_index == 0:
                grad_q, grad_k, grad_v = (hold(tensor, attn["sent"]) for tensor in (grad_q, grad_k, grad_v))
                grad_all = keys_back(grad_k, grad_v, qkv)
                passed = dot_tn(other_spread, grad_all).astype(LOW)
            if "high_begun" in pending:
                high = grid.scatter_end(pending["high_begun"], attn["sent"])
                matrix_rows[layer_index + 1] = finish_rows(high)
            if layer_index > 0:
                total = jnp.concatenate([ffn_sum, held["proj"], attn_sum], axis=1)
                pending = {"attn_sent": attn["sent"], "sum": total, "low_begun": grid.low_begin(total)}
            else:
                attn_begun = grid.low_begin(attn_sum)
                ffn_low = grid.scatter_end(ffn_begun, attn["sent"])
                ffn_begun = grid.high_begin(ffn_low)
                pending = {"attn_sum": attn_sum, "ffn_low": ffn_low}
        else:
            grad_q, grad_k, grad_v, score_sum = attend_back_call((0, pairs), *back, None)
            grad_q = grad_q.reshape(2 * rows, width)
            terms = [
                jnp.concatenate(
                    [dot_tn(stream_low, grad_q), dot_tn(all_content, grad_k), dot_tn(all_content, grad_v)], axis=1
                ),
                dot_tn(out_low, branch_low),
                dot_tn(middle_low, inner_low),
                dot_tn(two_low, active),
            ]
            matrix_rows[layer_index] = tuple(grid.scatter(term.astype(LOW)) for term in terms)
        query_side = grad_one + dot_nt(grad_q, qkv[:, :width])
        if layer_index == 0:
            table_grad = table_call([score_sum], place_column, bucket_count, *waits("attn_sum", "ffn_low"))
        if paired:
            come = grid.from_block(passed)
            if layer_index == 0:
                come = hold(come, table_grad)
            grad_keys_in = dot_tn(own_spread, grad_all) + come.astype(F32)
        else:
            grad_split = dot_tn(spread, keys_back(grad_k, grad_v, qkv)).astype(LOW)
            grad_keys_in = lax.psum_scatter(grad_split, "blk", scatter_dimension=0, tiled=True).astype(F32)
        grad_stream = [query_side[:rows] + grad_keys_in, query_side[rows:]]
    if paired:
        attn_begun = grid.high_begin(grid.scatter_end(attn_begun, table_grad))
        high = jnp.concatenate([grid.scatter_end(ffn_begun, table_grad), grid.scatter_end(attn_begun)], axis=1)
        matrix_rows[0] = finish_rows(high)
    table_lines = jnp.pad(table_grad.T, ((0, 0), (0, width - bucket_count)))
    sums = grid.sum_all(jnp.concatenate([*[terms[:4] for terms in norm_terms], table_lines], axis=0))
    norm_sum = sums[: 4 * layer_count].reshape(layer_count, 2, 2, width)
    table_total = sums[4 * layer_count :, :bucket_count].T
    matrix_grads = tuple(jnp.stack(layers, axis=0) for layers in zip(*matrix_rows))
    return (
        content_out[None],
        query_out[None],
        unsort_wide(grad_stream[0])[None],
        unsort_wide(grad_stream[1])[None],
        *matrix_grads,
        norm_sum[:, 0],
        norm_sum[:, 1],
        table_total,
    )


def solution(mesh):
    tokens = P("dp", "blk", None)
    matrix = P(None, "dp", None)
    whole = P()
    sequence = P("dp", None)
    return jax.shard_map(
        functools.partial(shards, Grid(mesh)),
        mesh=mesh,
        in_specs=(tokens,) * 4 + (matrix,) * 4 + (whole,) * 3 + (sequence,) * 3,
        out_specs=(tokens,) * 4 + (matrix,) * 4 + (whole,) * 3,
        check_vma=False,
    )
```

```python
import functools

import jax
import jax.numpy as jnp
from jax import lax
from jax.experimental import pallas as pl
from jax.experimental.pallas import tpu as pltpu
from jax.sharding import PartitionSpec as P

THRESHOLDS = (12, 16, 23, 32, 46, 64, 91)
MASKED = -1e30
F32 = jnp.float32
LOW = jnp.bfloat16
VMEM_LIMIT = 56 * 2**20
ROW_TILE = 128
PAIRS = 2


def dot_nn(left_side, right_side):
    return jnp.dot(left_side, right_side, preferred_element_type=F32)


def dot_nt(left_side, right_side):
    return lax.dot_general(left_side, right_side, (((1,), (1,)), ((), ())), preferred_element_type=F32)


def dot_tn(left_side, right_side):
    return lax.dot_general(left_side, right_side, (((0,), (0,)), ((), ())), preferred_element_type=F32)


def bucket_of(relative):
    distance = jnp.abs(relative)
    far_bucket = 8 + sum(((distance >= threshold).astype(jnp.int32) for threshold in THRESHOLDS))
    near_bucket = jnp.where(distance < 8, distance, jnp.minimum(far_bucket, 15))
    return jnp.where(relative > 0, 16, 0).astype(jnp.int32) + near_bucket


def window_counts(length):
    most = length // 128
    return [count for count in (2, 3, 4, 5, 6) if count < most] + [most]


def by_window(window_ref, tile, length, step):
    def one(at, carry):
        row = pl.multiple_of(at * tile, tile)
        first = pl.multiple_of(window_ref[0, at] * 128, 128)
        for count in window_counts(length):

            @pl.when(window_ref[1, at] == count)
            def _(count=count):
                step(pl.ds(row, tile), pl.ds(first, count * 128), count * 128, first)

        return carry

    lax.fori_loop(0, window_ref.shape[1], one, 0)


def setup_kernel(side_ref, lengths_ref, row_ref, column_ref, chosen_ref, *refs):
    streams, refs = refs[:4], refs[4:]
    outs = refs[-(11 + side_ref.shape[0]) :]
    window_ref, key_doc_ref, key_rank_ref, place_ref, doc_ref, rank_ref, own_ref, sorter_ref, low_ref, grad_ref = outs[:10]
    spread_refs = outs[10:-1]
    rank_row = outs[-1]
    length, rows = row_ref.shape[1], streams[0].shape[0]
    for first in range(0, length, 128):
        position = (first + lax.broadcasted_iota(jnp.int32, (length, 128), 1))
        rank = lax.broadcasted_iota(jnp.int32, (length, 128), 0).astype(F32)
        rank_row[:, first : first + 128] = jnp.sum(
            jnp.where(column_ref[...] == position, rank, 0.0), axis=0, keepdims=True
        )
    ranks = rank_row[...]
    position = lax.broadcasted_iota(jnp.int32, (1, length), 1)
    doc = jnp.zeros((1, length), jnp.int32)
    start = position == 0
    bound = 0
    for index in range(lengths_ref.shape[1] - 1):
        bound = bound + lengths_ref[0, index]
        doc = doc + (position >= bound).astype(jnp.int32)
        start = start | (position == bound)
    live = (chosen_ref[...] == 1) & jnp.logical_not(start)
    key_doc_ref[...] = doc
    key_rank_ref[...] = jnp.where(live, ranks, -1.0).astype(jnp.int32)
    below = (
        lax.broadcasted_iota(jnp.int32, (length, length), 0) <= lax.broadcasted_iota(jnp.int32, (length, length), 1)
    )
    below = jnp.where(below, 1.0, 0.0).astype(LOW)
    slot = lax.broadcasted_iota(jnp.int32, (rows, length), 0).astype(F32)
    for index, spread_ref in enumerate(spread_refs):
        least = (side_ref[index] * rows).astype(F32)
        owned = (ranks >= least) & (ranks < least + rows)
        counted = jnp.broadcast_to(jnp.where(owned, 1.0, 0.0), (8, length)).astype(LOW)
        order = jnp.where(owned, dot_nn(counted, below)[0:1] - 1.0, -1.0)
        chosen = slot == order
        spread_ref[...] = jnp.where(chosen, 1.0, 0.0).astype(LOW)
        if index == 0:

            def pick(row):
                return jnp.sum(jnp.where(chosen, row, 0.0), axis=1, keepdims=True)

            place = pick(position.astype(F32))
            rank = pick(ranks)
            place_ref[...] = place.astype(jnp.int32)
            rank_ref[...] = rank.astype(jnp.int32)
            doc_ref[...] = pick(doc.astype(F32)).astype(jnp.int32)
            own_ref[...] = jnp.where(pick(jnp.where(live, 1.0, 0.0)) > 0.0, place, -1.0).astype(jnp.int32)
            tile = rows // window_ref.shape[1]
            for at in range(window_ref.shape[1]):
                lines = place[at * tile : (at + 1) * tile]
                least_place = jnp.min(lines).astype(jnp.int32)
                most_place = jnp.max(lines).astype(jnp.int32)
                first, last, bound = 0, length, 0
                for doc_index in range(lengths_ref.shape[1] - 1):
                    bound = bound + lengths_ref[0, doc_index]
                    first = jnp.where(least_place >= bound, bound, first)
                    last = jnp.where((most_place < bound) & (last == length), bound, last)
                first = first // 128
                needed = (last + 127) // 128 - first
                count = length // 128
                for choice in reversed(window_counts(length)):
                    count = jnp.where(needed <= choice, choice, count)
                window_ref[0, at] = jnp.minimum(first, length // 128 - count)
                window_ref[1, at] = count
            spot = lax.broadcasted_iota(jnp.int32, (rows, rows), 1).astype(F32)
            sorter = jnp.where(spot == rank - least, 1.0, 0.0).astype(LOW)
            sorter_ref[...] = sorter
    for index, stream in enumerate(streams):
        target = (low_ref, grad_ref)[index // 2]
        target[index % 2 * rows : (index % 2 + 1) * rows] = dot_nn(sorter, stream[...]).astype(LOW)


def setup_call(sides, lengths, anchor, chosen, streams, *waits):
    length = anchor.shape[1]
    rows, width = streams[0].shape
    count = sides.shape[0]
    here = pl.BlockSpec(memory_space=pltpu.VMEM)
    scalars = pl.BlockSpec(memory_space=pltpu.SMEM)

    def whole(lines, columns, kind):
        return jax.ShapeDtypeStruct((lines, columns), kind)

    return pl.pallas_call(
        setup_kernel,
        in_specs=[scalars, scalars, here, here, here] + [here] * 4 + [pl.BlockSpec(memory_space=pl.ANY)] * len(waits),
        out_specs=[scalars] + [here] * (9 + count),
        out_shape=[whole(2, rows // min(ROW_TILE, rows), jnp.int32)]
        + [whole(1, length, jnp.int32)] * 2
        + [whole(rows, 1, jnp.int32)] * 4
        + [whole(rows, rows, LOW), whole(2 * rows, width, LOW), whole(2 * rows, width, LOW)]
        + [whole(rows, length, LOW)] * count,
        scratch_shapes=[pltpu.VMEM((1, length), F32)],
        compiler_params=pltpu.CompilerParams(vmem_limit_bytes=VMEM_LIMIT),
        cost_estimate=pl.CostEstimate(flops=8 * rows * rows * width, bytes_accessed=16 * rows * width, transcendentals=0),
        name="setup_rows",
    )(sides, lengths, anchor, anchor.reshape(length, 1), chosen, *streams, *waits)


def bias_kernel(window_ref, table_ref, place_ref, doc_ref, rank_ref, key_doc_ref, key_rank_ref, *refs):
    out_ref = refs[-1]
    head_count, rows, length = out_ref.shape
    place = place_ref[...]
    doc = doc_ref[...]
    rank = rank_ref[...]
    at = pl.program_id(0) * window_ref.shape[1] // pl.num_programs(0)
    for block in range(length // 128):
        first = block * 128

        @pl.when((block >= window_ref[0, at]) & (block < window_ref[0, at] + window_ref[1, at]))
        def _(first=first):
            key_place = first + lax.broadcasted_iota(jnp.int32, (rows, 128), 1)
            seen = (key_doc_ref[:, first : first + 128] == doc) & (
                key_rank_ref[:, first : first + 128] <= rank
            )
            choice = jnp.where(seen, bucket_of(key_place - place), 32)
            for head in range(head_count):
                line = jnp.broadcast_to(table_ref[head : head + 1, :], (8, 128))
                for row in range(0, rows, 8):
                    out_ref[head, row : row + 8, first : first + 128] = jnp.take_along_axis(
                        line, choice[row : row + 8], axis=1
                    )


def bias_call(window, table_rows, place, doc, rank, key_doc, key_rank, *waits):
    head_count = table_rows.shape[0]
    rows, length = place.shape[0], key_doc.shape[1]
    tile = min(64, rows)
    column = pl.BlockSpec((tile, 1), lambda i: (i, 0))
    line = pl.BlockSpec((1, length), lambda i: (0, 0))
    return pl.pallas_call(
        bias_kernel,
        grid=(rows // tile,),
        in_specs=[
            pl.BlockSpec(memory_space=pltpu.SMEM),
            pl.BlockSpec((head_count, 128), lambda i: (0, 0)),
            column,
            column,
            column,
            line,
            line,
        ]
        + [pl.BlockSpec(memory_space=pl.ANY)] * len(waits),
        out_specs=pl.BlockSpec((head_count, tile, length), lambda i: (0, i, 0)),
        out_shape=jax.ShapeDtypeStruct((head_count, rows, length), F32),
        compiler_params=pltpu.CompilerParams(vmem_limit_bytes=VMEM_LIMIT),
        cost_estimate=pl.CostEstimate(
            flops=0, bytes_accessed=head_count * rows * length * 8, transcendentals=0
        ),
        name="bias_rows",
    )(window, table_rows, place, doc, rank, key_doc, key_rank, *waits)


def attend_kernel(window_ref, q_ref, k_ref, v_ref, bias_ref, own_ref, *refs):
    o_ref, low_ref, p_ref = refs[-3:]
    length = bias_ref.shape[2]
    tile = bias_ref.shape[1] // window_ref.shape[1]
    heads = range(bias_ref.shape[0])

    def step(lines, columns, span, first):
        first_half = lax.broadcasted_iota(jnp.int32, (2 * tile, 128), 1) < 64
        zero = jnp.zeros((2 * tile, 128), LOW)
        hidden = lax.broadcasted_iota(jnp.int32, (tile, span), 1) == own_ref[lines, :] - first
        mine = []
        for head in heads:
            lanes = slice(head // 2 * 128, head // 2 * 128 + 128)
            queries = q_ref[:, lines, lanes].reshape(2 * tile, 128) * jnp.array(0.125, LOW)
            mine.append(jnp.where(first_half, queries, zero) if head % 2 == 0 else jnp.where(first_half, zero, queries))
        raw = [dot_nt(mine[head], k_ref[columns, head // 2 * 128 : head // 2 * 128 + 128]) for head in heads]
        scores = []
        for head in heads:
            bias = bias_ref[head, lines, columns]
            scores.append((raw[head][:tile] + bias, jnp.where(hidden, MASKED, raw[head][tile:] + bias)))
        most = [[jnp.max(part, axis=1, keepdims=True) for part in pair] for pair in scores]
        weights = [[jnp.exp(part - top) for part, top in zip(pair, tops)] for pair, tops in zip(scores, most)]
        shares = [[1.0 / jnp.sum(part, axis=1, keepdims=True) for part in pair] for pair in weights]
        lows = [[(part * share).astype(LOW) for part, share in zip(pair, both)] for pair, both in zip(weights, shares)]
        parts = []
        for head in heads:
            for stream in range(2):
                p_ref[head, stream, lines, columns] = lows[head][stream]
            values = v_ref[columns, head // 2 * 128 : head // 2 * 128 + 128]
            parts.append(dot_nn(jnp.concatenate(lows[head], axis=0), values))
        for pair in range(len(heads) // 2):
            lanes = slice(pair * 128, pair * 128 + 128)
            out = jnp.where(first_half, parts[2 * pair], parts[2 * pair + 1])
            o_ref[:, lines, lanes] = out.reshape(2, tile, 128)
            low_ref[:, lines, lanes] = out.astype(LOW).reshape(2, tile, 128)

    by_window(window_ref, tile, length, step)


def attend_call(window, queries, keys, values, bias, own, *waits):
    _, rows, width = queries.shape
    length = keys.shape[0]
    pairs = width // 128
    group = PAIRS
    per_row = pl.BlockSpec((2, rows, 128 * group), lambda h: (0, 0, h))
    per_key = pl.BlockSpec((length, 128 * group), lambda h: (0, h))
    return pl.pallas_call(
        attend_kernel,
        grid=(pairs // group,),
        in_specs=[
            pl.BlockSpec(memory_space=pltpu.SMEM),
            per_row,
            per_key,
            per_key,
            pl.BlockSpec((2 * group, rows, length), lambda h: (h, 0, 0)),
            pl.BlockSpec((rows, 1), lambda h: (0, 0)),
        ]
        + [pl.BlockSpec(memory_space=pl.ANY)] * len(waits),
        out_specs=[
            per_row,
            per_row,
            pl.BlockSpec((2 * group, 2, rows, length), lambda h: (h, 0, 0, 0)),
        ],
        out_shape=[
            jax.ShapeDtypeStruct((2, rows, width), F32),
            jax.ShapeDtypeStruct((2, rows, width), LOW),
            jax.ShapeDtypeStruct((2 * pairs, 2, rows, length), LOW),
        ],
        compiler_params=pltpu.CompilerParams(vmem_limit_bytes=VMEM_LIMIT),
        cost_estimate=pl.CostEstimate(
            flops=16 * rows * length * width,
            bytes_accessed=pairs * rows * length * 16,
            transcendentals=4 * pairs * rows * length,
        ),
        name="attend",
    )(window, queries, keys, values, bias, own, *waits)


def attend_back_kernel(window_ref, *refs):
    q_ref, k_ref, v_ref, do_ref, o_ref, p_ref = refs[:6]
    dq_ref, dk_ref, dv_ref, sum_ref, dk_sum, dv_sum = refs[-6:]
    rows, length = sum_ref.shape[1:]
    tile = rows // window_ref.shape[1]
    dk_sum[...] = jnp.zeros_like(dk_sum)
    dv_sum[...] = jnp.zeros_like(dv_sum)

    def step(lines, columns, span, first):
        first_half = lax.broadcasted_iota(jnp.int32, (2 * tile, 128), 1) < 64
        zero = jnp.zeros((2 * tile, 128), LOW)
        queries = q_ref[:, lines, :].reshape(2 * tile, 128) * jnp.array(0.125, LOW)
        grad_out = do_ref[:, lines, :].reshape(2 * tile, 128)
        out = o_ref[:, lines, :].reshape(2 * tile, 128)
        queries_t, grad_out_t = queries.T, grad_out.T
        keys, values = k_ref[columns, :], v_ref[columns, :]
        heads = [slice(0, 64), slice(64, 128)]
        mine = [jnp.where(first_half, grad_out, zero), jnp.where(first_half, zero, grad_out)]
        raw = [dot_nt(part, values) for part in mine]
        low_p = [p_ref[half, :, lines, columns].reshape(2 * tile, span) for half in range(2)]
        for half in range(2):
            dv_sum[heads[half], columns] += dot_nn(grad_out_t[heads[half]], low_p[half])
        delta = [jnp.sum(part.astype(F32) * out, axis=1, keepdims=True) for part in mine]
        grads = [low_p[half].astype(F32) * (raw[half] - delta[half]) for half in range(2)]
        lows = [grad.astype(LOW) for grad in grads]
        parts = [dot_nn(low, keys) for low in lows]
        for half in range(2):
            sum_ref[half, lines, columns] = (grads[half][:tile] + grads[half][tile:]).astype(LOW)
            dk_sum[heads[half], columns] += dot_nn(queries_t[heads[half]], lows[half])
        grad_q = (jnp.where(first_half, parts[0], parts[1]) * 0.125).astype(LOW)
        dq_ref[:, lines, :] = grad_q.reshape(2, tile, 128)

    by_window(window_ref, tile, length, step)
    dk_ref[...] = dk_sum[...].T.astype(LOW)
    dv_ref[...] = dv_sum[...].T.astype(LOW)


def attend_back_call(heads, window, queries, keys, values, grad_out, out, weights, partial, *waits):
    first, pairs = heads
    rows, width = queries.shape[1:]
    length = keys.shape[0]
    per_row = pl.BlockSpec((2, rows, 128), lambda h: (0, 0, h + first))
    per_key = pl.BlockSpec((length, 128), lambda h: (0, h + first))
    per_score = pl.BlockSpec((2, rows, length), lambda h: (h + first, 0, 0))
    begun = [] if partial is None else list(partial)
    return pl.pallas_call(
        attend_back_kernel,
        grid=(pairs,),
        in_specs=[
            pl.BlockSpec(memory_space=pltpu.SMEM),
            per_row,
            per_key,
            per_key,
            per_row,
            per_row,
            pl.BlockSpec((2, 2, rows, length), lambda h: (h + first, 0, 0, 0)),
        ]
        + [pl.BlockSpec(memory_space=pl.ANY)] * len(begun + list(waits)),
        out_specs=[per_row, per_key, per_key, per_score],
        out_shape=[
            jax.ShapeDtypeStruct((2, rows, width), LOW),
            jax.ShapeDtypeStruct((length, width), LOW),
            jax.ShapeDtypeStruct((length, width), LOW),
            jax.ShapeDtypeStruct((width // 64, rows, length), LOW),
        ],
        input_output_aliases={7 + index: index for index in range(len(begun))},
        scratch_shapes=[pltpu.VMEM((128, length), F32)] * 2,
        compiler_params=pltpu.CompilerParams(vmem_limit_bytes=VMEM_LIMIT),
        cost_estimate=pl.CostEstimate(
            flops=32 * rows * length * 128 * pairs,
            bytes_accessed=pairs * rows * length * 16,
            transcendentals=0,
        ),
        name="attend_back",
    )(window, queries, keys, values, grad_out, out, weights, *begun, *waits)


def table_kernel(layers, window_ref, place_ref, *refs):
    sum_refs, (out_ref, total_ref) = refs[:layers], refs[-2:]
    head_count, rows, length = sum_refs[0].shape
    bucket_count = out_ref.shape[0] // 8

    @pl.when(pl.program_id(0) == 0)
    def _():
        total_ref[...] = jnp.zeros_like(total_ref)

    at = pl.program_id(0) * window_ref.shape[1] // pl.num_programs(0)
    first = pl.multiple_of(window_ref[0, at] * 128, 128)
    for count in window_counts(length):

        @pl.when(window_ref[1, at] == count)
        def _(span=count * 128):
            key_place = first + lax.broadcasted_iota(jnp.int32, (8, span), 1)
            chosen, parts = [], []
            for lines in range(0, rows, 16):
                both = sum(ref[:, lines : lines + 16, pl.ds(first, span)].astype(F32) for ref in sum_refs)
                for row in range(0, 16, 8):
                    choice = bucket_of(key_place - place_ref[lines + row : lines + row + 8])
                    masks = [jnp.where(choice == bucket, 1.0, 0.0) for bucket in range(bucket_count)]
                    chosen.append(jnp.concatenate(masks, axis=0).astype(LOW))
                    parts.append(both[:, row : row + 8].reshape(head_count * 8, span).astype(LOW))
            total_ref[...] += dot_nt(jnp.concatenate(chosen, axis=1), jnp.concatenate(parts, axis=1))

    out_ref[...] = total_ref[...]


def table_call(window, score_sums, place, bucket_count, *waits):
    head_count, rows, length = score_sums[0].shape
    tile = min(128, rows)
    layers = len(score_sums)
    grouped = pl.pallas_call(
        functools.partial(table_kernel, layers),
        grid=(rows // tile,),
        in_specs=[
            pl.BlockSpec(memory_space=pltpu.SMEM),
            pl.BlockSpec((tile, 1), lambda i: (i, 0)),
        ]
        + [pl.BlockSpec((head_count, tile, length), lambda i: (0, i, 0))] * layers
        + [pl.BlockSpec(memory_space=pl.ANY)] * len(waits),
        out_specs=pl.BlockSpec((8 * bucket_count, 8 * head_count), lambda i: (0, 0)),
        out_shape=jax.ShapeDtypeStruct((8 * bucket_count, 8 * head_count), F32),
        scratch_shapes=[pltpu.VMEM((8 * bucket_count, 8 * head_count), F32)],
        compiler_params=pltpu.CompilerParams(vmem_limit_bytes=VMEM_LIMIT),
        cost_estimate=pl.CostEstimate(
            flops=512 * rows * length * head_count,
            bytes_accessed=rows * length * head_count * 4,
            transcendentals=0,
        ),
        name="table_sums",
    )(window, place, *score_sums, *waits)
    grouped = grouped.reshape(bucket_count, 8, head_count, 8)
    return jnp.sum(grouped * jnp.eye(8, dtype=F32)[None, :, None, :], axis=(1, 3))


def norm_rows(tensor, scale_row, shift_row):
    center = tensor - jnp.mean(tensor, axis=1, keepdims=True)
    inverse = lax.rsqrt(jnp.mean(center * center, axis=1, keepdims=True) + 1e-05)
    return center * inverse * scale_row + shift_row, inverse


def norm_rows_back(grad, normal, inverse, scale_row):
    scaled = grad * scale_row
    mean_one = jnp.mean(scaled, axis=1, keepdims=True)
    mean_two = jnp.mean(scaled * normal, axis=1, keepdims=True)
    return inverse * (scaled - mean_one - normal * mean_two)


def pieces_of(pieces):
    arrays, plan = [], []
    for pair in pieces:
        spots = []
        for array, first in pair:
            known = [i for i, other in enumerate(arrays) if other is array]
            if not known:
                arrays.append(array)
            spots.append((known[0] if known else len(arrays) - 1, first))
        plan.append(tuple(spots))
    return arrays, tuple(plan)


def layer_tail_kernel(count, plan, span, *refs):
    (stream_ref, out_ref, proj_ref), refs = refs[:3], refs[3:]
    piece_refs, refs = refs[:count], refs[count:]
    gain_ref, shift_ref = refs[:2]
    result_ref, low_ref, middle_ref, middle_low_ref, active_ref, slope_ref, one_ref, two_ref = refs[-8:]
    mixed = stream_ref[...].astype(F32) + dot_nn(out_ref[...], proj_ref[...])
    middle, one_ref[...] = norm_rows(mixed, gain_ref[0:1], shift_ref[0:1])
    middle_ref[...] = middle
    middle_low = middle.astype(LOW)
    middle_low_ref[...] = middle_low
    total = middle
    for index, ((inner_at, inner_first), (outer_at, outer_first)) in enumerate(plan):
        columns = slice(index * span, (index + 1) * span)
        inner = dot_nn(middle_low, piece_refs[inner_at][:, inner_first : inner_first + span])
        cdf = 0.5 + 0.5 * lax.erf(inner * (2.0**-0.5))
        active = (inner * cdf).astype(LOW)
        active_ref[:, columns] = active
        density = jnp.exp(inner * inner * -0.5) * 0.3989422804014327
        slope_ref[:, columns] = (cdf + inner * density).astype(LOW)
        total = total + dot_nt(active, piece_refs[outer_at][:, outer_first : outer_first + span])
    result, two_ref[...] = norm_rows(total, gain_ref[1:2], shift_ref[1:2])
    result_ref[...] = result
    low_ref[...] = result.astype(LOW)


def layer_tail_call(stream, out_low, proj, pieces, span, gains, shifts, part, partial, *waits):
    rows, width = stream.shape
    share = 1 if part is None else 2
    hidden = span * len(pieces)
    pieces, plan = pieces_of(pieces)
    proj, proj_at = proj
    tile = min(256, rows // share)
    first = (part or 0) * (rows // 2 // tile)
    begun = [] if partial is None else list(partial)

    def per_row(columns):
        return pl.BlockSpec((tile, columns), lambda i: (i + first, 0))

    def fixed(shape):
        return pl.BlockSpec(shape, lambda i: (0, 0), pipeline_mode=pl.Buffered(1))

    def whole(columns, kind):
        return jax.ShapeDtypeStruct((rows, columns), kind)

    return pl.pallas_call(
        functools.partial(layer_tail_kernel, len(pieces), plan, span),
        grid=(rows // share // tile,),
        in_specs=[per_row(width), per_row(width), pl.BlockSpec((width, width), lambda i: (0, proj_at), pipeline_mode=pl.Buffered(1))]
        + [fixed(piece.shape) for piece in pieces]
        + [fixed((2, width))] * 2
        + [pl.BlockSpec(memory_space=pl.ANY)] * len(begun + list(waits)),
        out_specs=[
            per_row(width), per_row(width), per_row(width), per_row(width),
            per_row(hidden), per_row(hidden), per_row(1), per_row(1),
        ],
        out_shape=[
            whole(width, F32), whole(width, LOW), whole(width, F32), whole(width, LOW),
            whole(hidden, LOW), whole(hidden, LOW), whole(1, F32), whole(1, F32),
        ],
        input_output_aliases={5 + len(pieces) + index: index for index in range(len(begun))},
        compiler_params=pltpu.CompilerParams(vmem_limit_bytes=VMEM_LIMIT),
        cost_estimate=pl.CostEstimate(
            flops=2 * rows // share * width * (width + 2 * hidden),
            bytes_accessed=4 * rows * hidden + 12 * rows * width + 4 * width * hidden,
            transcendentals=2 * rows * hidden,
        ),
        name="layer_tail",
    )(stream, out_low, proj, *pieces, gains, shifts, *begun, *waits)


def layer_tail_back_kernel(count, plan, span, *refs):
    (grad_ref, result_ref, two_ref, middle_ref, one_ref, slope_ref, proj_ref), refs = refs[:7], refs[7:]
    piece_refs, refs = refs[:count], refs[count:]
    gain_ref, shift_ref, begun_ref = refs[:3]
    two_low_ref, inner_ref, stream_ref, branch_ref, out_ref, terms_ref = refs[-6:]

    @pl.when(pl.program_id(0) == 0)
    def _():
        terms_ref[...] = begun_ref[...]

    grad = grad_ref[...].astype(F32)
    normal = (result_ref[...] - shift_ref[1:2]) / gain_ref[1:2]
    terms_ref[1:2] += jnp.sum(grad * normal, axis=0, keepdims=True)
    terms_ref[3:4] += jnp.sum(grad, axis=0, keepdims=True)
    grad = norm_rows_back(grad, normal, two_ref[...], gain_ref[1:2])
    low = grad.astype(LOW)
    two_low_ref[...] = low
    for index, ((inner_at, inner_first), (outer_at, outer_first)) in enumerate(plan):
        columns = slice(index * span, (index + 1) * span)
        outer_piece = piece_refs[outer_at][:, outer_first : outer_first + span]
        inner = (dot_nn(low, outer_piece) * slope_ref[:, columns].astype(F32)).astype(LOW)
        inner_ref[:, columns] = inner
        grad = grad + dot_nt(inner, piece_refs[inner_at][:, inner_first : inner_first + span])
    normal = (middle_ref[...] - shift_ref[0:1]) / gain_ref[0:1]
    terms_ref[0:1] += jnp.sum(grad * normal, axis=0, keepdims=True)
    terms_ref[2:3] += jnp.sum(grad, axis=0, keepdims=True)
    grad = norm_rows_back(grad, normal, one_ref[...], gain_ref[0:1])
    stream_ref[...] = grad
    low = grad.astype(LOW)
    branch_ref[...] = low
    out_ref[...] = dot_nt(low, proj_ref[...]).astype(LOW)


def layer_tail_back_call(grad, result, two, middle, one, slope, proj, pieces, span, gains, shifts, part, partial, *waits):
    rows, width = result.shape
    share = 1 if part is None else 2
    hidden = span * len(pieces)
    pieces, plan = pieces_of(pieces)
    proj, proj_at = proj
    tile = min(256, rows // share)

    first = (part or 0) * (rows // 2 // tile)
    begun = [] if partial is None else list(partial[:-1])
    terms = jnp.zeros((8, width), F32) if partial is None else partial[-1]

    def per_row(columns):
        return pl.BlockSpec((tile, columns), lambda i: (i + first, 0))

    def fixed(shape):
        return pl.BlockSpec(shape, lambda i: (0, 0), pipeline_mode=pl.Buffered(1))

    def whole(columns, kind):
        return jax.ShapeDtypeStruct((rows, columns), kind)

    return pl.pallas_call(
        functools.partial(layer_tail_back_kernel, len(pieces), plan, span),
        grid=(rows // share // tile,),
        in_specs=[pl.BlockSpec((tile, width), lambda i: (i, 0)), per_row(width), per_row(1), per_row(width), per_row(1), per_row(hidden)]
        + [pl.BlockSpec((width, width), lambda i: (0, proj_at), pipeline_mode=pl.Buffered(1))]
        + [fixed(piece.shape) for piece in pieces]
        + [fixed((2, width))] * 2
        + [fixed((8, width))]
        + [pl.BlockSpec(memory_space=pl.ANY)] * len(begun + list(waits)),
        out_specs=[
            per_row(width), per_row(hidden), per_row(width), per_row(width), per_row(width),
            pl.BlockSpec((8, width), lambda i: (0, 0)),
        ],
        out_shape=[
            whole(width, LOW), whole(hidden, LOW), whole(width, F32), whole(width, LOW), whole(width, LOW),
            jax.ShapeDtypeStruct((8, width), F32),
        ],
        input_output_aliases={10 + len(pieces) + index: index for index in range(len(begun))},
        compiler_params=pltpu.CompilerParams(vmem_limit_bytes=VMEM_LIMIT),
        cost_estimate=pl.CostEstimate(
            flops=2 * rows // share * width * (width + 2 * hidden),
            bytes_accessed=4 * rows * hidden + 20 * rows * width + 4 * width * hidden,
            transcendentals=0,
        ),
        name="layer_tail_back",
    )(grad, result, two, middle, one, slope, proj, *pieces, gains, shifts, terms, *begun, *waits)


def product_kernel(plan, side_ref, *refs):
    step = pl.program_id(0)
    for index, (lhs, rhs, out, plus) in enumerate(plan):

        @pl.when(step == index)
        def _(lhs=lhs, rhs=rhs, out=out, plus=plus):
            total = dot_tn(refs[lhs][...], refs[rhs][...])
            if plus is not None:
                total = total + refs[plus][...].astype(F32)
            refs[out][...] = total.astype(refs[out].dtype)


def products_call(name, side, steps, outs, waits=()):
    arrays, specs, plan, place = [], [], [], {}
    total = len(steps)

    def column_of(kind, side_ref):
        if kind == "side":
            return side_ref[0]
        if kind == "other":
            return 1 - side_ref[0]
        return kind

    def chain(at):
        table = []
        for step in range(total):
            later = [at[u] for u in sorted(at) if u >= step]
            table.append(later[0] if later else at[max(at)])
        def index(i, side_ref):
            value = column_of(table[-1], side_ref)
            for step in reversed(range(total - 1)):
                if table[step] != table[step + 1]:
                    value = jnp.where(i <= step, column_of(table[step], side_ref), value)
            return (0, value)
        return index

    uses = {}
    for step, (lhs, rhs, span, block, out, out_block, plus) in enumerate(steps):
        uses.setdefault(("in", id(lhs), lhs.shape[1]), [lhs, {}])[1][step] = 0
        uses.setdefault(("in", id(rhs), span), [rhs, {}])[1][step] = block
        if plus is not None:
            uses.setdefault(("in", id(plus), outs[out][2]), [plus, {}])[1][step] = out_block
    for key, (array, at) in uses.items():
        place[key] = len(arrays)
        arrays.append(array)
        specs.append(pl.BlockSpec((array.shape[0], key[2]), chain(at)))
    first_out = len(arrays) + len(waits)
    out_names = list(outs)
    out_specs = []
    for out in out_names:
        at = {step: entry[5] for step, entry in enumerate(steps) if entry[4] == out}
        out_specs.append(pl.BlockSpec((outs[out][0], outs[out][2]), chain(at)))
    flops = 0
    for lhs, rhs, span, block, out, out_block, plus in steps:
        flops += 2 * lhs.shape[0] * lhs.shape[1] * span
        plan.append(
            (
                place[("in", id(lhs), lhs.shape[1])],
                place[("in", id(rhs), span)],
                first_out + out_names.index(out),
                None if plus is None else place[("in", id(plus), outs[out][2])],
            )
        )
    results = pl.pallas_call(
        functools.partial(product_kernel, plan),
        grid_spec=pltpu.PrefetchScalarGridSpec(
            num_scalar_prefetch=1,
            grid=(total,),
            in_specs=specs + [pl.BlockSpec(memory_space=pl.ANY)] * len(waits),
            out_specs=out_specs,
        ),
        out_shape=[jax.ShapeDtypeStruct(outs[out][:2], LOW) for out in out_names],
        compiler_params=pltpu.CompilerParams(vmem_limit_bytes=VMEM_LIMIT),
        cost_estimate=pl.CostEstimate(flops=flops, bytes_accessed=flops // 300, transcendentals=0),
        name=name,
    )(side, *arrays, *waits)
    return dict(zip(out_names, results))


def hold_kernel(*refs):
    del refs


def hold(tensor, *waits):
    anywhere = pl.BlockSpec(memory_space=pl.ANY)
    return pl.pallas_call(
        hold_kernel,
        in_specs=[anywhere] * (1 + len(waits)),
        out_specs=anywhere,
        out_shape=jax.ShapeDtypeStruct(tensor.shape, tensor.dtype),
        input_output_aliases={0: 0},
        cost_estimate=pl.CostEstimate(flops=0, bytes_accessed=0, transcendentals=0),
        name="hold",
    )(tensor, *waits)


def place_kernel(count, place_ref, *refs):
    out_ref = refs[-1]
    for index in range(count):
        out_ref[place_ref[index]] = refs[index][...]


def place_call(name, parts, spots, waits):
    shape = (len(parts), *parts[0].shape)
    return pl.pallas_call(
        functools.partial(place_kernel, len(parts)),
        in_specs=[pl.BlockSpec(memory_space=pltpu.SMEM)]
        + [pl.BlockSpec(memory_space=pltpu.VMEM)] * len(parts)
        + [pl.BlockSpec(memory_space=pl.ANY)] * len(waits),
        out_specs=pl.BlockSpec(memory_space=pltpu.VMEM),
        out_shape=jax.ShapeDtypeStruct(shape, parts[0].dtype),
        compiler_params=pltpu.CompilerParams(vmem_limit_bytes=VMEM_LIMIT),
        cost_estimate=pl.CostEstimate(flops=0, bytes_accessed=4 * parts[0].size * len(parts), transcendentals=0),
        name=name,
    )(jnp.stack(spots).astype(jnp.int32), *parts, *waits)


def weave_kernel(count, place_ref, *refs):
    out_ref = refs[-1]
    for index in range(count):
        for row in range(refs[index].shape[0]):
            out_ref[row, place_ref[index]] = refs[index][row]


def weave_call(name, parts, spots, waits):
    lead, *rest = parts[0].shape
    return pl.pallas_call(
        functools.partial(weave_kernel, len(parts)),
        in_specs=[pl.BlockSpec(memory_space=pltpu.SMEM)]
        + [pl.BlockSpec(memory_space=pltpu.VMEM)] * len(parts)
        + [pl.BlockSpec(memory_space=pl.ANY)] * len(waits),
        out_specs=pl.BlockSpec(memory_space=pltpu.VMEM),
        out_shape=jax.ShapeDtypeStruct((lead, len(parts), *rest), parts[0].dtype),
        compiler_params=pltpu.CompilerParams(vmem_limit_bytes=VMEM_LIMIT),
        cost_estimate=pl.CostEstimate(flops=0, bytes_accessed=4 * parts[0].size * len(parts), transcendentals=0),
        name=name,
    )(jnp.stack(spots).astype(jnp.int32), *parts, *waits)


class Grid:
    def __init__(self, mesh):
        self.blocks = mesh.shape["blk"]
        self.total = mesh.shape["dp"]
        self.paired = self.blocks == 2 and self.total == 16
        self.high = 4
        self.low = self.total // 8

    def place(self):
        index = lax.axis_index("dp")
        self.core_at = index % 2
        self.low_at = index // 2 % self.low
        self.high_at = index // (2 * self.low)
        self.block_at = lax.axis_index("blk")

    def from_core(self, tensor):
        return lax.ppermute(tensor, "dp", [(i, i ^ 1) for i in range(self.total)])

    def from_block(self, tensor):
        return lax.ppermute(tensor, "blk", [(0, 1), (1, 0)])

    def from_low(self, tensor, step):
        span = 2 * self.low
        pairs = [(i, i // span * span + (i + 2 * step) % span) for i in range(self.total)]
        return lax.ppermute(tensor, "dp", pairs)

    def from_high(self, tensor, step):
        return lax.ppermute(tensor, "dp", [(i, (i + 2 * self.low * step) % self.total) for i in range(self.total)])

    def gather(self, shard):
        return lax.all_gather(shard, "dp", axis=0, tiled=True)

    def gather_chip(self, shards, waits):
        rows, columns = shards[0].shape
        width = columns // 4

        def quarter(core):
            first = (2 * self.block_at + core) * width
            parts = [lax.dynamic_slice_in_dim(shard, first, width, 1) for shard in shards]
            return jnp.concatenate(parts, axis=1) if len(parts) > 1 else parts[0]

        mine = quarter(self.core_at)
        other = self.from_core(quarter(1 - self.core_at))
        chip = place_call("chip_rows", [mine, other], [self.core_at, 1 - self.core_at], waits)
        return chip.reshape(2 * rows, -1)

    def gather_line(self, chip, waits):
        parts = [chip] + [self.from_high(chip, step) for step in range(1, self.high)]
        spots = [(self.high_at - step) % self.high for step in range(self.high)]
        return place_call("line_rows", parts, spots, waits)

    def gather_sheet(self, line, waits):
        parts = [line] + [self.from_low(line, step) for step in range(1, self.low)]
        spots = [(self.low_at - step) % self.low for step in range(self.low)]
        return weave_call("sheet_rows", parts, spots, waits).reshape(-1, line.shape[2])

    def scatter_begin(self, tensor, axis):
        size, index, send = (
            (self.low, self.low_at, self.from_low) if axis == 1 else (self.high, self.high_at, self.from_high)
        )

        def at(step):
            return lax.dynamic_index_in_dim(tensor, (index + step) % size, axis, False)

        return at(0), [send(at(step), step) for step in range(1, size)]

    def low_begin(self, tensor):
        rows, columns = tensor.shape
        return self.scatter_begin(tensor.reshape(self.high, self.low, -1, columns), 1)

    def high_begin(self, tensor):
        return self.scatter_begin(tensor, 0)

    def scatter_end(self, begun, *waits):
        own, arrived = begun
        if waits:
            arrived = [hold(arrived[0], *waits), *arrived[1:]]
        return sum((tensor.astype(F32) for tensor in arrived), own.astype(F32)).astype(LOW)

    def sum_blocks(self, tensor):
        return (tensor.astype(F32) + self.from_block(tensor).astype(F32)).astype(LOW)

    def halves(self, tensor):
        rows = tensor.shape[0] // 2
        own = lax.dynamic_slice_in_dim(tensor, self.core_at * rows, rows, 0)
        other = self.from_core(lax.dynamic_slice_in_dim(tensor, (1 - self.core_at) * rows, rows, 0))
        first = self.core_at == 0
        return jnp.where(first, own, other), jnp.where(first, other, own)

    def sum_all(self, tensor):
        if not self.paired or self.total & (self.total - 1):
            return lax.psum(tensor, ("blk", "dp"))
        tensor = tensor + self.from_block(tensor)
        bit = 1
        while bit < self.total:
            tensor = tensor + lax.ppermute(tensor, "dp", [(i, i ^ bit) for i in range(self.total)])
            bit *= 2
        return tensor

    def scatter(self, tensor):
        return self.scatter_end_blocks(self.scatter_rows(tensor))

    def scatter_rows(self, tensor):
        return lax.psum_scatter(tensor, "dp", scatter_dimension=0, tiled=True)

    def scatter_end_blocks(self, part):
        if self.blocks == 2:
            return part.astype(F32) + self.from_block(part).astype(F32)
        return lax.psum(part, "blk").astype(F32)


def shards(
    grid,
    content_in,
    query_in,
    cot_content,
    cot_query,
    attn_weights,
    out_weight,
    ffn_in,
    ffn_out_t,
    norm_gains,
    norm_shifts,
    bias_table,
    permutation,
    predicted,
    doc_lengths,
):
    _, rows, width = content_in.shape
    length = permutation.shape[1]
    blocks = length // rows
    bucket_count, head_count = bias_table.shape
    layer_count = attn_weights.shape[0]
    grid.place()
    block_index = grid.block_at

    paired = grid.paired
    layers = range(layer_count)

    def chip_of(layer_index, *waits):
        return grid.gather_chip((ffn_in[layer_index], ffn_out_t[layer_index]), waits)

    chip = chip_of(0) if paired else None
    sides = jnp.stack([block_index, 1 - block_index]) if paired else (block_index + jnp.arange(blocks)) % blocks
    (
        window, key_doc, key_rank, place_column, place_doc, place_rank, own_column, sorter, stream_low, grad_low,
        *spreads,
    ) = setup_call(
        sides.astype(jnp.int32), doc_lengths, permutation, predicted,
        (content_in[0], query_in[0], cot_content[0], cot_query[0]), *((chip,) if paired else ()),
    )
    stream = stream_low
    table_rows = jnp.concatenate(
        [bias_table.T, jnp.full((head_count, 128 - bucket_count), MASKED, F32)], axis=1
    )

    def other_blocks(tensor, come):
        if paired:
            come = grid.from_block(tensor) if come is None else come
            return (dot_tn(spreads[0], tensor) + dot_tn(spreads[1], come)).astype(LOW)
        gathered = lax.all_gather(tensor, "blk", axis=0, tiled=False)
        parts = [
            dot_tn(spread, lax.dynamic_index_in_dim(gathered, (block_index + step) % blocks, 0, False))
            for step, spread in enumerate(spreads)
        ]
        return sum(parts).astype(LOW)

    hidden = ffn_in.shape[2]
    span = hidden // 4 if paired else hidden
    bias = bias_call(
        window, table_rows, place_column, place_doc, place_rank, key_doc, key_rank, *((chip,) if paired else ())
    )
    first_qkv = attn_weights[0]
    if paired:
        line = grid.gather_line(chip, (bias,))
        if layer_count > 1:
            next_chip = chip_of(1, line)
        sheet = grid.gather_sheet(line, ())
    first_qkv = grid.gather(first_qkv)
    if paired:
        first_qkv = hold(first_qkv, sheet)
    others = grid.gather(
        jnp.concatenate([out_weight[i] for i in layers] + [attn_weights[i] for i in layers[1:]], axis=1)
    )
    starts = [(layer_count + 3 * index) * width for index in range(layer_count - 1)]
    qkv_full = [first_qkv] + [others[:, start : start + 3 * width] for start in starts]
    kept = []
    next_content = None
    all_pieces = []
    for layer_index in range(layer_count):
        qkv = qkv_full[layer_index]
        all_content = other_blocks(stream_low[:rows], next_content)
        queries = dot_nn(stream_low, qkv[:, :width]).astype(LOW).reshape(2, rows, width)
        keys = dot_nn(all_content, qkv[:, width : 2 * width]).astype(LOW)
        values = dot_nn(all_content, qkv[:, 2 * width :]).astype(LOW)
        later = ()
        more = paired and layer_index + 1 < layer_count
        if paired:
            if layer_index > 0:
                sheet = grid.gather_sheet(line, (stream_low, queries))
            later = (sheet,)
        if more:
            later = (sheet, next_chip)
        out, out_low, weights = attend_call(window, queries, keys, values, bias, own_column, *later)
        later = ()
        if paired:
            waits_near = (out_low,)
            if more:
                line = grid.gather_line(next_chip, (out_low,))
                waits_near = (out_low, line)
            near = hold(grid.from_block(sheet), *waits_near)
            quarters = (sheet, grid.from_core(sheet), near, grid.from_core(near))
            pieces = [((quarter, 0), (quarter, span)) for quarter in quarters]
        else:
            pieces = [((grid.gather(ffn_in[layer_index]), 0), (grid.gather(ffn_out_t[layer_index]), 0))]
        all_pieces.append(pieces)
        if more:
            later = (line,)
            if layer_index + 2 < layer_count:
                next_chip = chip_of(layer_index + 2, line)
        out_low = out_low.reshape(2 * rows, width)
        partial = None
        for part in (0, 1) if more else (None,):
            partial = layer_tail_call(
                stream, out_low, (others, layer_index), pieces, span,
                norm_gains[layer_index], norm_shifts[layer_index], part, partial, *later,
            )
            if part == 0:
                next_content = grid.from_block(partial[1][:rows])
        result, low, middle, middle_low, active, slope, inverse_one, inverse_two = partial
        kept.append(
            (
                stream_low, all_content, queries, keys, values, out, out_low, weights,
                result, middle, middle_low, active, slope, inverse_one, inverse_two,
            )
        )
        stream, stream_low = result, low

    def unsort(tensor):
        return dot_tn(sorter, tensor)

    def unsort_wide(tensor):
        high = tensor.astype(LOW)
        rest = (tensor - high.astype(F32)).astype(LOW)
        return unsort(high) + unsort(rest)

    content_out = unsort(stream_low[:rows]).astype(LOW)
    query_out = unsort(stream_low[rows:]).astype(LOW)

    grad_stream = None
    norm_terms = [None] * layer_count
    matrix_rows = [None] * layer_count
    attn_rows = [None] * layer_count
    attn_parts = [None] * layer_count
    side = jnp.full((1,), grid.core_at, jnp.int32)
    pairs = width // 128
    score_sums = []
    pending = {}
    third = width // 2

    def content_side(own, come):
        own, grad_all = own
        if grad_all is not None:
            own = own + dot_nn(spreads[0], grad_all)
        return own + come.astype(F32)

    def keys_back(grad_k, grad_v, qkv):
        return (dot_nt(grad_k, qkv[:, width : 2 * width]) + dot_nt(grad_v, qkv[:, 2 * width :])).astype(LOW)

    def finish_rows(high):
        shared = grid.sum_blocks(high[:, 2 * span :])
        sides = grid.halves(jnp.concatenate([high[:, : 2 * span], shared], axis=1))
        proj_grad = jnp.concatenate([one[:, 2 * span :] for one in sides], axis=1)
        half = jnp.concatenate([one[:, : 2 * span] for one in sides], axis=1)
        other = grid.from_block(half)
        first = grid.block_at == 0
        quarters = (jnp.where(first, half, other), jnp.where(first, other, half))
        inner_grad, outer_grad = (
            jnp.concatenate(
                [
                    one[:, (2 * core + which) * span : (2 * core + which + 1) * span]
                    for one in quarters
                    for core in range(2)
                ],
                axis=1,
            )
            for which in range(2)
        )
        return tuple(tensor.astype(F32) for tensor in (proj_grad, inner_grad, outer_grad))

    def waits(*names):
        return [pending[name] for name in names if name in pending]

    come = None
    for layer_index in reversed(range(layer_count)):
        (
            stream_low, all_content, queries, keys, values, out, out_low, weights,
            result, middle, middle_low, active, slope, inverse_one, inverse_two,
        ) = kept[layer_index]
        qkv = qkv_full[layer_index]
        partial = None
        for part in (None,) if layer_index == layer_count - 1 else (1, 0):
            if part is None:
                grad = grad_low
            elif part == 1:
                grad = grad_stream[1]
            else:
                grad = content_side(grad_stream[0], hold(come, partial[0]) if paired else come)
            partial = layer_tail_back_call(
                grad, result, inverse_two, middle, inverse_one, slope, (others, layer_index),
                all_pieces[layer_index], span, norm_gains[layer_index], norm_shifts[layer_index],
                part, partial, *waits("attn"),
            )
        two_low, inner_low, grad_one, branch_low, grad_out, norm_terms[layer_index] = partial
        grad_out = grad_out.reshape(2, rows, width)
        back = (window, queries, keys, values, grad_out, out, weights)
        if paired:
            def steps(name, quarter, come=None):
                return [
                    (middle_low, inner_low, span, quarter, name, 0, come),
                    (two_low, active, span, quarter, name, 1, come),
                ]

            sent = products_call(
                "products_sent", side,
                steps("far", 3) + steps("beside", 1) + [(out_low, branch_low, third, "other", "proj", 0, None)],
                {"far": (width, 2 * span, span), "beside": (width, 2 * span, span), "proj": (width, third, third)},
                (),
            )
            come = {name: grid.from_core(tensor) for name, tensor in sent.items()}
            near = products_call(
                "products_near", side, steps("near", 2, come["far"]), {"near": (width, 2 * span, span)}
            )["near"]
            arrived = grid.from_block(near)
            held = products_call(
                "products_held", side,
                steps("mine", 0, come["beside"]) + [(out_low, branch_low, third, "side", "proj", 0, come["proj"])],
                {"mine": (width, 2 * span, span), "proj": (width, third, third)},
                [near],
            )
            partial = attend_back_call((0, pairs // 2), *back, None, *held.values())
            if "low_begun" in pending:
                pending["low"] = grid.scatter_end(pending["low_begun"], partial[0])
                pending["high_begun"] = grid.high_begin(pending["low"])
            grad_q, grad_k, grad_v, score_sum = attend_back_call(
                (pairs // 2, pairs - pairs // 2), *back, partial, *waits("low")
            )
            score_sums.append(score_sum)
            grad_q = grad_q.reshape(2 * rows, width)
            ffn_sum = (held["mine"].astype(F32) + arrived.astype(F32)).astype(LOW)
            ffn_sum = jnp.concatenate([ffn_sum, held["proj"]], axis=1)
            if layer_index == 0:
                ffn_begun = grid.low_begin(ffn_sum)
            if layer_index > 0:
                grad_all = keys_back(grad_k, grad_v, qkv)
                passed = dot_nn(spreads[1], grad_all).astype(LOW)
            attn = products_call(
                "products_attn", side,
                [
                    (lhs, rhs, width, 0, "attn", index, None)
                    for index, (lhs, rhs) in enumerate(
                        ((stream_low, grad_q), (all_content, grad_k), (all_content, grad_v))
                    )
                ],
                {"attn": (width, 3 * width, width)},
                [passed, ffn_sum] if layer_index > 0 else [ffn_sum],
            )["attn"]
            if layer_index == 0:
                grad_q, grad_k, grad_v = (hold(tensor, attn) for tensor in (grad_q, grad_k, grad_v))
                grad_all = keys_back(grad_k, grad_v, qkv)
                ffn_low = grid.scatter_end(ffn_begun, grad_all)
                ffn_begun = grid.high_begin(ffn_low)
                passed = dot_nn(spreads[1], grad_all).astype(LOW)
            attn_part = grid.scatter_rows(attn)
            attn_parts[layer_index] = attn_part
            if "high_begun" in pending:
                upper = pending["high_begun"]
            if layer_index > 0:
                pending = {"attn": attn, "sum": ffn_sum, "low_begun": grid.low_begin(ffn_sum)}
            else:
                pending = {"passed": passed, "ffn_low": ffn_low}
        else:
            grad_q, grad_k, grad_v, score_sum = attend_back_call((0, pairs), *back, None)
            score_sums.append(score_sum)
            grad_q = grad_q.reshape(2 * rows, width)
            terms = [
                jnp.concatenate(
                    [dot_tn(stream_low, grad_q), dot_tn(all_content, grad_k), dot_tn(all_content, grad_v)], axis=1
                ),
                dot_tn(out_low, branch_low),
                dot_tn(middle_low, inner_low),
                dot_tn(two_low, active),
            ]
            attn_rows[layer_index], *matrix_rows[layer_index] = (grid.scatter(term.astype(LOW)) for term in terms)
        query_side = grad_one + dot_nt(grad_q, qkv[:, :width])
        grad_stream = [(query_side[:rows], grad_all if paired else None), query_side[rows:]]
        if layer_index == 0:
            rest = grad_stream[1]
            if paired:
                rest = hold(rest, ffn_low)
            query_grad = unsort_wide(rest)
            table_grad = table_call(
                window, score_sums, place_column, bucket_count, *([passed, ffn_low, query_grad] if paired else [])
            )
        if paired:
            come = grid.from_block(passed)
        else:
            grad_all = keys_back(grad_k, grad_v, qkv)
            grad_split = jnp.stack([dot_nn(spread, grad_all).astype(LOW) for spread in spreads])
            grad_split = jnp.roll(grad_split, block_index, axis=0)
            come = lax.psum_scatter(grad_split, "blk", scatter_dimension=0, tiled=False)
    if paired:
        come = hold(come, table_grad)
        ffn_high = grid.scatter_end(ffn_begun, table_grad)
        if layer_count > 1:
            matrix_rows[1] = finish_rows(grid.scatter_end(upper, table_grad))
        matrix_rows[0] = finish_rows(hold(ffn_high, attn_part))
        attn_rows = [grid.scatter_end_blocks(hold(part, table_grad)) for part in attn_parts]
    grad_stream[0] = content_side(grad_stream[0], come)
    table_lines = jnp.pad(table_grad.T, ((0, 0), (0, width - bucket_count)))
    sums = grid.sum_all(jnp.concatenate([*[terms[:4] for terms in norm_terms], table_lines], axis=0))
    norm_sum = sums[: 4 * layer_count].reshape(layer_count, 2, 2, width)
    table_total = sums[4 * layer_count :, :bucket_count].T
    matrix_grads = tuple(jnp.stack(rows_of, axis=0) for rows_of in (attn_rows, *zip(*matrix_rows)))
    return (
        content_out[None],
        query_out[None],
        unsort_wide(grad_stream[0])[None],
        query_grad[None],
        *matrix_grads,
        norm_sum[:, 0],
        norm_sum[:, 1],
        table_total,
    )


def solution(mesh):
    tokens = P("dp", "blk", None)
    matrix = P(None, "dp", None)
    whole = P()
    sequence = P("dp", None)
    return jax.shard_map(
        functools.partial(shards, Grid(mesh)),
        mesh=mesh,
        in_specs=(tokens,) * 4 + (matrix,) * 4 + (whole,) * 3 + (sequence,) * 3,
        out_specs=(tokens,) * 4 + (matrix,) * 4 + (whole,) * 3,
        check_vma=False,
    )
```

```python
import functools

import jax
import jax.numpy as jnp
from jax import lax
from jax.experimental import pallas as pl
from jax.experimental.pallas import tpu as pltpu
from jax.sharding import PartitionSpec as P

THRESHOLDS = (12, 16, 23, 32, 46, 64, 91)
MASKED = -1e30
F32 = jnp.float32
LOW = jnp.bfloat16
VMEM_LIMIT = 56 * 2**20
ROW_TILE = 128
PAIRS = 2


def dot_nn(left_side, right_side):
    return jnp.dot(left_side, right_side, preferred_element_type=F32)


def dot_nt(left_side, right_side):
    return lax.dot_general(left_side, right_side, (((1,), (1,)), ((), ())), preferred_element_type=F32)


def dot_tn(left_side, right_side):
    return lax.dot_general(left_side, right_side, (((0,), (0,)), ((), ())), preferred_element_type=F32)


def bucket_of(relative):
    distance = jnp.abs(relative)
    far_bucket = 8 + sum(((distance >= threshold).astype(jnp.int32) for threshold in THRESHOLDS))
    near_bucket = jnp.where(distance < 8, distance, jnp.minimum(far_bucket, 15))
    return jnp.where(relative > 0, 16, 0).astype(jnp.int32) + near_bucket


def window_counts(length):
    most = length // 128
    return [count for count in (2, 3, 4, 5, 6) if count < most] + [most]


def by_window(window_ref, tile, length, step):
    def one(at, carry):
        row = pl.multiple_of(at * tile, tile)
        first = pl.multiple_of(window_ref[0, at] * 128, 128)
        for count in window_counts(length):

            @pl.when(window_ref[1, at] == count)
            def _(count=count):
                step(pl.ds(row, tile), pl.ds(first, count * 128), count * 128, first)

        return carry

    lax.fori_loop(0, window_ref.shape[1], one, 0)


def setup_kernel(side_ref, lengths_ref, row_ref, column_ref, chosen_ref, *refs):
    streams, refs = refs[:4], refs[4:]
    outs = refs[-(11 + side_ref.shape[0]) :]
    window_ref, key_doc_ref, key_rank_ref, place_ref, doc_ref, rank_ref, own_ref, sorter_ref, low_ref, grad_ref = outs[:10]
    spread_refs = outs[10:-1]
    rank_row = outs[-1]
    length, rows = row_ref.shape[1], streams[0].shape[0]
    for first in range(0, length, 128):
        position = (first + lax.broadcasted_iota(jnp.int32, (length, 128), 1))
        rank = lax.broadcasted_iota(jnp.int32, (length, 128), 0).astype(F32)
        rank_row[:, first : first + 128] = jnp.sum(
            jnp.where(column_ref[...] == position, rank, 0.0), axis=0, keepdims=True
        )
    ranks = rank_row[...]
    position = lax.broadcasted_iota(jnp.int32, (1, length), 1)
    doc = jnp.zeros((1, length), jnp.int32)
    start = position == 0
    bound = 0
    for index in range(lengths_ref.shape[1] - 1):
        bound = bound + lengths_ref[0, index]
        doc = doc + (position >= bound).astype(jnp.int32)
        start = start | (position == bound)
    live = (chosen_ref[...] == 1) & jnp.logical_not(start)
    key_doc_ref[...] = doc
    key_rank_ref[...] = jnp.where(live, ranks, -1.0).astype(jnp.int32)
    below = (
        lax.broadcasted_iota(jnp.int32, (length, length), 0) <= lax.broadcasted_iota(jnp.int32, (length, length), 1)
    )
    below = jnp.where(below, 1.0, 0.0).astype(LOW)
    slot = lax.broadcasted_iota(jnp.int32, (rows, length), 0).astype(F32)
    for index, spread_ref in enumerate(spread_refs):
        least = (side_ref[index] * rows).astype(F32)
        owned = (ranks >= least) & (ranks < least + rows)
        counted = jnp.broadcast_to(jnp.where(owned, 1.0, 0.0), (8, length)).astype(LOW)
        order = jnp.where(owned, dot_nn(counted, below)[0:1] - 1.0, -1.0)
        chosen = slot == order
        spread_ref[...] = jnp.where(chosen, 1.0, 0.0).astype(LOW)
        if index == 0:

            def pick(row):
                return jnp.sum(jnp.where(chosen, row, 0.0), axis=1, keepdims=True)

            place = pick(position.astype(F32))
            rank = pick(ranks)
            place_ref[...] = place.astype(jnp.int32)
            rank_ref[...] = rank.astype(jnp.int32)
            doc_ref[...] = pick(doc.astype(F32)).astype(jnp.int32)
            own_ref[...] = jnp.where(pick(jnp.where(live, 1.0, 0.0)) > 0.0, place, -1.0).astype(jnp.int32)
            tile = rows // window_ref.shape[1]
            for at in range(window_ref.shape[1]):
                lines = place[at * tile : (at + 1) * tile]
                least_place = jnp.min(lines).astype(jnp.int32)
                most_place = jnp.max(lines).astype(jnp.int32)
                first, last, bound = 0, length, 0
                for doc_index in range(lengths_ref.shape[1] - 1):
                    bound = bound + lengths_ref[0, doc_index]
                    first = jnp.where(least_place >= bound, bound, first)
                    last = jnp.where((most_place < bound) & (last == length), bound, last)
                first = first // 128
                needed = (last + 127) // 128 - first
                count = length // 128
                for choice in reversed(window_counts(length)):
                    count = jnp.where(needed <= choice, choice, count)
                window_ref[0, at] = jnp.minimum(first, length // 128 - count)
                window_ref[1, at] = count
            spot = lax.broadcasted_iota(jnp.int32, (rows, rows), 1).astype(F32)
            sorter = jnp.where(spot == rank - least, 1.0, 0.0).astype(LOW)
            sorter_ref[...] = sorter
    for index, stream in enumerate(streams):
        target = (low_ref, grad_ref)[index // 2]
        target[index % 2 * rows : (index % 2 + 1) * rows] = dot_nn(sorter, stream[...]).astype(LOW)


def setup_call(sides, lengths, anchor, chosen, streams, *waits):
    length = anchor.shape[1]
    rows, width = streams[0].shape
    count = sides.shape[0]
    here = pl.BlockSpec(memory_space=pltpu.VMEM)
    scalars = pl.BlockSpec(memory_space=pltpu.SMEM)

    def whole(lines, columns, kind):
        return jax.ShapeDtypeStruct((lines, columns), kind)

    return pl.pallas_call(
        setup_kernel,
        in_specs=[scalars, scalars, here, here, here] + [here] * 4 + [pl.BlockSpec(memory_space=pl.ANY)] * len(waits),
        out_specs=[scalars] + [here] * (9 + count),
        out_shape=[whole(2, rows // min(ROW_TILE, rows), jnp.int32)]
        + [whole(1, length, jnp.int32)] * 2
        + [whole(rows, 1, jnp.int32)] * 4
        + [whole(rows, rows, LOW), whole(2 * rows, width, LOW), whole(2 * rows, width, LOW)]
        + [whole(rows, length, LOW)] * count,
        scratch_shapes=[pltpu.VMEM((1, length), F32)],
        compiler_params=pltpu.CompilerParams(vmem_limit_bytes=VMEM_LIMIT),
        cost_estimate=pl.CostEstimate(flops=8 * rows * rows * width, bytes_accessed=16 * rows * width, transcendentals=0),
        name="setup_rows",
    )(sides, lengths, anchor, anchor.reshape(length, 1), chosen, *streams, *waits)


def bias_kernel(window_ref, table_ref, place_ref, doc_ref, rank_ref, key_doc_ref, key_rank_ref, *refs):
    out_ref = refs[-1]
    head_count, rows, length = out_ref.shape
    place = place_ref[...]
    doc = doc_ref[...]
    rank = rank_ref[...]
    at = pl.program_id(0) * window_ref.shape[1] // pl.num_programs(0)
    for block in range(length // 128):
        first = block * 128

        @pl.when((block >= window_ref[0, at]) & (block < window_ref[0, at] + window_ref[1, at]))
        def _(first=first):
            key_place = first + lax.broadcasted_iota(jnp.int32, (rows, 128), 1)
            seen = (key_doc_ref[:, first : first + 128] == doc) & (
                key_rank_ref[:, first : first + 128] <= rank
            )
            choice = jnp.where(seen, bucket_of(key_place - place), 32)
            for head in range(head_count):
                line = jnp.broadcast_to(table_ref[head : head + 1, :], (8, 128))
                for row in range(0, rows, 16):
                    taken = [jnp.take_along_axis(line, choice[at : at + 8], axis=1) for at in (row, row + 8)]
                    out_ref[head, row : row + 16, first : first + 128] = jnp.concatenate(taken, axis=0).astype(LOW)


def bias_call(window, table_rows, place, doc, rank, key_doc, key_rank, *waits):
    head_count = table_rows.shape[0]
    rows, length = place.shape[0], key_doc.shape[1]
    tile = min(64, rows)
    column = pl.BlockSpec((tile, 1), lambda i: (i, 0))
    line = pl.BlockSpec((1, length), lambda i: (0, 0))
    return pl.pallas_call(
        bias_kernel,
        grid=(rows // tile,),
        in_specs=[
            pl.BlockSpec(memory_space=pltpu.SMEM),
            pl.BlockSpec((head_count, 128), lambda i: (0, 0)),
            column,
            column,
            column,
            line,
            line,
        ]
        + [pl.BlockSpec(memory_space=pl.ANY)] * len(waits),
        out_specs=pl.BlockSpec((head_count, tile, length), lambda i: (0, i, 0)),
        out_shape=jax.ShapeDtypeStruct((head_count, rows, length), LOW),
        compiler_params=pltpu.CompilerParams(vmem_limit_bytes=VMEM_LIMIT),
        cost_estimate=pl.CostEstimate(
            flops=0, bytes_accessed=head_count * rows * length * 8, transcendentals=0
        ),
        name="bias_rows",
    )(window, table_rows, place, doc, rank, key_doc, key_rank, *waits)


def attend_kernel(window_ref, q_ref, k_ref, v_ref, bias_ref, own_ref, *refs):
    o_ref, low_ref, p_ref = refs[-3:]
    length = bias_ref.shape[2]
    tile = bias_ref.shape[1] // window_ref.shape[1]
    heads = range(bias_ref.shape[0])

    def step(lines, columns, span, first):
        first_half = lax.broadcasted_iota(jnp.int32, (2 * tile, 128), 1) < 64
        zero = jnp.zeros((2 * tile, 128), LOW)
        hidden = lax.broadcasted_iota(jnp.int32, (tile, span), 1) == own_ref[lines, :] - first
        mine = []
        for head in heads:
            lanes = slice(head // 2 * 128, head // 2 * 128 + 128)
            queries = q_ref[:, lines, lanes].reshape(2 * tile, 128) * jnp.array(0.125, LOW)
            mine.append(jnp.where(first_half, queries, zero) if head % 2 == 0 else jnp.where(first_half, zero, queries))
        raw = [dot_nt(mine[head], k_ref[columns, head // 2 * 128 : head // 2 * 128 + 128]) for head in heads]
        scores = []
        for head in heads:
            bias = bias_ref[head, lines, columns].astype(F32)
            scores.append((raw[head][:tile] + bias, jnp.where(hidden, MASKED, raw[head][tile:] + bias)))
        most = [[jnp.max(part, axis=1, keepdims=True) for part in pair] for pair in scores]
        weights = [[jnp.exp(part - top) for part, top in zip(pair, tops)] for pair, tops in zip(scores, most)]
        shares = [[1.0 / jnp.sum(part, axis=1, keepdims=True) for part in pair] for pair in weights]
        lows = [[(part * share).astype(LOW) for part, share in zip(pair, both)] for pair, both in zip(weights, shares)]
        parts = []
        for head in heads:
            for stream in range(2):
                p_ref[head, stream, lines, columns] = lows[head][stream]
            values = v_ref[columns, head // 2 * 128 : head // 2 * 128 + 128]
            parts.append(dot_nn(jnp.concatenate(lows[head], axis=0), values))
        for pair in range(len(heads) // 2):
            lanes = slice(pair * 128, pair * 128 + 128)
            out = jnp.where(first_half, parts[2 * pair], parts[2 * pair + 1])
            o_ref[:, lines, lanes] = out.reshape(2, tile, 128)
            low_ref[:, lines, lanes] = out.astype(LOW).reshape(2, tile, 128)

    by_window(window_ref, tile, length, step)


def attend_call(window, queries, keys, values, bias, own, *waits):
    _, rows, width = queries.shape
    length = keys.shape[0]
    pairs = width // 128
    group = PAIRS
    per_row = pl.BlockSpec((2, rows, 128 * group), lambda h: (0, 0, h))
    per_key = pl.BlockSpec((length, 128 * group), lambda h: (0, h))
    return pl.pallas_call(
        attend_kernel,
        grid=(pairs // group,),
        in_specs=[
            pl.BlockSpec(memory_space=pltpu.SMEM),
            per_row,
            per_key,
            per_key,
            pl.BlockSpec((2 * group, rows, length), lambda h: (h, 0, 0)),
            pl.BlockSpec((rows, 1), lambda h: (0, 0)),
        ]
        + [pl.BlockSpec(memory_space=pl.ANY)] * len(waits),
        out_specs=[
            per_row,
            per_row,
            pl.BlockSpec((2 * group, 2, rows, length), lambda h: (h, 0, 0, 0)),
        ],
        out_shape=[
            jax.ShapeDtypeStruct((2, rows, width), F32),
            jax.ShapeDtypeStruct((2, rows, width), LOW),
            jax.ShapeDtypeStruct((2 * pairs, 2, rows, length), LOW),
        ],
        compiler_params=pltpu.CompilerParams(vmem_limit_bytes=VMEM_LIMIT),
        cost_estimate=pl.CostEstimate(
            flops=16 * rows * length * width,
            bytes_accessed=pairs * rows * length * 16,
            transcendentals=4 * pairs * rows * length,
        ),
        name="attend",
    )(window, queries, keys, values, bias, own, *waits)


def attend_back_kernel(window_ref, *refs):
    q_ref, k_ref, v_ref, do_ref, o_ref, p_ref = refs[:6]
    dq_ref, dk_ref, dv_ref, sum_ref, dk_sum, dv_sum = refs[-6:]
    rows, length = sum_ref.shape[1:]
    tile = rows // window_ref.shape[1]
    dk_sum[...] = jnp.zeros_like(dk_sum)
    dv_sum[...] = jnp.zeros_like(dv_sum)

    def step(lines, columns, span, first):
        first_half = lax.broadcasted_iota(jnp.int32, (2 * tile, 128), 1) < 64
        zero = jnp.zeros((2 * tile, 128), LOW)
        queries = q_ref[:, lines, :].reshape(2 * tile, 128) * jnp.array(0.125, LOW)
        grad_out = do_ref[:, lines, :].reshape(2 * tile, 128)
        out = o_ref[:, lines, :].reshape(2 * tile, 128)
        queries_t, grad_out_t = queries.T, grad_out.T
        keys, values = k_ref[columns, :], v_ref[columns, :]
        heads = [slice(0, 64), slice(64, 128)]
        mine = [jnp.where(first_half, grad_out, zero), jnp.where(first_half, zero, grad_out)]
        raw = [dot_nt(part, values) for part in mine]
        low_p = [p_ref[half, :, lines, columns].reshape(2 * tile, span) for half in range(2)]
        for half in range(2):
            dv_sum[heads[half], columns] += dot_nn(grad_out_t[heads[half]], low_p[half])
        delta = [jnp.sum(part.astype(F32) * out, axis=1, keepdims=True) for part in mine]
        grads = [low_p[half].astype(F32) * (raw[half] - delta[half]) for half in range(2)]
        lows = [grad.astype(LOW) for grad in grads]
        parts = [dot_nn(low, keys) for low in lows]
        for half in range(2):
            sum_ref[half, lines, columns] = (grads[half][:tile] + grads[half][tile:]).astype(LOW)
            dk_sum[heads[half], columns] += dot_nn(queries_t[heads[half]], lows[half])
        grad_q = (jnp.where(first_half, parts[0], parts[1]) * 0.125).astype(LOW)
        dq_ref[:, lines, :] = grad_q.reshape(2, tile, 128)

    by_window(window_ref, tile, length, step)
    dk_ref[...] = dk_sum[...].T.astype(LOW)
    dv_ref[...] = dv_sum[...].T.astype(LOW)


def attend_back_call(heads, window, queries, keys, values, grad_out, out, weights, partial, *waits):
    first, pairs = heads
    rows, width = queries.shape[1:]
    length = keys.shape[0]
    per_row = pl.BlockSpec((2, rows, 128), lambda h: (0, 0, h + first))
    per_key = pl.BlockSpec((length, 128), lambda h: (0, h + first))
    per_score = pl.BlockSpec((2, rows, length), lambda h: (h + first, 0, 0))
    begun = [] if partial is None else list(partial)
    return pl.pallas_call(
        attend_back_kernel,
        grid=(pairs,),
        in_specs=[
            pl.BlockSpec(memory_space=pltpu.SMEM),
            per_row,
            per_key,
            per_key,
            per_row,
            per_row,
            pl.BlockSpec((2, 2, rows, length), lambda h: (h + first, 0, 0, 0)),
        ]
        + [pl.BlockSpec(memory_space=pl.ANY)] * len(begun + list(waits)),
        out_specs=[per_row, per_key, per_key, per_score],
        out_shape=[
            jax.ShapeDtypeStruct((2, rows, width), LOW),
            jax.ShapeDtypeStruct((length, width), LOW),
            jax.ShapeDtypeStruct((length, width), LOW),
            jax.ShapeDtypeStruct((width // 64, rows, length), LOW),
        ],
        input_output_aliases={7 + index: index for index in range(len(begun))},
        scratch_shapes=[pltpu.VMEM((128, length), F32)] * 2,
        compiler_params=pltpu.CompilerParams(vmem_limit_bytes=VMEM_LIMIT),
        cost_estimate=pl.CostEstimate(
            flops=32 * rows * length * 128 * pairs,
            bytes_accessed=pairs * rows * length * 16,
            transcendentals=0,
        ),
        name="attend_back",
    )(window, queries, keys, values, grad_out, out, weights, *begun, *waits)


def table_kernel(layers, window_ref, place_ref, *refs):
    sum_refs, (out_ref, total_ref) = refs[:layers], refs[-2:]
    head_count, rows, length = sum_refs[0].shape
    bucket_count = out_ref.shape[0] // 8

    @pl.when(pl.program_id(0) == 0)
    def _():
        total_ref[...] = jnp.zeros_like(total_ref)

    at = pl.program_id(0) * window_ref.shape[1] // pl.num_programs(0)
    first = pl.multiple_of(window_ref[0, at] * 128, 128)
    for count in window_counts(length):

        @pl.when(window_ref[1, at] == count)
        def _(span=count * 128):
            key_place = first + lax.broadcasted_iota(jnp.int32, (8, span), 1)
            chosen, parts = [], []
            for lines in range(0, rows, 16):
                both = sum(ref[:, lines : lines + 16, pl.ds(first, span)].astype(F32) for ref in sum_refs)
                for row in range(0, 16, 8):
                    choice = bucket_of(key_place - place_ref[lines + row : lines + row + 8])
                    masks = [jnp.where(choice == bucket, 1.0, 0.0) for bucket in range(bucket_count)]
                    chosen.append(jnp.concatenate(masks, axis=0).astype(LOW))
                    parts.append(both[:, row : row + 8].reshape(head_count * 8, span).astype(LOW))
            total_ref[...] += dot_nt(jnp.concatenate(chosen, axis=1), jnp.concatenate(parts, axis=1))

    out_ref[...] = total_ref[...]


def table_call(window, score_sums, place, bucket_count, *waits):
    head_count, rows, length = score_sums[0].shape
    tile = min(128, rows)
    layers = len(score_sums)
    grouped = pl.pallas_call(
        functools.partial(table_kernel, layers),
        grid=(rows // tile,),
        in_specs=[
            pl.BlockSpec(memory_space=pltpu.SMEM),
            pl.BlockSpec((tile, 1), lambda i: (i, 0)),
        ]
        + [pl.BlockSpec((head_count, tile, length), lambda i: (0, i, 0))] * layers
        + [pl.BlockSpec(memory_space=pl.ANY)] * len(waits),
        out_specs=pl.BlockSpec((8 * bucket_count, 8 * head_count), lambda i: (0, 0)),
        out_shape=jax.ShapeDtypeStruct((8 * bucket_count, 8 * head_count), F32),
        scratch_shapes=[pltpu.VMEM((8 * bucket_count, 8 * head_count), F32)],
        compiler_params=pltpu.CompilerParams(vmem_limit_bytes=VMEM_LIMIT),
        cost_estimate=pl.CostEstimate(
            flops=512 * rows * length * head_count,
            bytes_accessed=rows * length * head_count * 4,
            transcendentals=0,
        ),
        name="table_sums",
    )(window, place, *score_sums, *waits)
    grouped = grouped.reshape(bucket_count, 8, head_count, 8)
    return jnp.sum(grouped * jnp.eye(8, dtype=F32)[None, :, None, :], axis=(1, 3))


def norm_rows(tensor, scale_row, shift_row):
    center = tensor - jnp.mean(tensor, axis=1, keepdims=True)
    inverse = lax.rsqrt(jnp.mean(center * center, axis=1, keepdims=True) + 1e-05)
    return center * inverse * scale_row + shift_row, inverse


def norm_rows_back(grad, normal, inverse, scale_row):
    scaled = grad * scale_row
    mean_one = jnp.mean(scaled, axis=1, keepdims=True)
    mean_two = jnp.mean(scaled * normal, axis=1, keepdims=True)
    return inverse * (scaled - mean_one - normal * mean_two)


def pieces_of(pieces):
    arrays, plan = [], []
    for pair in pieces:
        spots = []
        for array, first in pair:
            known = [i for i, other in enumerate(arrays) if other is array]
            if not known:
                arrays.append(array)
            spots.append((known[0] if known else len(arrays) - 1, first))
        plan.append(tuple(spots))
    return arrays, tuple(plan)


def layer_tail_kernel(count, plan, span, *refs):
    (stream_ref, out_ref, proj_ref), refs = refs[:3], refs[3:]
    piece_refs, refs = refs[:count], refs[count:]
    gain_ref, shift_ref = refs[:2]
    result_ref, low_ref, middle_ref, middle_low_ref, active_ref, slope_ref, one_ref, two_ref = refs[-8:]
    mixed = stream_ref[...].astype(F32) + dot_nn(out_ref[...], proj_ref[...])
    middle, one_ref[...] = norm_rows(mixed, gain_ref[0:1], shift_ref[0:1])
    middle_ref[...] = middle
    middle_low = middle.astype(LOW)
    middle_low_ref[...] = middle_low
    total = middle
    for index, ((inner_at, inner_first), (outer_at, outer_first)) in enumerate(plan):
        columns = slice(index * span, (index + 1) * span)
        inner = dot_nn(middle_low, piece_refs[inner_at][:, inner_first : inner_first + span])
        cdf = 0.5 + 0.5 * lax.erf(inner * (2.0**-0.5))
        active = (inner * cdf).astype(LOW)
        active_ref[:, columns] = active
        density = jnp.exp(inner * inner * -0.5) * 0.3989422804014327
        slope_ref[:, columns] = (cdf + inner * density).astype(LOW)
        total = total + dot_nt(active, piece_refs[outer_at][:, outer_first : outer_first + span])
    result, two_ref[...] = norm_rows(total, gain_ref[1:2], shift_ref[1:2])
    result_ref[...] = result
    low_ref[...] = result.astype(LOW)


def layer_tail_call(stream, out_low, proj, pieces, span, gains, shifts, part, partial, *waits):
    rows, width = stream.shape
    share = 1 if part is None else 2
    hidden = span * len(pieces)
    pieces, plan = pieces_of(pieces)
    proj, proj_at = proj
    tile = min(256, rows // share)
    first = (part or 0) * (rows // 2 // tile)
    begun = [] if partial is None else list(partial)

    def per_row(columns):
        return pl.BlockSpec((tile, columns), lambda i: (i + first, 0))

    def fixed(shape):
        return pl.BlockSpec(shape, lambda i: (0, 0), pipeline_mode=pl.Buffered(1))

    def whole(columns, kind):
        return jax.ShapeDtypeStruct((rows, columns), kind)

    return pl.pallas_call(
        functools.partial(layer_tail_kernel, len(pieces), plan, span),
        grid=(rows // share // tile,),
        in_specs=[per_row(width), per_row(width), pl.BlockSpec((width, width), lambda i: (0, proj_at), pipeline_mode=pl.Buffered(1))]
        + [fixed(piece.shape) for piece in pieces]
        + [fixed((2, width))] * 2
        + [pl.BlockSpec(memory_space=pl.ANY)] * len(begun + list(waits)),
        out_specs=[
            per_row(width), per_row(width), per_row(width), per_row(width),
            per_row(hidden), per_row(hidden), per_row(1), per_row(1),
        ],
        out_shape=[
            whole(width, F32), whole(width, LOW), whole(width, F32), whole(width, LOW),
            whole(hidden, LOW), whole(hidden, LOW), whole(1, F32), whole(1, F32),
        ],
        input_output_aliases={5 + len(pieces) + index: index for index in range(len(begun))},
        compiler_params=pltpu.CompilerParams(vmem_limit_bytes=VMEM_LIMIT),
        cost_estimate=pl.CostEstimate(
            flops=2 * rows // share * width * (width + 2 * hidden),
            bytes_accessed=4 * rows * hidden + 12 * rows * width + 4 * width * hidden,
            transcendentals=2 * rows * hidden,
        ),
        name="layer_tail",
    )(stream, out_low, proj, *pieces, gains, shifts, *begun, *waits)


def layer_tail_back_kernel(count, plan, span, *refs):
    (grad_ref, result_ref, two_ref, middle_ref, one_ref, slope_ref, proj_ref), refs = refs[:7], refs[7:]
    piece_refs, refs = refs[:count], refs[count:]
    gain_ref, shift_ref, begun_ref = refs[:3]
    two_low_ref, inner_ref, stream_ref, branch_ref, out_ref, terms_ref = refs[-6:]

    @pl.when(pl.program_id(0) == 0)
    def _():
        terms_ref[...] = begun_ref[...]

    grad = grad_ref[...].astype(F32)
    normal = (result_ref[...] - shift_ref[1:2]) / gain_ref[1:2]
    terms_ref[1:2] += jnp.sum(grad * normal, axis=0, keepdims=True)
    terms_ref[3:4] += jnp.sum(grad, axis=0, keepdims=True)
    grad = norm_rows_back(grad, normal, two_ref[...], gain_ref[1:2])
    low = grad.astype(LOW)
    two_low_ref[...] = low
    for index, ((inner_at, inner_first), (outer_at, outer_first)) in enumerate(plan):
        columns = slice(index * span, (index + 1) * span)
        outer_piece = piece_refs[outer_at][:, outer_first : outer_first + span]
        inner = (dot_nn(low, outer_piece) * slope_ref[:, columns].astype(F32)).astype(LOW)
        inner_ref[:, columns] = inner
        grad = grad + dot_nt(inner, piece_refs[inner_at][:, inner_first : inner_first + span])
    normal = (middle_ref[...] - shift_ref[0:1]) / gain_ref[0:1]
    terms_ref[0:1] += jnp.sum(grad * normal, axis=0, keepdims=True)
    terms_ref[2:3] += jnp.sum(grad, axis=0, keepdims=True)
    grad = norm_rows_back(grad, normal, one_ref[...], gain_ref[0:1])
    stream_ref[...] = grad
    low = grad.astype(LOW)
    branch_ref[...] = low
    out_ref[...] = dot_nt(low, proj_ref[...]).astype(LOW)


def layer_tail_back_call(grad, result, two, middle, one, slope, proj, pieces, span, gains, shifts, part, partial, *waits):
    rows, width = result.shape
    share = 1 if part is None else 2
    hidden = span * len(pieces)
    pieces, plan = pieces_of(pieces)
    proj, proj_at = proj
    tile = min(256, rows // share)

    first = (part or 0) * (rows // 2 // tile)
    begun = [] if partial is None else list(partial[:-1])
    terms = jnp.zeros((8, width), F32) if partial is None else partial[-1]

    def per_row(columns):
        return pl.BlockSpec((tile, columns), lambda i: (i + first, 0))

    def fixed(shape):
        return pl.BlockSpec(shape, lambda i: (0, 0), pipeline_mode=pl.Buffered(1))

    def whole(columns, kind):
        return jax.ShapeDtypeStruct((rows, columns), kind)

    return pl.pallas_call(
        functools.partial(layer_tail_back_kernel, len(pieces), plan, span),
        grid=(rows // share // tile,),
        in_specs=[pl.BlockSpec((tile, width), lambda i: (i, 0)), per_row(width), per_row(1), per_row(width), per_row(1), per_row(hidden)]
        + [pl.BlockSpec((width, width), lambda i: (0, proj_at), pipeline_mode=pl.Buffered(1))]
        + [fixed(piece.shape) for piece in pieces]
        + [fixed((2, width))] * 2
        + [fixed((8, width))]
        + [pl.BlockSpec(memory_space=pl.ANY)] * len(begun + list(waits)),
        out_specs=[
            per_row(width), per_row(hidden), per_row(width), per_row(width), per_row(width),
            pl.BlockSpec((8, width), lambda i: (0, 0)),
        ],
        out_shape=[
            whole(width, LOW), whole(hidden, LOW), whole(width, F32), whole(width, LOW), whole(width, LOW),
            jax.ShapeDtypeStruct((8, width), F32),
        ],
        input_output_aliases={10 + len(pieces) + index: index for index in range(len(begun))},
        compiler_params=pltpu.CompilerParams(vmem_limit_bytes=VMEM_LIMIT),
        cost_estimate=pl.CostEstimate(
            flops=2 * rows // share * width * (width + 2 * hidden),
            bytes_accessed=4 * rows * hidden + 20 * rows * width + 4 * width * hidden,
            transcendentals=0,
        ),
        name="layer_tail_back",
    )(grad, result, two, middle, one, slope, proj, *pieces, gains, shifts, terms, *begun, *waits)


def product_kernel(plan, side_ref, *refs):
    step = pl.program_id(0)
    for index, (lhs, rhs, out, plus) in enumerate(plan):

        @pl.when(step == index)
        def _(lhs=lhs, rhs=rhs, out=out, plus=plus):
            total = dot_tn(refs[lhs][...], refs[rhs][...])
            if plus is not None:
                total = total + refs[plus][...].astype(F32)
            refs[out][...] = total.astype(refs[out].dtype)


def products_call(name, side, steps, outs, waits=()):
    arrays, specs, plan, place = [], [], [], {}
    total = len(steps)

    def column_of(kind, side_ref):
        if kind == "side":
            return side_ref[0]
        if kind == "other":
            return 1 - side_ref[0]
        return kind

    def chain(at):
        table = []
        for step in range(total):
            later = [at[u] for u in sorted(at) if u >= step]
            table.append(later[0] if later else at[max(at)])
        def index(i, side_ref):
            value = column_of(table[-1], side_ref)
            for step in reversed(range(total - 1)):
                if table[step] != table[step + 1]:
                    value = jnp.where(i <= step, column_of(table[step], side_ref), value)
            return (0, value)
        return index

    uses = {}
    for step, (lhs, rhs, span, block, out, out_block, plus) in enumerate(steps):
        uses.setdefault(("in", id(lhs), lhs.shape[1]), [lhs, {}])[1][step] = 0
        uses.setdefault(("in", id(rhs), span), [rhs, {}])[1][step] = block
        if plus is not None:
            uses.setdefault(("in", id(plus), outs[out][2]), [plus, {}])[1][step] = out_block
    for key, (array, at) in uses.items():
        place[key] = len(arrays)
        arrays.append(array)
        specs.append(pl.BlockSpec((array.shape[0], key[2]), chain(at)))
    first_out = len(arrays) + len(waits)
    out_names = list(outs)
    out_specs = []
    for out in out_names:
        at = {step: entry[5] for step, entry in enumerate(steps) if entry[4] == out}
        out_specs.append(pl.BlockSpec((outs[out][0], outs[out][2]), chain(at)))
    flops = 0
    for lhs, rhs, span, block, out, out_block, plus in steps:
        flops += 2 * lhs.shape[0] * lhs.shape[1] * span
        plan.append(
            (
                place[("in", id(lhs), lhs.shape[1])],
                place[("in", id(rhs), span)],
                first_out + out_names.index(out),
                None if plus is None else place[("in", id(plus), outs[out][2])],
            )
        )
    results = pl.pallas_call(
        functools.partial(product_kernel, plan),
        grid_spec=pltpu.PrefetchScalarGridSpec(
            num_scalar_prefetch=1,
            grid=(total,),
            in_specs=specs + [pl.BlockSpec(memory_space=pl.ANY)] * len(waits),
            out_specs=out_specs,
        ),
        out_shape=[jax.ShapeDtypeStruct(outs[out][:2], LOW) for out in out_names],
        compiler_params=pltpu.CompilerParams(vmem_limit_bytes=VMEM_LIMIT),
        cost_estimate=pl.CostEstimate(flops=flops, bytes_accessed=flops // 300, transcendentals=0),
        name=name,
    )(side, *arrays, *waits)
    return dict(zip(out_names, results))


def hold_kernel(*refs):
    del refs


def hold(tensor, *waits):
    anywhere = pl.BlockSpec(memory_space=pl.ANY)
    return pl.pallas_call(
        hold_kernel,
        in_specs=[anywhere] * (1 + len(waits)),
        out_specs=anywhere,
        out_shape=jax.ShapeDtypeStruct(tensor.shape, tensor.dtype),
        input_output_aliases={0: 0},
        cost_estimate=pl.CostEstimate(flops=0, bytes_accessed=0, transcendentals=0),
        name="hold",
    )(tensor, *waits)


def place_kernel(count, place_ref, *refs):
    out_ref = refs[-1]
    for index in range(count):
        out_ref[place_ref[index]] = refs[index][...]


def place_call(name, parts, spots, waits):
    shape = (len(parts), *parts[0].shape)
    return pl.pallas_call(
        functools.partial(place_kernel, len(parts)),
        in_specs=[pl.BlockSpec(memory_space=pltpu.SMEM)]
        + [pl.BlockSpec(memory_space=pltpu.VMEM)] * len(parts)
        + [pl.BlockSpec(memory_space=pl.ANY)] * len(waits),
        out_specs=pl.BlockSpec(memory_space=pltpu.VMEM),
        out_shape=jax.ShapeDtypeStruct(shape, parts[0].dtype),
        compiler_params=pltpu.CompilerParams(vmem_limit_bytes=VMEM_LIMIT),
        cost_estimate=pl.CostEstimate(flops=0, bytes_accessed=4 * parts[0].size * len(parts), transcendentals=0),
        name=name,
    )(jnp.stack(spots).astype(jnp.int32), *parts, *waits)


def weave_kernel(count, place_ref, *refs):
    out_ref = refs[-1]
    for index in range(count):
        for row in range(refs[index].shape[0]):
            out_ref[row, place_ref[index]] = refs[index][row]


def weave_call(name, parts, spots, waits):
    lead, *rest = parts[0].shape
    return pl.pallas_call(
        functools.partial(weave_kernel, len(parts)),
        in_specs=[pl.BlockSpec(memory_space=pltpu.SMEM)]
        + [pl.BlockSpec(memory_space=pltpu.VMEM)] * len(parts)
        + [pl.BlockSpec(memory_space=pl.ANY)] * len(waits),
        out_specs=pl.BlockSpec(memory_space=pltpu.VMEM),
        out_shape=jax.ShapeDtypeStruct((lead, len(parts), *rest), parts[0].dtype),
        compiler_params=pltpu.CompilerParams(vmem_limit_bytes=VMEM_LIMIT),
        cost_estimate=pl.CostEstimate(flops=0, bytes_accessed=4 * parts[0].size * len(parts), transcendentals=0),
        name=name,
    )(jnp.stack(spots).astype(jnp.int32), *parts, *waits)


class Grid:
    def __init__(self, mesh):
        self.blocks = mesh.shape["blk"]
        self.total = mesh.shape["dp"]
        self.paired = self.blocks == 2 and self.total == 16
        self.high = 4
        self.low = self.total // 8

    def place(self):
        index = lax.axis_index("dp")
        self.core_at = index % 2
        self.low_at = index // 2 % self.low
        self.high_at = index // (2 * self.low)
        self.block_at = lax.axis_index("blk")

    def from_core(self, tensor):
        return lax.ppermute(tensor, "dp", [(i, i ^ 1) for i in range(self.total)])

    def from_block(self, tensor):
        return lax.ppermute(tensor, "blk", [(0, 1), (1, 0)])

    def from_low(self, tensor, step):
        span = 2 * self.low
        pairs = [(i, i // span * span + (i + 2 * step) % span) for i in range(self.total)]
        return lax.ppermute(tensor, "dp", pairs)

    def from_high(self, tensor, step):
        return lax.ppermute(tensor, "dp", [(i, (i + 2 * self.low * step) % self.total) for i in range(self.total)])

    def gather(self, shard):
        return lax.all_gather(shard, "dp", axis=0, tiled=True)

    def gather_chip(self, inner, outer, halves, waits):
        rows, columns = inner.shape
        width = columns // 4

        def chosen(core):
            own, other = ((2 * block + core) * width for block in (self.block_at, 1 - self.block_at))
            parts = ((inner, own), (outer, own), (outer, other))[: 3 if halves else 2]
            return jnp.concatenate([lax.dynamic_slice_in_dim(shard, first, width, 1) for shard, first in parts], axis=1)

        mine = chosen(self.core_at)
        other = self.from_core(chosen(1 - self.core_at))
        chip = place_call("chip_rows", [mine, other], [self.core_at, 1 - self.core_at], waits)
        return chip.reshape(2 * rows, -1)

    def gather_line(self, chip, waits):
        parts = [chip] + [self.from_high(chip, step) for step in range(1, self.high)]
        spots = [(self.high_at - step) % self.high for step in range(self.high)]
        return place_call("line_rows", parts, spots, waits)

    def gather_sheet(self, line, waits):
        parts = [line] + [self.from_low(line, step) for step in range(1, self.low)]
        spots = [(self.low_at - step) % self.low for step in range(self.low)]
        return weave_call("sheet_rows", parts, spots, waits).reshape(-1, line.shape[2])

    def scatter_begin(self, tensor, axis):
        size, index, send = (
            (self.low, self.low_at, self.from_low) if axis == 1 else (self.high, self.high_at, self.from_high)
        )

        def at(step):
            return lax.dynamic_index_in_dim(tensor, (index + step) % size, axis, False)

        return at(0), [send(at(step), step) for step in range(1, size)]

    def low_begin(self, tensor):
        rows, columns = tensor.shape
        return self.scatter_begin(tensor.reshape(self.high, self.low, -1, columns), 1)

    def high_begin(self, tensor):
        return self.scatter_begin(tensor, 0)

    def scatter_end(self, begun, *waits):
        own, arrived = begun
        if waits:
            arrived = [hold(arrived[0], *waits), *arrived[1:]]
        return sum((tensor.astype(F32) for tensor in arrived), own.astype(F32)).astype(LOW)

    def sum_blocks(self, tensor):
        return (tensor.astype(F32) + self.from_block(tensor).astype(F32)).astype(LOW)

    def halves(self, tensor):
        rows = tensor.shape[0] // 2
        own = lax.dynamic_slice_in_dim(tensor, self.core_at * rows, rows, 0)
        other = self.from_core(lax.dynamic_slice_in_dim(tensor, (1 - self.core_at) * rows, rows, 0))
        first = self.core_at == 0
        return jnp.where(first, own, other), jnp.where(first, other, own)

    def sum_all(self, tensor):
        if not self.paired or self.total & (self.total - 1):
            return lax.psum(tensor, ("blk", "dp"))
        tensor = tensor + self.from_block(tensor)
        bit = 1
        while bit < self.total:
            tensor = tensor + lax.ppermute(tensor, "dp", [(i, i ^ bit) for i in range(self.total)])
            bit *= 2
        return tensor

    def scatter(self, tensor):
        return self.scatter_end_blocks(self.scatter_rows(tensor))

    def scatter_rows(self, tensor):
        return lax.psum_scatter(tensor, "dp", scatter_dimension=0, tiled=True)

    def scatter_end_blocks(self, part):
        if self.blocks == 2:
            return part.astype(F32) + self.from_block(part).astype(F32)
        return lax.psum(part, "blk").astype(F32)


def shards(
    grid,
    content_in,
    query_in,
    cot_content,
    cot_query,
    attn_weights,
    out_weight,
    ffn_in,
    ffn_out_t,
    norm_gains,
    norm_shifts,
    bias_table,
    permutation,
    predicted,
    doc_lengths,
):
    _, rows, width = content_in.shape
    length = permutation.shape[1]
    blocks = length // rows
    bucket_count, head_count = bias_table.shape
    layer_count = attn_weights.shape[0]
    grid.place()
    block_index = grid.block_at

    paired = grid.paired
    layers = range(layer_count)

    def chip_of(layer_index, *waits):
        return grid.gather_chip(ffn_in[layer_index], ffn_out_t[layer_index], layer_index > 0, waits)

    chip = chip_of(0) if paired else None
    sides = jnp.stack([block_index, 1 - block_index]) if paired else (block_index + jnp.arange(blocks)) % blocks
    (
        window, key_doc, key_rank, place_column, place_doc, place_rank, own_column, sorter, stream_low, grad_low,
        *spreads,
    ) = setup_call(
        sides.astype(jnp.int32), doc_lengths, permutation, predicted,
        (content_in[0], query_in[0], cot_content[0], cot_query[0]), *((chip,) if paired else ()),
    )
    stream = stream_low
    table_rows = jnp.concatenate(
        [bias_table.T, jnp.full((head_count, 128 - bucket_count), MASKED, F32)], axis=1
    )

    def other_blocks(tensor, come):
        if paired:
            come = grid.from_block(tensor) if come is None else come
            return (dot_tn(spreads[0], tensor) + dot_tn(spreads[1], come)).astype(LOW)
        gathered = lax.all_gather(tensor, "blk", axis=0, tiled=False)
        parts = [
            dot_tn(spread, lax.dynamic_index_in_dim(gathered, (block_index + step) % blocks, 0, False))
            for step, spread in enumerate(spreads)
        ]
        return sum(parts).astype(LOW)

    hidden = ffn_in.shape[2]
    span = hidden // 4 if paired else hidden
    bias = bias_call(
        window, table_rows, place_column, place_doc, place_rank, key_doc, key_rank, *((chip,) if paired else ())
    )
    first_qkv = attn_weights[0]
    if paired:
        line = grid.gather_line(chip, (bias,))
        if layer_count > 1:
            next_chip = chip_of(1, line)
        sheet = grid.gather_sheet(line, ())
    first_qkv = grid.gather(first_qkv)
    if paired:
        first_qkv = hold(first_qkv, sheet)
    others = grid.gather(
        jnp.concatenate([out_weight[i] for i in layers] + [attn_weights[i] for i in layers[1:]], axis=1)
    )
    starts = [(layer_count + 3 * index) * width for index in range(layer_count - 1)]
    qkv_full = [first_qkv] + [others[:, start : start + 3 * width] for start in starts]
    kept = []
    next_content = None
    all_pieces = []
    for layer_index in range(layer_count):
        qkv = qkv_full[layer_index]
        all_content = other_blocks(stream_low[:rows], next_content)
        queries = dot_nn(stream_low, qkv[:, :width]).astype(LOW).reshape(2, rows, width)
        keys = dot_nn(all_content, qkv[:, width : 2 * width]).astype(LOW)
        values = dot_nn(all_content, qkv[:, 2 * width :]).astype(LOW)
        later = ()
        more = paired and layer_index + 1 < layer_count
        if paired:
            if layer_index > 0:
                sheet = grid.gather_sheet(line, (stream_low, queries))
            later = (sheet,)
        if more:
            later = (sheet, next_chip)
        out, out_low, weights = attend_call(window, queries, keys, values, bias, own_column, *later)
        later = ()
        if paired:
            waits_near = (out_low,)
            if more:
                line = grid.gather_line(next_chip, (out_low,))
                waits_near = (out_low, line)
            beside = grid.from_core(sheet)
            if layer_index > 0:
                near = hold(grid.from_block(sheet[:, :span]), *waits_near)
                outers = ((sheet, span), (beside, span), (sheet, 2 * span), (beside, 2 * span))
            else:
                near = hold(grid.from_block(sheet), *waits_near)
            far = grid.from_core(near)
            quarters = (sheet, beside, near, far)
            if layer_index == 0:
                outers = [(quarter, span) for quarter in quarters]
            pieces = [((quarter, 0), outer) for quarter, outer in zip(quarters, outers)]
        else:
            pieces = [((grid.gather(ffn_in[layer_index]), 0), (grid.gather(ffn_out_t[layer_index]), 0))]
        all_pieces.append(pieces)
        if more:
            later = (line,)
            if layer_index + 2 < layer_count:
                next_chip = chip_of(layer_index + 2, line)
        out_low = out_low.reshape(2 * rows, width)
        partial = None
        for part in (0, 1) if more else (None,):
            partial = layer_tail_call(
                stream, out_low, (others, layer_index), pieces, span,
                norm_gains[layer_index], norm_shifts[layer_index], part, partial, *later,
            )
            if part == 0:
                next_content = grid.from_block(partial[1][:rows])
        result, low, middle, middle_low, active, slope, inverse_one, inverse_two = partial
        kept.append(
            (
                stream_low, all_content, queries, keys, values, out, out_low, weights,
                result, middle, middle_low, active, slope, inverse_one, inverse_two,
            )
        )
        stream, stream_low = result, low

    def unsort(tensor):
        return dot_tn(sorter, tensor)

    def unsort_wide(tensor):
        high = tensor.astype(LOW)
        rest = (tensor - high.astype(F32)).astype(LOW)
        return unsort(high) + unsort(rest)

    content_out = unsort(stream_low[:rows]).astype(LOW)
    query_out = unsort(stream_low[rows:]).astype(LOW)

    grad_stream = None
    norm_terms = [None] * layer_count
    matrix_rows = [None] * layer_count
    attn_rows = [None] * layer_count
    attn_parts = [None] * layer_count
    side = jnp.full((1,), grid.core_at, jnp.int32)
    pairs = width // 128
    score_sums = []
    pending = {}
    third = width // 2

    def content_side(own, come):
        own, grad_all = own
        if grad_all is not None:
            own = own + dot_nn(spreads[0], grad_all)
        return own + come.astype(F32)

    def keys_back(grad_k, grad_v, qkv):
        return (dot_nt(grad_k, qkv[:, width : 2 * width]) + dot_nt(grad_v, qkv[:, 2 * width :])).astype(LOW)

    def finish_rows(high):
        shared = grid.sum_blocks(high[:, 2 * span :])
        sides = grid.halves(jnp.concatenate([high[:, : 2 * span], shared], axis=1))
        proj_grad = jnp.concatenate([one[:, 2 * span :] for one in sides], axis=1)
        half = jnp.concatenate([one[:, : 2 * span] for one in sides], axis=1)
        other = grid.from_block(half)
        first = grid.block_at == 0
        quarters = (jnp.where(first, half, other), jnp.where(first, other, half))
        inner_grad, outer_grad = (
            jnp.concatenate(
                [
                    one[:, (2 * core + which) * span : (2 * core + which + 1) * span]
                    for one in quarters
                    for core in range(2)
                ],
                axis=1,
            )
            for which in range(2)
        )
        return tuple(tensor.astype(F32) for tensor in (proj_grad, inner_grad, outer_grad))

    def waits(*names):
        return [pending[name] for name in names if name in pending]

    come = None
    for layer_index in reversed(range(layer_count)):
        (
            stream_low, all_content, queries, keys, values, out, out_low, weights,
            result, middle, middle_low, active, slope, inverse_one, inverse_two,
        ) = kept[layer_index]
        qkv = qkv_full[layer_index]
        partial = None
        for part in (None,) if layer_index == layer_count - 1 else (1, 0):
            if part is None:
                grad = grad_low
            elif part == 1:
                grad = grad_stream[1]
            else:
                grad = content_side(grad_stream[0], hold(come, partial[0]) if paired else come)
            partial = layer_tail_back_call(
                grad, result, inverse_two, middle, inverse_one, slope, (others, layer_index),
                all_pieces[layer_index], span, norm_gains[layer_index], norm_shifts[layer_index],
                part, partial, *waits("attn"),
            )
        two_low, inner_low, grad_one, branch_low, grad_out, norm_terms[layer_index] = partial
        grad_out = grad_out.reshape(2, rows, width)
        back = (window, queries, keys, values, grad_out, out, weights)
        if paired:
            def steps(name, quarter, come=None):
                return [
                    (middle_low, inner_low, span, quarter, name, 0, come),
                    (two_low, active, span, quarter, name, 1, come),
                ]

            sent = products_call(
                "products_sent", side,
                steps("far", 3) + steps("beside", 1) + [(out_low, branch_low, third, "other", "proj", 0, None)],
                {"far": (width, 2 * span, span), "beside": (width, 2 * span, span), "proj": (width, third, third)},
                (),
            )
            come = {name: grid.from_core(tensor) for name, tensor in sent.items()}
            near = products_call(
                "products_near", side, steps("near", 2, come["far"]), {"near": (width, 2 * span, span)}
            )["near"]
            arrived = grid.from_block(near)
            held = products_call(
                "products_held", side,
                steps("mine", 0, come["beside"]) + [(out_low, branch_low, third, "side", "proj", 0, come["proj"])],
                {"mine": (width, 2 * span, span), "proj": (width, third, third)},
                [near],
            )
            partial = attend_back_call((0, pairs // 2), *back, None, *held.values())
            if "low_begun" in pending:
                pending["low"] = grid.scatter_end(pending["low_begun"], partial[0])
                pending["high_begun"] = grid.high_begin(pending["low"])
            grad_q, grad_k, grad_v, score_sum = attend_back_call(
                (pairs // 2, pairs - pairs // 2), *back, partial, *waits("low")
            )
            score_sums.append(score_sum)
            grad_q = grad_q.reshape(2 * rows, width)
            ffn_sum = (held["mine"].astype(F32) + arrived.astype(F32)).astype(LOW)
            ffn_sum = jnp.concatenate([ffn_sum, held["proj"]], axis=1)
            if layer_index == 0:
                ffn_begun = grid.low_begin(ffn_sum)
            if layer_index > 0:
                grad_all = keys_back(grad_k, grad_v, qkv)
                passed = dot_nn(spreads[1], grad_all).astype(LOW)
            attn = products_call(
                "products_attn", side,
                [
                    (lhs, rhs, width, 0, "attn", index, None)
                    for index, (lhs, rhs) in enumerate(
                        ((stream_low, grad_q), (all_content, grad_k), (all_content, grad_v))
                    )
                ],
                {"attn": (width, 3 * width, width)},
                [passed, ffn_sum] if layer_index > 0 else (),
            )["attn"]
            if layer_index == 0:
                grad_q, grad_k, grad_v = (hold(tensor, attn) for tensor in (grad_q, grad_k, grad_v))
                grad_all = keys_back(grad_k, grad_v, qkv)
                before = [grad_all]
                if "high_begun" in pending:
                    upper = grid.scatter_end(pending["high_begun"], attn)
                    before.append(upper)
                ffn_low = grid.scatter_end(ffn_begun, *before)
                ffn_begun = grid.high_begin(ffn_low)
                passed = dot_nn(spreads[1], grad_all).astype(LOW)
            attn_part = grid.scatter_rows(attn)
            attn_parts[layer_index] = attn_part
            if layer_index > 0:
                pending = {"attn": attn, "sum": ffn_sum, "low_begun": grid.low_begin(ffn_sum)}
            else:
                pending = {"passed": passed, "ffn_low": ffn_low}
        else:
            grad_q, grad_k, grad_v, score_sum = attend_back_call((0, pairs), *back, None)
            score_sums.append(score_sum)
            grad_q = grad_q.reshape(2 * rows, width)
            terms = [
                jnp.concatenate(
                    [dot_tn(stream_low, grad_q), dot_tn(all_content, grad_k), dot_tn(all_content, grad_v)], axis=1
                ),
                dot_tn(out_low, branch_low),
                dot_tn(middle_low, inner_low),
                dot_tn(two_low, active),
            ]
            attn_rows[layer_index], *matrix_rows[layer_index] = (grid.scatter(term.astype(LOW)) for term in terms)
        query_side = grad_one + dot_nt(grad_q, qkv[:, :width])
        grad_stream = [(query_side[:rows], grad_all if paired else None), query_side[rows:]]
        if layer_index == 0:
            rest = grad_stream[1]
            if paired:
                rest = hold(rest, ffn_low)
            query_grad = unsort_wide(rest)
            table_grad = table_call(
                window, score_sums, place_column, bucket_count, *([passed, ffn_low, query_grad] if paired else [])
            )
        if paired:
            come = grid.from_block(passed)
        else:
            grad_all = keys_back(grad_k, grad_v, qkv)
            grad_split = jnp.stack([dot_nn(spread, grad_all).astype(LOW) for spread in spreads])
            grad_split = jnp.roll(grad_split, block_index, axis=0)
            come = lax.psum_scatter(grad_split, "blk", scatter_dimension=0, tiled=False)
    if paired:
        come = hold(come, table_grad)
        ffn_high = grid.scatter_end(ffn_begun, table_grad)
        if layer_count > 1:
            matrix_rows[1] = finish_rows(hold(upper, table_grad))
        matrix_rows[0] = finish_rows(hold(ffn_high, attn_part))
        attn_rows = [grid.scatter_end_blocks(hold(part, table_grad)) for part in attn_parts]
    grad_stream[0] = content_side(grad_stream[0], come)
    table_lines = jnp.pad(table_grad.T, ((0, 0), (0, width - bucket_count)))
    sums = grid.sum_all(jnp.concatenate([*[terms[:4] for terms in norm_terms], table_lines], axis=0))
    norm_sum = sums[: 4 * layer_count].reshape(layer_count, 2, 2, width)
    table_total = sums[4 * layer_count :, :bucket_count].T
    matrix_grads = tuple(jnp.stack(rows_of, axis=0) for rows_of in (attn_rows, *zip(*matrix_rows)))
    return (
        content_out[None],
        query_out[None],
        unsort_wide(grad_stream[0])[None],
        query_grad[None],
        *matrix_grads,
        norm_sum[:, 0],
        norm_sum[:, 1],
        table_total,
    )


def solution(mesh):
    tokens = P("dp", "blk", None)
    matrix = P(None, "dp", None)
    whole = P()
    sequence = P("dp", None)
    return jax.shard_map(
        functools.partial(shards, Grid(mesh)),
        mesh=mesh,
        in_specs=(tokens,) * 4 + (matrix,) * 4 + (whole,) * 3 + (sequence,) * 3,
        out_specs=(tokens,) * 4 + (matrix,) * 4 + (whole,) * 3,
        check_vma=False,
    )
```

```python
import functools

import jax
import jax.numpy as jnp
from jax import lax
from jax.experimental import pallas as pl
from jax.experimental.pallas import tpu as pltpu
from jax.sharding import PartitionSpec as P

THRESHOLDS = (12, 16, 23, 32, 46, 64, 91)
MASKED = -1e30
F32 = jnp.float32
LOW = jnp.bfloat16
VMEM_LIMIT = 56 * 2**20
ROW_TILE = 128
PAIRS = 2


def dot_nn(left_side, right_side):
    return jnp.dot(left_side, right_side, preferred_element_type=F32)


def dot_nt(left_side, right_side):
    return lax.dot_general(left_side, right_side, (((1,), (1,)), ((), ())), preferred_element_type=F32)


def dot_tn(left_side, right_side):
    return lax.dot_general(left_side, right_side, (((0,), (0,)), ((), ())), preferred_element_type=F32)


def bucket_of(relative):
    distance = jnp.abs(relative)
    far_bucket = 8 + sum(((distance >= threshold).astype(jnp.int32) for threshold in THRESHOLDS))
    near_bucket = jnp.where(distance < 8, distance, jnp.minimum(far_bucket, 15))
    return jnp.where(relative > 0, 16, 0).astype(jnp.int32) + near_bucket


def window_counts(length):
    most = length // 128
    return [count for count in (2, 3, 4, 5, 6) if count < most] + [most]


def by_window(window_ref, tile, length, step):
    def one(at, carry):
        row = pl.multiple_of(at * tile, tile)
        first = pl.multiple_of(window_ref[0, at] * 128, 128)
        for count in window_counts(length):

            @pl.when(window_ref[1, at] == count)
            def _(count=count):
                step(pl.ds(row, tile), pl.ds(first, count * 128), count * 128, first)

        return carry

    lax.fori_loop(0, window_ref.shape[1], one, 0)


def setup_kernel(side_ref, lengths_ref, row_ref, column_ref, chosen_ref, *refs):
    streams, refs = refs[:4], refs[4:]
    outs = refs[-(11 + side_ref.shape[0]) :]
    window_ref, key_doc_ref, key_rank_ref, place_ref, doc_ref, rank_ref, own_ref, sorter_ref, low_ref, grad_ref = outs[:10]
    spread_refs = outs[10:-1]
    rank_row = outs[-1]
    length, rows = row_ref.shape[1], streams[0].shape[0]
    for first in range(0, length, 128):
        position = (first + lax.broadcasted_iota(jnp.int32, (length, 128), 1))
        rank = lax.broadcasted_iota(jnp.int32, (length, 128), 0).astype(F32)
        rank_row[:, first : first + 128] = jnp.sum(
            jnp.where(column_ref[...] == position, rank, 0.0), axis=0, keepdims=True
        )
    ranks = rank_row[...]
    position = lax.broadcasted_iota(jnp.int32, (1, length), 1)
    doc = jnp.zeros((1, length), jnp.int32)
    start = position == 0
    bound = 0
    for index in range(lengths_ref.shape[1] - 1):
        bound = bound + lengths_ref[0, index]
        doc = doc + (position >= bound).astype(jnp.int32)
        start = start | (position == bound)
    live = (chosen_ref[...] == 1) & jnp.logical_not(start)
    key_doc_ref[...] = doc
    key_rank_ref[...] = jnp.where(live, ranks, -1.0).astype(jnp.int32)
    below = (
        lax.broadcasted_iota(jnp.int32, (length, length), 0) <= lax.broadcasted_iota(jnp.int32, (length, length), 1)
    )
    below = jnp.where(below, 1.0, 0.0).astype(LOW)
    slot = lax.broadcasted_iota(jnp.int32, (rows, length), 0).astype(F32)
    for index, spread_ref in enumerate(spread_refs):
        least = (side_ref[index] * rows).astype(F32)
        owned = (ranks >= least) & (ranks < least + rows)
        counted = jnp.broadcast_to(jnp.where(owned, 1.0, 0.0), (8, length)).astype(LOW)
        order = jnp.where(owned, dot_nn(counted, below)[0:1] - 1.0, -1.0)
        chosen = slot == order
        spread_ref[...] = jnp.where(chosen, 1.0, 0.0).astype(LOW)
        if index == 0:

            def pick(row):
                return jnp.sum(jnp.where(chosen, row, 0.0), axis=1, keepdims=True)

            place = pick(position.astype(F32))
            rank = pick(ranks)
            place_ref[...] = place.astype(jnp.int32)
            rank_ref[...] = rank.astype(jnp.int32)
            doc_ref[...] = pick(doc.astype(F32)).astype(jnp.int32)
            own_ref[...] = jnp.where(pick(jnp.where(live, 1.0, 0.0)) > 0.0, place, -1.0).astype(jnp.int32)
            tile = rows // window_ref.shape[1]
            for at in range(window_ref.shape[1]):
                lines = place[at * tile : (at + 1) * tile]
                least_place = jnp.min(lines).astype(jnp.int32)
                most_place = jnp.max(lines).astype(jnp.int32)
                first, last, bound = 0, length, 0
                for doc_index in range(lengths_ref.shape[1] - 1):
                    bound = bound + lengths_ref[0, doc_index]
                    first = jnp.where(least_place >= bound, bound, first)
                    last = jnp.where((most_place < bound) & (last == length), bound, last)
                first = first // 128
                needed = (last + 127) // 128 - first
                count = length // 128
                for choice in reversed(window_counts(length)):
                    count = jnp.where(needed <= choice, choice, count)
                window_ref[0, at] = jnp.minimum(first, length // 128 - count)
                window_ref[1, at] = count
            spot = lax.broadcasted_iota(jnp.int32, (rows, rows), 1).astype(F32)
            sorter = jnp.where(spot == rank - least, 1.0, 0.0).astype(LOW)
            sorter_ref[...] = sorter
    for index, stream in enumerate(streams):
        target = (low_ref, grad_ref)[index // 2]
        target[index % 2 * rows : (index % 2 + 1) * rows] = dot_nn(sorter, stream[...]).astype(LOW)


def setup_call(sides, lengths, anchor, chosen, streams, *waits):
    length = anchor.shape[1]
    rows, width = streams[0].shape
    count = sides.shape[0]
    here = pl.BlockSpec(memory_space=pltpu.VMEM)
    scalars = pl.BlockSpec(memory_space=pltpu.SMEM)

    def whole(lines, columns, kind):
        return jax.ShapeDtypeStruct((lines, columns), kind)

    return pl.pallas_call(
        setup_kernel,
        in_specs=[scalars, scalars, here, here, here] + [here] * 4 + [pl.BlockSpec(memory_space=pl.ANY)] * len(waits),
        out_specs=[scalars] + [here] * (9 + count),
        out_shape=[whole(2, rows // min(ROW_TILE, rows), jnp.int32)]
        + [whole(1, length, jnp.int32)] * 2
        + [whole(rows, 1, jnp.int32)] * 4
        + [whole(rows, rows, LOW), whole(2 * rows, width, LOW), whole(2 * rows, width, LOW)]
        + [whole(rows, length, LOW)] * count,
        scratch_shapes=[pltpu.VMEM((1, length), F32)],
        compiler_params=pltpu.CompilerParams(vmem_limit_bytes=VMEM_LIMIT),
        cost_estimate=pl.CostEstimate(flops=8 * rows * rows * width, bytes_accessed=16 * rows * width, transcendentals=0),
        name="setup_rows",
    )(sides, lengths, anchor, anchor.reshape(length, 1), chosen, *streams, *waits)


def bias_kernel(window_ref, table_ref, place_ref, doc_ref, rank_ref, key_doc_ref, key_rank_ref, *refs):
    out_ref = refs[-1]
    head_count, rows, length = out_ref.shape
    place = place_ref[...]
    doc = doc_ref[...]
    rank = rank_ref[...]
    at = pl.program_id(0) * window_ref.shape[1] // pl.num_programs(0)
    for block in range(length // 128):
        first = block * 128

        @pl.when((block >= window_ref[0, at]) & (block < window_ref[0, at] + window_ref[1, at]))
        def _(first=first):
            key_place = first + lax.broadcasted_iota(jnp.int32, (rows, 128), 1)
            seen = (key_doc_ref[:, first : first + 128] == doc) & (
                key_rank_ref[:, first : first + 128] <= rank
            )
            choice = jnp.where(seen, bucket_of(key_place - place), 32)
            for head in range(head_count):
                line = jnp.broadcast_to(table_ref[head : head + 1, :], (8, 128))
                for row in range(0, rows, 16):
                    taken = [jnp.take_along_axis(line, choice[at : at + 8], axis=1) for at in (row, row + 8)]
                    out_ref[head, row : row + 16, first : first + 128] = jnp.concatenate(taken, axis=0).astype(LOW)


def bias_call(window, table_rows, place, doc, rank, key_doc, key_rank, *waits):
    head_count = table_rows.shape[0]
    rows, length = place.shape[0], key_doc.shape[1]
    tile = min(64, rows)
    column = pl.BlockSpec((tile, 1), lambda i: (i, 0))
    line = pl.BlockSpec((1, length), lambda i: (0, 0))
    return pl.pallas_call(
        bias_kernel,
        grid=(rows // tile,),
        in_specs=[
            pl.BlockSpec(memory_space=pltpu.SMEM),
            pl.BlockSpec((head_count, 128), lambda i: (0, 0)),
            column,
            column,
            column,
            line,
            line,
        ]
        + [pl.BlockSpec(memory_space=pl.ANY)] * len(waits),
        out_specs=pl.BlockSpec((head_count, tile, length), lambda i: (0, i, 0)),
        out_shape=jax.ShapeDtypeStruct((head_count, rows, length), LOW),
        compiler_params=pltpu.CompilerParams(vmem_limit_bytes=VMEM_LIMIT),
        cost_estimate=pl.CostEstimate(
            flops=0, bytes_accessed=head_count * rows * length * 8, transcendentals=0
        ),
        name="bias_rows",
    )(window, table_rows, place, doc, rank, key_doc, key_rank, *waits)


def attend_kernel(window_ref, q_ref, k_ref, v_ref, bias_ref, own_ref, *refs):
    o_ref, low_ref, p_ref = refs[-3:]
    length = bias_ref.shape[2]
    tile = bias_ref.shape[1] // window_ref.shape[1]
    heads = range(bias_ref.shape[0])

    def step(lines, columns, span, first):
        first_half = lax.broadcasted_iota(jnp.int32, (2 * tile, 128), 1) < 64
        zero = jnp.zeros((2 * tile, 128), LOW)
        hidden = lax.broadcasted_iota(jnp.int32, (tile, span), 1) == own_ref[lines, :] - first
        mine = []
        for head in heads:
            lanes = slice(head // 2 * 128, head // 2 * 128 + 128)
            queries = q_ref[:, lines, lanes].reshape(2 * tile, 128) * jnp.array(0.125, LOW)
            mine.append(jnp.where(first_half, queries, zero) if head % 2 == 0 else jnp.where(first_half, zero, queries))
        raw = [dot_nt(mine[head], k_ref[columns, head // 2 * 128 : head // 2 * 128 + 128]) for head in heads]
        scores = []
        for head in heads:
            bias = bias_ref[head, lines, columns].astype(F32)
            scores.append((raw[head][:tile] + bias, jnp.where(hidden, MASKED, raw[head][tile:] + bias)))
        most = [[jnp.max(part, axis=1, keepdims=True) for part in pair] for pair in scores]
        weights = [[jnp.exp(part - top) for part, top in zip(pair, tops)] for pair, tops in zip(scores, most)]
        shares = [[1.0 / jnp.sum(part, axis=1, keepdims=True) for part in pair] for pair in weights]
        lows = [[(part * share).astype(LOW) for part, share in zip(pair, both)] for pair, both in zip(weights, shares)]
        parts = []
        for head in heads:
            for stream in range(2):
                p_ref[head, stream, lines, columns] = lows[head][stream]
            values = v_ref[columns, head // 2 * 128 : head // 2 * 128 + 128]
            parts.append(dot_nn(jnp.concatenate(lows[head], axis=0), values))
        for pair in range(len(heads) // 2):
            lanes = slice(pair * 128, pair * 128 + 128)
            out = jnp.where(first_half, parts[2 * pair], parts[2 * pair + 1])
            o_ref[:, lines, lanes] = out.reshape(2, tile, 128)
            low_ref[:, lines, lanes] = out.astype(LOW).reshape(2, tile, 128)

    by_window(window_ref, tile, length, step)


def attend_call(window, queries, keys, values, bias, own, *waits):
    _, rows, width = queries.shape
    length = keys.shape[0]
    pairs = width // 128
    group = PAIRS
    per_row = pl.BlockSpec((2, rows, 128 * group), lambda h: (0, 0, h))
    per_key = pl.BlockSpec((length, 128 * group), lambda h: (0, h))
    return pl.pallas_call(
        attend_kernel,
        grid=(pairs // group,),
        in_specs=[
            pl.BlockSpec(memory_space=pltpu.SMEM),
            per_row,
            per_key,
            per_key,
            pl.BlockSpec((2 * group, rows, length), lambda h: (h, 0, 0)),
            pl.BlockSpec((rows, 1), lambda h: (0, 0)),
        ]
        + [pl.BlockSpec(memory_space=pl.ANY)] * len(waits),
        out_specs=[
            per_row,
            per_row,
            pl.BlockSpec((2 * group, 2, rows, length), lambda h: (h, 0, 0, 0)),
        ],
        out_shape=[
            jax.ShapeDtypeStruct((2, rows, width), F32),
            jax.ShapeDtypeStruct((2, rows, width), LOW),
            jax.ShapeDtypeStruct((2 * pairs, 2, rows, length), LOW),
        ],
        compiler_params=pltpu.CompilerParams(vmem_limit_bytes=VMEM_LIMIT),
        cost_estimate=pl.CostEstimate(
            flops=16 * rows * length * width,
            bytes_accessed=pairs * rows * length * 16,
            transcendentals=4 * pairs * rows * length,
        ),
        name="attend",
    )(window, queries, keys, values, bias, own, *waits)


def attend_back_kernel(window_ref, *refs):
    q_ref, k_ref, v_ref, do_ref, o_ref, p_ref = refs[:6]
    dq_ref, dk_ref, dv_ref, sum_ref, dk_sum, dv_sum = refs[-6:]
    rows, length = sum_ref.shape[1:]
    tile = rows // window_ref.shape[1]
    dk_sum[...] = jnp.zeros_like(dk_sum)
    dv_sum[...] = jnp.zeros_like(dv_sum)

    def step(lines, columns, span, first):
        first_half = lax.broadcasted_iota(jnp.int32, (2 * tile, 128), 1) < 64
        zero = jnp.zeros((2 * tile, 128), LOW)
        queries = q_ref[:, lines, :].reshape(2 * tile, 128) * jnp.array(0.125, LOW)
        grad_out = do_ref[:, lines, :].reshape(2 * tile, 128)
        out = o_ref[:, lines, :].reshape(2 * tile, 128)
        queries_t, grad_out_t = queries.T, grad_out.T
        keys, values = k_ref[columns, :], v_ref[columns, :]
        heads = [slice(0, 64), slice(64, 128)]
        mine = [jnp.where(first_half, grad_out, zero), jnp.where(first_half, zero, grad_out)]
        raw = [dot_nt(part, values) for part in mine]
        low_p = [p_ref[half, :, lines, columns].reshape(2 * tile, span) for half in range(2)]
        for half in range(2):
            dv_sum[heads[half], columns] += dot_nn(grad_out_t[heads[half]], low_p[half])
        delta = [jnp.sum(part.astype(F32) * out, axis=1, keepdims=True) for part in mine]
        grads = [low_p[half].astype(F32) * (raw[half] - delta[half]) for half in range(2)]
        lows = [grad.astype(LOW) for grad in grads]
        parts = [dot_nn(low, keys) for low in lows]
        for half in range(2):
            sum_ref[half, lines, columns] = (grads[half][:tile] + grads[half][tile:]).astype(LOW)
            dk_sum[heads[half], columns] += dot_nn(queries_t[heads[half]], lows[half])
        grad_q = (jnp.where(first_half, parts[0], parts[1]) * 0.125).astype(LOW)
        dq_ref[:, lines, :] = grad_q.reshape(2, tile, 128)

    by_window(window_ref, tile, length, step)
    dk_ref[...] = dk_sum[...].T.astype(LOW)
    dv_ref[...] = dv_sum[...].T.astype(LOW)


def attend_back_call(heads, window, queries, keys, values, grad_out, out, weights, partial, *waits):
    first, pairs = heads
    rows, width = queries.shape[1:]
    length = keys.shape[0]
    per_row = pl.BlockSpec((2, rows, 128), lambda h: (0, 0, h + first))
    per_key = pl.BlockSpec((length, 128), lambda h: (0, h + first))
    per_score = pl.BlockSpec((2, rows, length), lambda h: (h + first, 0, 0))
    begun = [] if partial is None else list(partial)
    return pl.pallas_call(
        attend_back_kernel,
        grid=(pairs,),
        in_specs=[
            pl.BlockSpec(memory_space=pltpu.SMEM),
            per_row,
            per_key,
            per_key,
            per_row,
            per_row,
            pl.BlockSpec((2, 2, rows, length), lambda h: (h + first, 0, 0, 0)),
        ]
        + [pl.BlockSpec(memory_space=pl.ANY)] * len(begun + list(waits)),
        out_specs=[per_row, per_key, per_key, per_score],
        out_shape=[
            jax.ShapeDtypeStruct((2, rows, width), LOW),
            jax.ShapeDtypeStruct((length, width), LOW),
            jax.ShapeDtypeStruct((length, width), LOW),
            jax.ShapeDtypeStruct((width // 64, rows, length), LOW),
        ],
        input_output_aliases={7 + index: index for index in range(len(begun))},
        scratch_shapes=[pltpu.VMEM((128, length), F32)] * 2,
        compiler_params=pltpu.CompilerParams(vmem_limit_bytes=VMEM_LIMIT),
        cost_estimate=pl.CostEstimate(
            flops=32 * rows * length * 128 * pairs,
            bytes_accessed=pairs * rows * length * 16,
            transcendentals=0,
        ),
        name="attend_back",
    )(window, queries, keys, values, grad_out, out, weights, *begun, *waits)


def table_kernel(layers, window_ref, place_ref, *refs):
    sum_refs, (out_ref, total_ref) = refs[:layers], refs[-2:]
    head_count, rows, length = sum_refs[0].shape
    bucket_count = out_ref.shape[0] // 8

    @pl.when(pl.program_id(0) == 0)
    def _():
        total_ref[...] = jnp.zeros_like(total_ref)

    at = pl.program_id(0) * window_ref.shape[1] // pl.num_programs(0)
    first = pl.multiple_of(window_ref[0, at] * 128, 128)
    for count in window_counts(length):

        @pl.when(window_ref[1, at] == count)
        def _(span=count * 128):
            key_place = first + lax.broadcasted_iota(jnp.int32, (8, span), 1)
            chosen, parts = [], []
            for lines in range(0, rows, 16):
                both = sum(ref[:, lines : lines + 16, pl.ds(first, span)].astype(F32) for ref in sum_refs)
                for row in range(0, 16, 8):
                    choice = bucket_of(key_place - place_ref[lines + row : lines + row + 8])
                    masks = [jnp.where(choice == bucket, 1.0, 0.0) for bucket in range(bucket_count)]
                    chosen.append(jnp.concatenate(masks, axis=0).astype(LOW))
                    parts.append(both[:, row : row + 8].reshape(head_count * 8, span).astype(LOW))
            total_ref[...] += dot_nt(jnp.concatenate(chosen, axis=1), jnp.concatenate(parts, axis=1))

    out_ref[...] = total_ref[...]


def table_call(window, score_sums, place, bucket_count, *waits):
    head_count, rows, length = score_sums[0].shape
    tile = min(128, rows)
    layers = len(score_sums)
    grouped = pl.pallas_call(
        functools.partial(table_kernel, layers),
        grid=(rows // tile,),
        in_specs=[
            pl.BlockSpec(memory_space=pltpu.SMEM),
            pl.BlockSpec((tile, 1), lambda i: (i, 0)),
        ]
        + [pl.BlockSpec((head_count, tile, length), lambda i: (0, i, 0))] * layers
        + [pl.BlockSpec(memory_space=pl.ANY)] * len(waits),
        out_specs=pl.BlockSpec((8 * bucket_count, 8 * head_count), lambda i: (0, 0)),
        out_shape=jax.ShapeDtypeStruct((8 * bucket_count, 8 * head_count), F32),
        scratch_shapes=[pltpu.VMEM((8 * bucket_count, 8 * head_count), F32)],
        compiler_params=pltpu.CompilerParams(vmem_limit_bytes=VMEM_LIMIT),
        cost_estimate=pl.CostEstimate(
            flops=512 * rows * length * head_count,
            bytes_accessed=rows * length * head_count * 4,
            transcendentals=0,
        ),
        name="table_sums",
    )(window, place, *score_sums, *waits)
    table = grouped.reshape(bucket_count, 8, head_count, 8)
    return jnp.sum(table * jnp.eye(8, dtype=F32)[None, :, None, :], axis=(1, 3)), grouped


def norm_rows(tensor, scale_row, shift_row):
    center = tensor - jnp.mean(tensor, axis=1, keepdims=True)
    inverse = lax.rsqrt(jnp.mean(center * center, axis=1, keepdims=True) + 1e-05)
    return center * inverse * scale_row + shift_row, inverse


def norm_rows_back(grad, normal, inverse, scale_row):
    scaled = grad * scale_row
    mean_one = jnp.mean(scaled, axis=1, keepdims=True)
    mean_two = jnp.mean(scaled * normal, axis=1, keepdims=True)
    return inverse * (scaled - mean_one - normal * mean_two)


def pieces_of(pieces):
    arrays, plan = [], []
    for pair in pieces:
        spots = []
        for array, first in pair:
            known = [i for i, other in enumerate(arrays) if other is array]
            if not known:
                arrays.append(array)
            spots.append((known[0] if known else len(arrays) - 1, first))
        plan.append(tuple(spots))
    return arrays, tuple(plan)


def layer_tail_kernel(count, plan, span, *refs):
    (stream_ref, out_ref, proj_ref), refs = refs[:3], refs[3:]
    piece_refs, refs = refs[:count], refs[count:]
    gain_ref, shift_ref = refs[:2]
    result_ref, low_ref, middle_ref, middle_low_ref, active_ref, slope_ref, one_ref, two_ref = refs[-8:]
    mixed = stream_ref[...].astype(F32) + dot_nn(out_ref[...], proj_ref[...])
    middle, one_ref[...] = norm_rows(mixed, gain_ref[0:1], shift_ref[0:1])
    middle_ref[...] = middle
    middle_low = middle.astype(LOW)
    middle_low_ref[...] = middle_low
    total = middle
    for index, ((inner_at, inner_first), (outer_at, outer_first)) in enumerate(plan):
        columns = slice(index * span, (index + 1) * span)
        inner = dot_nn(middle_low, piece_refs[inner_at][:, inner_first : inner_first + span])
        cdf = 0.5 + 0.5 * lax.erf(inner * (2.0**-0.5))
        active = (inner * cdf).astype(LOW)
        active_ref[:, columns] = active
        density = jnp.exp(inner * inner * -0.5) * 0.3989422804014327
        slope_ref[:, columns] = (cdf + inner * density).astype(LOW)
        total = total + dot_nt(active, piece_refs[outer_at][:, outer_first : outer_first + span])
    result, two_ref[...] = norm_rows(total, gain_ref[1:2], shift_ref[1:2])
    result_ref[...] = result
    low_ref[...] = result.astype(LOW)


def layer_tail_call(stream, out_low, proj, pieces, span, gains, shifts, part, partial, *waits):
    rows, width = stream.shape
    share = 1 if part is None else 2
    hidden = span * len(pieces)
    pieces, plan = pieces_of(pieces)
    proj, proj_at = proj
    tile = min(256, rows // share)
    first = (part or 0) * (rows // 2 // tile)
    begun = [] if partial is None else list(partial)

    def per_row(columns):
        return pl.BlockSpec((tile, columns), lambda i: (i + first, 0))

    def fixed(shape):
        return pl.BlockSpec(shape, lambda i: (0, 0), pipeline_mode=pl.Buffered(1))

    def whole(columns, kind):
        return jax.ShapeDtypeStruct((rows, columns), kind)

    return pl.pallas_call(
        functools.partial(layer_tail_kernel, len(pieces), plan, span),
        grid=(rows // share // tile,),
        in_specs=[per_row(width), per_row(width), pl.BlockSpec((width, width), lambda i: (0, proj_at), pipeline_mode=pl.Buffered(1))]
        + [fixed(piece.shape) for piece in pieces]
        + [fixed((2, width))] * 2
        + [pl.BlockSpec(memory_space=pl.ANY)] * len(begun + list(waits)),
        out_specs=[
            per_row(width), per_row(width), per_row(width), per_row(width),
            per_row(hidden), per_row(hidden), per_row(1), per_row(1),
        ],
        out_shape=[
            whole(width, F32), whole(width, LOW), whole(width, F32), whole(width, LOW),
            whole(hidden, LOW), whole(hidden, LOW), whole(1, F32), whole(1, F32),
        ],
        input_output_aliases={5 + len(pieces) + index: index for index in range(len(begun))},
        compiler_params=pltpu.CompilerParams(vmem_limit_bytes=VMEM_LIMIT),
        cost_estimate=pl.CostEstimate(
            flops=2 * rows // share * width * (width + 2 * hidden),
            bytes_accessed=4 * rows * hidden + 12 * rows * width + 4 * width * hidden,
            transcendentals=2 * rows * hidden,
        ),
        name="layer_tail",
    )(stream, out_low, proj, *pieces, gains, shifts, *begun, *waits)


def layer_tail_back_kernel(count, plan, span, *refs):
    (grad_ref, result_ref, two_ref, middle_ref, one_ref, slope_ref, proj_ref), refs = refs[:7], refs[7:]
    piece_refs, refs = refs[:count], refs[count:]
    gain_ref, shift_ref, begun_ref = refs[:3]
    two_low_ref, inner_ref, stream_ref, branch_ref, out_ref, terms_ref = refs[-6:]

    @pl.when(pl.program_id(0) == 0)
    def _():
        terms_ref[...] = begun_ref[...]

    grad = grad_ref[...].astype(F32)
    normal = (result_ref[...] - shift_ref[1:2]) / gain_ref[1:2]
    terms_ref[1:2] += jnp.sum(grad * normal, axis=0, keepdims=True)
    terms_ref[3:4] += jnp.sum(grad, axis=0, keepdims=True)
    grad = norm_rows_back(grad, normal, two_ref[...], gain_ref[1:2])
    low = grad.astype(LOW)
    two_low_ref[...] = low
    for index, ((inner_at, inner_first), (outer_at, outer_first)) in enumerate(plan):
        columns = slice(index * span, (index + 1) * span)
        outer_piece = piece_refs[outer_at][:, outer_first : outer_first + span]
        inner = (dot_nn(low, outer_piece) * slope_ref[:, columns].astype(F32)).astype(LOW)
        inner_ref[:, columns] = inner
        grad = grad + dot_nt(inner, piece_refs[inner_at][:, inner_first : inner_first + span])
    normal = (middle_ref[...] - shift_ref[0:1]) / gain_ref[0:1]
    terms_ref[0:1] += jnp.sum(grad * normal, axis=0, keepdims=True)
    terms_ref[2:3] += jnp.sum(grad, axis=0, keepdims=True)
    grad = norm_rows_back(grad, normal, one_ref[...], gain_ref[0:1])
    stream_ref[...] = grad
    low = grad.astype(LOW)
    branch_ref[...] = low
    out_ref[...] = dot_nt(low, proj_ref[...]).astype(LOW)


def layer_tail_back_call(grad, result, two, middle, one, slope, proj, pieces, span, gains, shifts, part, partial, *waits):
    rows, width = result.shape
    share = 1 if part is None else 2
    hidden = span * len(pieces)
    pieces, plan = pieces_of(pieces)
    proj, proj_at = proj
    tile = min(256, rows // share)

    first = (part or 0) * (rows // 2 // tile)
    begun = [] if partial is None else list(partial[:-1])
    terms = jnp.zeros((8, width), F32) if partial is None else partial[-1]

    def per_row(columns):
        return pl.BlockSpec((tile, columns), lambda i: (i + first, 0))

    def fixed(shape):
        return pl.BlockSpec(shape, lambda i: (0, 0), pipeline_mode=pl.Buffered(1))

    def whole(columns, kind):
        return jax.ShapeDtypeStruct((rows, columns), kind)

    return pl.pallas_call(
        functools.partial(layer_tail_back_kernel, len(pieces), plan, span),
        grid=(rows // share // tile,),
        in_specs=[pl.BlockSpec((tile, width), lambda i: (i, 0)), per_row(width), per_row(1), per_row(width), per_row(1), per_row(hidden)]
        + [pl.BlockSpec((width, width), lambda i: (0, proj_at), pipeline_mode=pl.Buffered(1))]
        + [fixed(piece.shape) for piece in pieces]
        + [fixed((2, width))] * 2
        + [fixed((8, width))]
        + [pl.BlockSpec(memory_space=pl.ANY)] * len(begun + list(waits)),
        out_specs=[
            per_row(width), per_row(hidden), per_row(width), per_row(width), per_row(width),
            pl.BlockSpec((8, width), lambda i: (0, 0)),
        ],
        out_shape=[
            whole(width, LOW), whole(hidden, LOW), whole(width, F32), whole(width, LOW), whole(width, LOW),
            jax.ShapeDtypeStruct((8, width), F32),
        ],
        input_output_aliases={10 + len(pieces) + index: index for index in range(len(begun))},
        compiler_params=pltpu.CompilerParams(vmem_limit_bytes=VMEM_LIMIT),
        cost_estimate=pl.CostEstimate(
            flops=2 * rows // share * width * (width + 2 * hidden),
            bytes_accessed=4 * rows * hidden + 20 * rows * width + 4 * width * hidden,
            transcendentals=0,
        ),
        name="layer_tail_back",
    )(grad, result, two, middle, one, slope, proj, *pieces, gains, shifts, terms, *begun, *waits)


def product_kernel(plan, side_ref, *refs):
    step = pl.program_id(0)
    for index, (lhs, rhs, out, plus) in enumerate(plan):

        @pl.when(step == index)
        def _(lhs=lhs, rhs=rhs, out=out, plus=plus):
            total = dot_tn(refs[lhs][...], refs[rhs][...])
            if plus is not None:
                total = total + refs[plus][...].astype(F32)
            refs[out][...] = total.astype(refs[out].dtype)


def products_call(name, side, steps, outs, waits=()):
    arrays, specs, plan, place = [], [], [], {}
    total = len(steps)

    def column_of(kind, side_ref):
        if kind == "side":
            return side_ref[0]
        if kind == "other":
            return 1 - side_ref[0]
        return kind

    def chain(at):
        table = []
        for step in range(total):
            later = [at[u] for u in sorted(at) if u >= step]
            table.append(later[0] if later else at[max(at)])
        def index(i, side_ref):
            value = column_of(table[-1], side_ref)
            for step in reversed(range(total - 1)):
                if table[step] != table[step + 1]:
                    value = jnp.where(i <= step, column_of(table[step], side_ref), value)
            return (0, value)
        return index

    uses = {}
    for step, (lhs, rhs, span, block, out, out_block, plus) in enumerate(steps):
        uses.setdefault(("in", id(lhs), lhs.shape[1]), [lhs, {}])[1][step] = 0
        uses.setdefault(("in", id(rhs), span), [rhs, {}])[1][step] = block
        if plus is not None:
            uses.setdefault(("in", id(plus), outs[out][2]), [plus, {}])[1][step] = out_block
    for key, (array, at) in uses.items():
        place[key] = len(arrays)
        arrays.append(array)
        specs.append(pl.BlockSpec((array.shape[0], key[2]), chain(at)))
    first_out = len(arrays) + len(waits)
    out_names = list(outs)
    out_specs = []
    for out in out_names:
        at = {step: entry[5] for step, entry in enumerate(steps) if entry[4] == out}
        out_specs.append(pl.BlockSpec((outs[out][0], outs[out][2]), chain(at)))
    flops = 0
    for lhs, rhs, span, block, out, out_block, plus in steps:
        flops += 2 * lhs.shape[0] * lhs.shape[1] * span
        plan.append(
            (
                place[("in", id(lhs), lhs.shape[1])],
                place[("in", id(rhs), span)],
                first_out + out_names.index(out),
                None if plus is None else place[("in", id(plus), outs[out][2])],
            )
        )
    results = pl.pallas_call(
        functools.partial(product_kernel, plan),
        grid_spec=pltpu.PrefetchScalarGridSpec(
            num_scalar_prefetch=1,
            grid=(total,),
            in_specs=specs + [pl.BlockSpec(memory_space=pl.ANY)] * len(waits),
            out_specs=out_specs,
        ),
        out_shape=[jax.ShapeDtypeStruct(outs[out][:2], LOW) for out in out_names],
        compiler_params=pltpu.CompilerParams(vmem_limit_bytes=VMEM_LIMIT),
        cost_estimate=pl.CostEstimate(flops=flops, bytes_accessed=flops // 300, transcendentals=0),
        name=name,
    )(side, *arrays, *waits)
    return dict(zip(out_names, results))


def hold_kernel(*refs):
    del refs


def hold(tensor, *waits):
    anywhere = pl.BlockSpec(memory_space=pl.ANY)
    return pl.pallas_call(
        hold_kernel,
        in_specs=[anywhere] * (1 + len(waits)),
        out_specs=anywhere,
        out_shape=jax.ShapeDtypeStruct(tensor.shape, tensor.dtype),
        input_output_aliases={0: 0},
        cost_estimate=pl.CostEstimate(flops=0, bytes_accessed=0, transcendentals=0),
        name="hold",
    )(tensor, *waits)


def place_kernel(count, place_ref, *refs):
    out_ref = refs[-1]
    for index in range(count):
        out_ref[place_ref[index]] = refs[index][...]


def place_call(name, parts, spots, waits):
    shape = (len(parts), *parts[0].shape)
    return pl.pallas_call(
        functools.partial(place_kernel, len(parts)),
        in_specs=[pl.BlockSpec(memory_space=pltpu.SMEM)]
        + [pl.BlockSpec(memory_space=pltpu.VMEM)] * len(parts)
        + [pl.BlockSpec(memory_space=pl.ANY)] * len(waits),
        out_specs=pl.BlockSpec(memory_space=pltpu.VMEM),
        out_shape=jax.ShapeDtypeStruct(shape, parts[0].dtype),
        compiler_params=pltpu.CompilerParams(vmem_limit_bytes=VMEM_LIMIT),
        cost_estimate=pl.CostEstimate(flops=0, bytes_accessed=4 * parts[0].size * len(parts), transcendentals=0),
        name=name,
    )(jnp.stack(spots).astype(jnp.int32), *parts, *waits)


def weave_kernel(count, place_ref, *refs):
    out_ref = refs[-1]
    for index in range(count):
        for row in range(refs[index].shape[0]):
            out_ref[row, place_ref[index]] = refs[index][row]


def weave_call(name, parts, spots, waits):
    lead, *rest = parts[0].shape
    return pl.pallas_call(
        functools.partial(weave_kernel, len(parts)),
        in_specs=[pl.BlockSpec(memory_space=pltpu.SMEM)]
        + [pl.BlockSpec(memory_space=pltpu.VMEM)] * len(parts)
        + [pl.BlockSpec(memory_space=pl.ANY)] * len(waits),
        out_specs=pl.BlockSpec(memory_space=pltpu.VMEM),
        out_shape=jax.ShapeDtypeStruct((lead, len(parts), *rest), parts[0].dtype),
        compiler_params=pltpu.CompilerParams(vmem_limit_bytes=VMEM_LIMIT),
        cost_estimate=pl.CostEstimate(flops=0, bytes_accessed=4 * parts[0].size * len(parts), transcendentals=0),
        name=name,
    )(jnp.stack(spots).astype(jnp.int32), *parts, *waits)


class Grid:
    def __init__(self, mesh):
        self.blocks = mesh.shape["blk"]
        self.total = mesh.shape["dp"]
        self.paired = self.blocks == 2 and self.total == 16
        self.high = 4
        self.low = self.total // 8

    def place(self):
        index = lax.axis_index("dp")
        self.core_at = index % 2
        self.low_at = index // 2 % self.low
        self.high_at = index // (2 * self.low)
        self.block_at = lax.axis_index("blk")

    def from_core(self, tensor):
        return lax.ppermute(tensor, "dp", [(i, i ^ 1) for i in range(self.total)])

    def from_block(self, tensor):
        return lax.ppermute(tensor, "blk", [(0, 1), (1, 0)])

    def from_low(self, tensor, step):
        span = 2 * self.low
        pairs = [(i, i // span * span + (i + 2 * step) % span) for i in range(self.total)]
        return lax.ppermute(tensor, "dp", pairs)

    def from_high(self, tensor, step):
        return lax.ppermute(tensor, "dp", [(i, (i + 2 * self.low * step) % self.total) for i in range(self.total)])

    def gather(self, shard):
        return lax.all_gather(shard, "dp", axis=0, tiled=True)

    def gather_chip(self, inner, outer, halves, waits):
        rows, columns = inner.shape
        width = columns // 4

        def chosen(core):
            own, other = ((2 * block + core) * width for block in (self.block_at, 1 - self.block_at))
            parts = ((inner, own), (outer, own), (outer, other))[: 3 if halves else 2]
            return jnp.concatenate([lax.dynamic_slice_in_dim(shard, first, width, 1) for shard, first in parts], axis=1)

        mine = chosen(self.core_at)
        other = self.from_core(chosen(1 - self.core_at))
        chip = place_call("chip_rows", [mine, other], [self.core_at, 1 - self.core_at], waits)
        return chip.reshape(2 * rows, -1)

    def gather_line(self, chip, waits):
        parts = [chip] + [self.from_high(chip, step) for step in range(1, self.high)]
        spots = [(self.high_at - step) % self.high for step in range(self.high)]
        return place_call("line_rows", parts, spots, waits)

    def gather_sheet(self, line, waits):
        parts = [line] + [self.from_low(line, step) for step in range(1, self.low)]
        spots = [(self.low_at - step) % self.low for step in range(self.low)]
        return weave_call("sheet_rows", parts, spots, waits).reshape(-1, line.shape[2])

    def scatter_begin(self, tensor, axis):
        size, index, send = (
            (self.low, self.low_at, self.from_low) if axis == 1 else (self.high, self.high_at, self.from_high)
        )

        def at(step):
            return lax.dynamic_index_in_dim(tensor, (index + step) % size, axis, False)

        return at(0), [send(at(step), step) for step in range(1, size)]

    def low_begin(self, tensor):
        rows, columns = tensor.shape
        return self.scatter_begin(tensor.reshape(self.high, self.low, -1, columns), 1)

    def high_begin(self, tensor):
        return self.scatter_begin(tensor, 0)

    def scatter_end(self, begun, *waits):
        own, arrived = begun
        if waits:
            arrived = [hold(arrived[0], *waits), *arrived[1:]]
        return sum((tensor.astype(F32) for tensor in arrived), own.astype(F32)).astype(LOW)

    def sum_blocks(self, tensor):
        return (tensor.astype(F32) + self.from_block(tensor).astype(F32)).astype(LOW)

    def halves(self, tensor):
        rows = tensor.shape[0] // 2
        own = lax.dynamic_slice_in_dim(tensor, self.core_at * rows, rows, 0)
        other = self.from_core(lax.dynamic_slice_in_dim(tensor, (1 - self.core_at) * rows, rows, 0))
        first = self.core_at == 0
        return jnp.where(first, own, other), jnp.where(first, other, own)

    def sum_all(self, tensor):
        if not self.paired or self.total & (self.total - 1):
            return lax.psum(tensor, ("blk", "dp"))
        tensor = tensor + self.from_block(tensor)
        bit = 1
        while bit < self.total:
            tensor = tensor + lax.ppermute(tensor, "dp", [(i, i ^ bit) for i in range(self.total)])
            bit *= 2
        return tensor

    def scatter(self, tensor):
        return self.scatter_end_blocks(self.scatter_rows(tensor))

    def scatter_rows(self, tensor):
        return lax.psum_scatter(tensor, "dp", scatter_dimension=0, tiled=True)

    def scatter_end_blocks(self, part):
        if self.blocks == 2:
            return part.astype(F32) + self.from_block(part).astype(F32)
        return lax.psum(part, "blk").astype(F32)


def shards(
    grid,
    content_in,
    query_in,
    cot_content,
    cot_query,
    attn_weights,
    out_weight,
    ffn_in,
    ffn_out_t,
    norm_gains,
    norm_shifts,
    bias_table,
    permutation,
    predicted,
    doc_lengths,
):
    _, rows, width = content_in.shape
    length = permutation.shape[1]
    blocks = length // rows
    bucket_count, head_count = bias_table.shape
    layer_count = attn_weights.shape[0]
    grid.place()
    block_index = grid.block_at

    paired = grid.paired
    layers = range(layer_count)

    def chip_of(layer_index, *waits):
        return grid.gather_chip(ffn_in[layer_index], ffn_out_t[layer_index], layer_index > 0, waits)

    chip = chip_of(0) if paired else None
    sides = jnp.stack([block_index, 1 - block_index]) if paired else (block_index + jnp.arange(blocks)) % blocks
    (
        window, key_doc, key_rank, place_column, place_doc, place_rank, own_column, sorter, stream_low, grad_low,
        *spreads,
    ) = setup_call(
        sides.astype(jnp.int32), doc_lengths, permutation, predicted,
        (content_in[0], query_in[0], cot_content[0], cot_query[0]), *((chip,) if paired else ()),
    )
    stream = stream_low
    table_rows = jnp.concatenate(
        [bias_table.T, jnp.full((head_count, 128 - bucket_count), MASKED, F32)], axis=1
    )

    def other_blocks(tensor, come):
        if paired:
            come = grid.from_block(tensor) if come is None else come
            return (dot_tn(spreads[0], tensor) + dot_tn(spreads[1], come)).astype(LOW)
        gathered = lax.all_gather(tensor, "blk", axis=0, tiled=False)
        parts = [
            dot_tn(spread, lax.dynamic_index_in_dim(gathered, (block_index + step) % blocks, 0, False))
            for step, spread in enumerate(spreads)
        ]
        return sum(parts).astype(LOW)

    hidden = ffn_in.shape[2]
    span = hidden // 4 if paired else hidden
    bias = bias_call(
        window, table_rows, place_column, place_doc, place_rank, key_doc, key_rank, *((chip,) if paired else ())
    )
    first_qkv = attn_weights[0]
    if paired:
        line = grid.gather_line(chip, (bias,))
        if layer_count > 1:
            next_chip = chip_of(1, line)
        sheet = grid.gather_sheet(line, ())
    first_qkv = grid.gather(first_qkv)
    if paired:
        first_qkv = hold(first_qkv, sheet)
    others = grid.gather(
        jnp.concatenate([out_weight[i] for i in layers] + [attn_weights[i] for i in layers[1:]], axis=1)
    )
    starts = [(layer_count + 3 * index) * width for index in range(layer_count - 1)]
    qkv_full = [first_qkv] + [others[:, start : start + 3 * width] for start in starts]
    kept = []
    next_content = None
    all_pieces = []
    for layer_index in range(layer_count):
        qkv = qkv_full[layer_index]
        all_content = other_blocks(stream_low[:rows], next_content)
        queries = dot_nn(stream_low, qkv[:, :width]).astype(LOW).reshape(2, rows, width)
        keys = dot_nn(all_content, qkv[:, width : 2 * width]).astype(LOW)
        values = dot_nn(all_content, qkv[:, 2 * width :]).astype(LOW)
        later = ()
        more = paired and layer_index + 1 < layer_count
        if paired:
            if layer_index > 0:
                sheet = grid.gather_sheet(line, (stream_low, queries))
            later = (sheet,)
        if more:
            later = (sheet, next_chip)
        out, out_low, weights = attend_call(window, queries, keys, values, bias, own_column, *later)
        later = ()
        if paired:
            waits_near = (out_low,)
            if more:
                line = grid.gather_line(next_chip, (out_low,))
                waits_near = (out_low, line)
            beside = grid.from_core(sheet)
            if layer_index > 0:
                near = hold(grid.from_block(sheet[:, :span]), *waits_near)
                outers = ((sheet, span), (beside, span), (sheet, 2 * span), (beside, 2 * span))
            else:
                near = hold(grid.from_block(sheet), *waits_near)
            far = grid.from_core(near)
            quarters = (sheet, beside, near, far)
            if layer_index == 0:
                outers = [(quarter, span) for quarter in quarters]
            pieces = [((quarter, 0), outer) for quarter, outer in zip(quarters, outers)]
        else:
            pieces = [((grid.gather(ffn_in[layer_index]), 0), (grid.gather(ffn_out_t[layer_index]), 0))]
        all_pieces.append(pieces)
        if more:
            later = (line,)
            if layer_index + 2 < layer_count:
                next_chip = chip_of(layer_index + 2, line)
        out_low = out_low.reshape(2 * rows, width)
        partial = None
        for part in (0, 1) if more else (None,):
            partial = layer_tail_call(
                stream, out_low, (others, layer_index), pieces, span,
                norm_gains[layer_index], norm_shifts[layer_index], part, partial, *later,
            )
            if part == 0:
                next_content = grid.from_block(partial[1][:rows])
        result, low, middle, middle_low, active, slope, inverse_one, inverse_two = partial
        kept.append(
            (
                stream_low, all_content, queries, keys, values, out, out_low, weights,
                result, middle, middle_low, active, slope, inverse_one, inverse_two,
            )
        )
        stream, stream_low = result, low

    def unsort(tensor):
        return dot_tn(sorter, tensor)

    def unsort_wide(tensor):
        high = tensor.astype(LOW)
        rest = (tensor - high.astype(F32)).astype(LOW)
        return unsort(high) + unsort(rest)

    content_out = unsort(stream_low[:rows]).astype(LOW)
    query_out = unsort(stream_low[rows:]).astype(LOW)

    grad_stream = None
    norm_terms = [None] * layer_count
    matrix_rows = [None] * layer_count
    attn_rows = [None] * layer_count
    attn_parts = [None] * layer_count
    side = jnp.full((1,), grid.core_at, jnp.int32)
    pairs = width // 128
    score_sums = []
    pending = {}
    third = width // 2

    def content_side(own, come):
        own, grad_all = own
        if grad_all is not None:
            own = own + dot_nn(spreads[0], grad_all)
        return own + come.astype(F32)

    def keys_back(grad_k, grad_v, qkv):
        return (dot_nt(grad_k, qkv[:, width : 2 * width]) + dot_nt(grad_v, qkv[:, 2 * width :])).astype(LOW)

    def finish_rows(high):
        shared = grid.sum_blocks(high[:, 2 * span :])
        sides = grid.halves(jnp.concatenate([high[:, : 2 * span], shared], axis=1))
        proj_grad = jnp.concatenate([one[:, 2 * span :] for one in sides], axis=1)
        half = jnp.concatenate([one[:, : 2 * span] for one in sides], axis=1)
        other = grid.from_block(half)
        first = grid.block_at == 0
        quarters = (jnp.where(first, half, other), jnp.where(first, other, half))
        inner_grad, outer_grad = (
            jnp.concatenate(
                [
                    one[:, (2 * core + which) * span : (2 * core + which + 1) * span]
                    for one in quarters
                    for core in range(2)
                ],
                axis=1,
            )
            for which in range(2)
        )
        return tuple(tensor.astype(F32) for tensor in (proj_grad, inner_grad, outer_grad))

    def waits(*names):
        return [pending[name] for name in names if name in pending]

    come = None
    for layer_index in reversed(range(layer_count)):
        (
            stream_low, all_content, queries, keys, values, out, out_low, weights,
            result, middle, middle_low, active, slope, inverse_one, inverse_two,
        ) = kept[layer_index]
        qkv = qkv_full[layer_index]
        partial = None
        for part in (None,) if layer_index == layer_count - 1 else (1, 0):
            if part is None:
                grad = grad_low
            elif part == 1:
                grad = grad_stream[1]
            else:
                grad = content_side(grad_stream[0], hold(come, partial[0]) if paired else come)
            partial = layer_tail_back_call(
                grad, result, inverse_two, middle, inverse_one, slope, (others, layer_index),
                all_pieces[layer_index], span, norm_gains[layer_index], norm_shifts[layer_index],
                part, partial, *waits("attn"),
            )
        two_low, inner_low, grad_one, branch_low, grad_out, norm_terms[layer_index] = partial
        grad_out = grad_out.reshape(2, rows, width)
        back = (window, queries, keys, values, grad_out, out, weights)
        if paired:
            def steps(name, quarter, come=None):
                return [
                    (middle_low, inner_low, span, quarter, name, 0, come),
                    (two_low, active, span, quarter, name, 1, come),
                ]

            sent = products_call(
                "products_sent", side,
                steps("far", 3) + steps("beside", 1) + [(out_low, branch_low, third, "other", "proj", 0, None)],
                {"far": (width, 2 * span, span), "beside": (width, 2 * span, span), "proj": (width, third, third)},
                (),
            )
            come = {name: grid.from_core(tensor) for name, tensor in sent.items()}
            near = products_call(
                "products_near", side, steps("near", 2, come["far"]), {"near": (width, 2 * span, span)}
            )["near"]
            arrived = grid.from_block(near)
            held = products_call(
                "products_held", side,
                steps("mine", 0, come["beside"]) + [(out_low, branch_low, third, "side", "proj", 0, come["proj"])],
                {"mine": (width, 2 * span, span), "proj": (width, third, third)},
                [near],
            )
            partial = attend_back_call((0, pairs // 2), *back, None, *held.values())
            if "low_begun" in pending:
                pending["low"] = grid.scatter_end(pending["low_begun"], partial[0])
                pending["high_begun"] = grid.high_begin(pending["low"])
            grad_q, grad_k, grad_v, score_sum = attend_back_call(
                (pairs // 2, pairs - pairs // 2), *back, partial, *waits("low")
            )
            score_sums.append(score_sum)
            grad_q = grad_q.reshape(2 * rows, width)
            ffn_sum = (held["mine"].astype(F32) + arrived.astype(F32)).astype(LOW)
            ffn_sum = jnp.concatenate([ffn_sum, held["proj"]], axis=1)
            if layer_index == 0:
                ffn_begun = grid.low_begin(ffn_sum)
            if layer_index > 0:
                grad_all = keys_back(grad_k, grad_v, qkv)
                passed = dot_nn(spreads[1], grad_all).astype(LOW)
            attn = products_call(
                "products_attn", side,
                [
                    (lhs, rhs, width, 0, "attn", index, None)
                    for index, (lhs, rhs) in enumerate(
                        ((stream_low, grad_q), (all_content, grad_k), (all_content, grad_v))
                    )
                ],
                {"attn": (width, 3 * width, width)},
                [passed, ffn_sum] if layer_index > 0 else (),
            )["attn"]
            if layer_index == 0:
                grad_q, grad_k, grad_v = (hold(tensor, attn) for tensor in (grad_q, grad_k, grad_v))
                grad_all = keys_back(grad_k, grad_v, qkv)
                before = [grad_all]
                if "high_begun" in pending:
                    upper = grid.scatter_end(pending["high_begun"], attn)
                    before.append(upper)
                ffn_low = grid.scatter_end(ffn_begun, *before)
                ffn_begun = grid.high_begin(ffn_low)
                passed = dot_nn(spreads[1], grad_all).astype(LOW)
            attn_part = grid.scatter_rows(attn)
            attn_parts[layer_index] = attn_part
            if layer_index > 0:
                pending = {"attn": attn, "sum": ffn_sum, "low_begun": grid.low_begin(ffn_sum)}
            else:
                pending = {"passed": passed, "ffn_low": ffn_low}
        else:
            grad_q, grad_k, grad_v, score_sum = attend_back_call((0, pairs), *back, None)
            score_sums.append(score_sum)
            grad_q = grad_q.reshape(2 * rows, width)
            terms = [
                jnp.concatenate(
                    [dot_tn(stream_low, grad_q), dot_tn(all_content, grad_k), dot_tn(all_content, grad_v)], axis=1
                ),
                dot_tn(out_low, branch_low),
                dot_tn(middle_low, inner_low),
                dot_tn(two_low, active),
            ]
            attn_rows[layer_index], *matrix_rows[layer_index] = (grid.scatter(term.astype(LOW)) for term in terms)
        query_side = grad_one + dot_nt(grad_q, qkv[:, :width])
        grad_stream = [(query_side[:rows], grad_all if paired else None), query_side[rows:]]
        if layer_index == 0:
            rest = grad_stream[1]
            if paired:
                rest = hold(rest, ffn_low)
            query_grad = unsort_wide(rest)
            table_grad, table_raw = table_call(
                window, score_sums, place_column, bucket_count, *([passed, ffn_low, query_grad] if paired else [])
            )
        if paired:
            come = grid.from_block(passed)
        else:
            grad_all = keys_back(grad_k, grad_v, qkv)
            grad_split = jnp.stack([dot_nn(spread, grad_all).astype(LOW) for spread in spreads])
            grad_split = jnp.roll(grad_split, block_index, axis=0)
            come = lax.psum_scatter(grad_split, "blk", scatter_dimension=0, tiled=False)
    if paired:
        ffn_high = grid.scatter_end(ffn_begun, table_raw)
        come = hold(come, ffn_high)
        if layer_count > 1:
            matrix_rows[1] = finish_rows(hold(upper, ffn_high))
        matrix_rows[0] = finish_rows(ffn_high)
        attn_rows = [grid.scatter_end_blocks(hold(part, ffn_high)) for part in attn_parts]
    grad_stream[0] = content_side(grad_stream[0], come)
    norm_lines = jnp.concatenate([terms[:4] for terms in norm_terms], axis=0)
    if paired:
        norm_lines = hold(norm_lines, ffn_high, attn_part)
    table_lines = jnp.pad(table_grad.T, ((0, 0), (0, width - bucket_count)))
    sums = grid.sum_all(jnp.concatenate([norm_lines, table_lines], axis=0))
    norm_sum = sums[: 4 * layer_count].reshape(layer_count, 2, 2, width)
    table_total = sums[4 * layer_count :, :bucket_count].T
    matrix_grads = tuple(jnp.stack(rows_of, axis=0) for rows_of in (attn_rows, *zip(*matrix_rows)))
    return (
        content_out[None],
        query_out[None],
        unsort_wide(grad_stream[0])[None],
        query_grad[None],
        *matrix_grads,
        norm_sum[:, 0],
        norm_sum[:, 1],
        table_total,
    )


def solution(mesh):
    tokens = P("dp", "blk", None)
    matrix = P(None, "dp", None)
    whole = P()
    sequence = P("dp", None)
    return jax.shard_map(
        functools.partial(shards, Grid(mesh)),
        mesh=mesh,
        in_specs=(tokens,) * 4 + (matrix,) * 4 + (whole,) * 3 + (sequence,) * 3,
        out_specs=(tokens,) * 4 + (matrix,) * 4 + (whole,) * 3,
        check_vma=False,
    )
```
